256 devices in a mesh: tile: 64 (over y_lo, x, z), chan: 4 (over y_hi, core).
Axes of the slice: x: 4, y: 4 (y_hi: 2, y_lo: 2; y = y_hi * 2 + y_lo), z: 8, core: 2. Of those that a mesh axis runs over, the one named last changes fastest.
Arguments:
- inputs: bfloat16 [192, 256, 64], P('tile', 'chan'), may hold values from -6 to 6
- prior_hidden_state: bfloat16 [192, 256, 64], P('tile', 'chan'), may hold values from -1 to 1
- cell_prev: float32 [192, 256, 64], P('tile', 'chan'), may hold values from -6 to 6
- kernel: bfloat16 [9, 4, 256, 512], P(None, None, 'chan'), may hold values from -0.09375 to 0.09375
- gate_bias: float32 [4, 256], P(None, 'chan'), may hold values from -3 to 3
- hidden_upstream: bfloat16 [192, 256, 64], P('tile', 'chan'), may hold values from -6 to 6
- cell_upstream: float32 [192, 256, 64], P('tile', 'chan'), may hold values from -6 to 6
- edge_source: int32 [192, 4], replicated, may hold values from 0 to 191
- edge_code: int32 [192, 4], replicated, may hold values from 0 to 7
- corner_source: int32 [192, 4], replicated, may hold values from 0 to 191
- corner_code: int32 [192, 4], replicated, may hold values from 0 to 3
Outputs:
- hidden_new: bfloat16 [192, 256, 64], P('tile', 'chan')
- cell_new: float32 [192, 256, 64], P('tile', 'chan')
- kernel_grad: float32 [9, 4, 256, 512], P(None, None, 'chan')
- bias_grad: float32 [4, 256], P(None, 'chan')
- input_grad: bfloat16 [192, 256, 64], P('tile', 'chan')
- hidden_grad: bfloat16 [192, 256, 64], P('tile', 'chan')
- cell_grad: float32 [192, 256, 64], P('tile', 'chan')
The draws below stay inside these ranges and needn't reach their ends.
All inputs are finite; a program needn't handle non-finite values.
Results may differ from the reference program's by a relative error of at most 0.0055.
Values may be sent and summed in bfloat16 or wider, within the bound.
A program may use at most 192 MiB of HBM per device.

```python
import jax
import jax.numpy as jnp
from jax import lax

C = 256
TS = 8
TILES = 192
PIX = 64


def set_ends(drawn, rng, smallest, top_value):
    longest = drawn.shape.index(max(drawn.shape))
    spots = []
    for shift in (0, 1):
        where = [jax.random.randint(jax.random.fold_in(rng, axis), (), 0, length) for axis, length in enumerate(drawn.shape)]
        where[longest] = (where[longest] + shift) % drawn.shape[longest]
        spots.append(tuple(where))
    return drawn.at[spots[0]].set(smallest).at[spots[1]].set(top_value)


def block_levels(key, dims, shards, smallest, high):
    def one(dim, shards_of):
        draws = jax.random.uniform(jax.random.fold_in(jax.random.fold_in(key, 6), dim), (shards_of,), jnp.float32, smallest / len(shards), high / len(shards))
        return jnp.repeat(jnp.exp(draws), dims[dim] // shards_of).reshape((-1,) + (1,) * (len(dims) - dim - 1))

    loudness = one(*shards[0])
    for cut in shards[1:]:
        loudness = loudness * one(*cut)
    return loudness


def bell_draw(rng, shape, width, most, pieces=(), dtype=jnp.bfloat16):
    entries = width * jax.random.normal(rng, shape, jnp.float32)
    if pieces:
        entries = entries * block_levels(rng, shape, pieces, -0.22, 0.18)
    return jnp.clip(entries, -most, most).astype(dtype)


def setup_inputs(seed: int = 0) -> dict:
    keys = jax.random.split(jax.random.key(seed), 12)
    inputs = bell_draw(keys[0], (TILES, C, PIX), 1.0, 6.0, ((0, 64), (1, 4)))
    prior_hidden_state = jnp.clip(jax.random.uniform(keys[1], (TILES, C, PIX), jnp.float32, -1.0, 1.0) * block_levels(keys[1], (TILES, C, PIX), ((0, 64), (1, 4)), -0.4, 0.0), -1.0, 1.0).astype(jnp.bfloat16)
    cell_prev = bell_draw(keys[2], (TILES, C, PIX), 1.0, 6.0, ((0, 64), (1, 4)), jnp.float32)
    kernel = bell_draw(keys[3], (9, 4, C, 2 * C), (18 * C) ** -0.5, 0.09375, ((2, 4),))
    gate_bias = bell_draw(keys[4], (4, C), 0.5, 3.0, ((1, 4),), jnp.float32)
    hidden_upstream = bell_draw(keys[5], (TILES, C, PIX), 1.0, 6.0, ((0, 64), (1, 4)))
    cell_upstream = bell_draw(keys[6], (TILES, C, PIX), 1.0, 6.0, ((0, 64), (1, 4)), jnp.float32)
    edge_source = set_ends(jax.random.randint(keys[7], (TILES, 4), 0, TILES), jax.random.fold_in(keys[7], 1), 0, TILES - 1).astype(jnp.int32)
    edge_code = set_ends(jax.random.randint(keys[8], (TILES, 4), 0, 8), jax.random.fold_in(keys[8], 1), 0, 7).astype(jnp.int32)
    corner_source = set_ends(jax.random.randint(keys[9], (TILES, 4), 0, TILES), jax.random.fold_in(keys[9], 1), 0, TILES - 1).astype(jnp.int32)
    corner_code = set_ends(jax.random.randint(keys[10], (TILES, 4), 0, 4), jax.random.fold_in(keys[10], 1), 0, 3).astype(jnp.int32)
    return {"inputs": inputs, "prior_hidden_state": prior_hidden_state, "cell_prev": cell_prev, "kernel": kernel, "gate_bias": gate_bias, "hidden_upstream": hidden_upstream, "cell_upstream": cell_upstream, "edge_source": edge_source, "edge_code": edge_code, "corner_source": corner_source, "corner_code": corner_code}


def rim_parts(tile_field):
    sides = jnp.stack([tile_field[:, :, 0, :], tile_field[:, :, :, -1], tile_field[:, :, -1, :], tile_field[:, :, :, 0]], axis=1)
    corners = jnp.stack([tile_field[:, :, 0, 0], tile_field[:, :, 0, -1], tile_field[:, :, -1, -1], tile_field[:, :, -1, 0]], axis=1)
    return sides, corners


def cycle_parts(padded):
    sides = jnp.stack([padded[:, :, 0, 1:-1], padded[:, :, 1:-1, -1], padded[:, :, -1, 1:-1], padded[:, :, 1:-1, 0]], axis=1)
    corners = jnp.stack([padded[:, :, 0, 0], padded[:, :, 0, -1], padded[:, :, -1, -1], padded[:, :, -1, 0]], axis=1)
    return sides, corners


def mirror_edge_order(edges, codes):
    flags = (codes % 2 == 1)[:, :, None, None]
    return jnp.where(flags, edges[..., ::-1], edges)


def assemble(tile_field, edges, corners):
    top_row = jnp.concatenate([corners[:, 0, :, None], edges[:, 0], corners[:, 1, :, None]], axis=2)
    bottom_row = jnp.concatenate([corners[:, 3, :, None], edges[:, 2], corners[:, 2, :, None]], axis=2)
    middle = jnp.concatenate([edges[:, 3][:, :, :, None], tile_field, edges[:, 1][:, :, :, None]], axis=3)
    return jnp.concatenate([top_row[:, :, None, :], middle, bottom_row[:, :, None, :]], axis=2)


def place_rims(interior, side_sum, corner_sum):
    result = interior
    result = result.at[:, :, 0, :].add(side_sum[:, 0])
    result = result.at[:, :, :, -1].add(side_sum[:, 1])
    result = result.at[:, :, -1, :].add(side_sum[:, 2])
    result = result.at[:, :, :, 0].add(side_sum[:, 3])
    result = result.at[:, :, 0, 0].add(corner_sum[:, 0])
    result = result.at[:, :, 0, -1].add(corner_sum[:, 1])
    result = result.at[:, :, -1, -1].add(corner_sum[:, 2])
    result = result.at[:, :, -1, 0].add(corner_sum[:, 3])
    return result


def reference(inputs, prior_hidden_state, cell_prev, kernel, gate_bias, hidden_upstream, cell_upstream, edge_source, edge_code, corner_source, corner_code):
    highest = lax.Precision.HIGHEST
    tile_field = jnp.concatenate([inputs, prior_hidden_state], axis=1).reshape(TILES, 2 * C, TS, TS)
    sides, corners = rim_parts(tile_field)
    picked = mirror_edge_order(sides[edge_source, edge_code // 2], edge_code)
    picked_corners = corners[corner_source, corner_code]
    padded = assemble(tile_field, picked, picked_corners)
    kernels = kernel.reshape(9, 4 * C, 2 * C).astype(jnp.float32)
    windows = [padded[:, :, offset // 3: offset // 3 + TS, offset % 3: offset % 3 + TS].reshape(TILES, 2 * C, TS * TS) for offset in range(9)]
    gates = gate_bias.reshape(1, 4 * C, 1)
    for offset in range(9):
        gates = gates + jnp.einsum('gc,ncp->ngp', kernels[offset], windows[offset].astype(jnp.float32), precision=highest)
    gates = gates.reshape(TILES, 4, C, TS * TS)
    in_gate = jax.nn.sigmoid(gates[:, 0])
    forget = jax.nn.sigmoid(gates[:, 1])
    cand = jnp.tanh(gates[:, 2])
    out_gate = jax.nn.sigmoid(gates[:, 3])
    cell_new = forget * cell_prev + in_gate * cand
    squashed = jnp.tanh(cell_new)
    hidden_new = (out_gate * squashed).astype(jnp.bfloat16)
    upstream = hidden_upstream.astype(jnp.float32)
    dcell = cell_upstream + upstream * out_gate * (1.0 - squashed * squashed)
    cell_grad = dcell * forget
    dgates = jnp.stack([dcell * cand * in_gate * (1.0 - in_gate), dcell * cell_prev * forget * (1.0 - forget), dcell * in_gate * (1.0 - cand * cand), upstream * squashed * out_gate * (1.0 - out_gate)], axis=1)
    dgates = dgates.reshape(TILES, 4 * C, TS * TS).astype(jnp.bfloat16).astype(jnp.float32)
    bias_grad = jnp.sum(dgates, axis=(0, 2)).reshape(4, C)
    kernel_grad = jnp.stack([jnp.einsum('ngp,ncp->gc', dgates, windows[offset].astype(jnp.float32), precision=highest) for offset in range(9)]).reshape(9, 4, C, 2 * C)
    dpadded = jnp.zeros((TILES, 2 * C, TS + 2, TS + 2), jnp.float32)
    for offset in range(9):
        product = jnp.einsum('gc,ngp->ncp', kernels[offset], dgates, precision=highest).reshape(TILES, 2 * C, TS, TS)
        dpadded = dpadded.at[:, :, offset // 3: offset // 3 + TS, offset % 3: offset % 3 + TS].add(product)
    cycle_sides, cycle_corners = cycle_parts(dpadded)
    cycle_sides = mirror_edge_order(cycle_sides, edge_code)
    side_sum = jnp.zeros_like(cycle_sides).at[edge_source, edge_code // 2].add(cycle_sides)
    corner_sum = jnp.zeros_like(cycle_corners).at[corner_source, corner_code].add(cycle_corners)
    dfield = place_rims(dpadded[:, :, 1:-1, 1:-1], side_sum, corner_sum).reshape(TILES, 2 * C, TS * TS)
    input_grad = dfield[:, :C].astype(jnp.bfloat16)
    hidden_grad = dfield[:, C:].astype(jnp.bfloat16)
    return (hidden_new.reshape(TILES, C, TS * TS), cell_new.reshape(TILES, C, TS * TS), kernel_grad, bias_grad, input_grad, hidden_grad, cell_grad.reshape(TILES, C, TS * TS))
```

```python
import functools

import jax
import jax.numpy as jnp
from jax import lax
from jax.experimental import pallas as pl
from jax.experimental.pallas import tpu as pltpu
from jax.sharding import PartitionSpec as P

F32, BF16, I32 = jnp.float32, jnp.bfloat16, jnp.int32
MESH = pl.DeviceIdType.MESH
NY, NX, NZ = 2, 4, 8
NQ = NY * NX
NC = 4
TPD = 3
PIX = 64
RIM = 32 * TPD
MARGIN = 112
BODY = 80 * TPD
DROWS = BODY + 64
UNIT = 1024
JOBS = ((0, 2, "zxy"), (2, 3, "xyz"), (5, 4, "yxz"))
VMEM_LIMIT = 56 * 1024 * 1024


def nn(a, b):
    return lax.dot_general(a, b, (((1,), (0,)), ((), ())), preferred_element_type=F32)


def nt(a, b):
    return lax.dot_general(a, b, (((1,), (1,)), ((), ())), preferred_element_type=F32)


def iota(shape, dim):
    return lax.broadcasted_iota(I32, shape, dim)


def eye(n):
    return (iota((n, n), 0) == iota((n, n), 1)).astype(BF16)


def position():
    t = lax.axis_index("tile")
    z, q = lax.rem(t, NZ), lax.div(t, NZ)
    return q, lax.div(q, NX), lax.rem(q, NX), z, lax.axis_index("chan")


def peers():
    q, y, x, z, c = position()
    return {
        "z": lambda d: (q * NZ + lax.rem(z + d, NZ), c),
        "q": lambda d: (lax.rem(q + d, NQ) * NZ + z, c),
        "x": lambda d: ((y * NX + lax.rem(x + d, NX)) * NZ + z, c),
        "y": lambda d: ((lax.rem(y + d, NY) * NX + x) * NZ + z, c),
        "c": lambda d: (q * NZ + z, lax.rem(c + d, NC)),
    }


def entry_barrier(to):
    barrier = pltpu.get_barrier_semaphore()
    count = 0
    for axis, size in (("z", NZ), ("q", NQ), ("c", NC)):
        for d in range(1, size):
            pl.semaphore_signal(barrier, inc=1, device_id=to[axis](d), device_id_type=MESH)
            count += 1
    pl.semaphore_wait(barrier, count)


def send(src, dst, send_sem, recv_sem, device):
    pltpu.make_async_remote_copy(
        src_ref=src,
        dst_ref=dst,
        send_sem=send_sem,
        recv_sem=recv_sem,
        device_id=device,
        device_id_type=MESH,
    ).start()


def await_bytes(like, sem):
    pltpu.make_async_copy(like, like, sem).wait()


def prepare_kernel(
    inp, hid, esrc, ecode, csrc, ccode, field_out, rim_out, index_out, cells, index
):
    ident = eye(PIX)
    for t in range(TPD):
        both = jnp.concatenate([inp[t], hid[t]], axis=0)
        cells[t * PIX : (t + 1) * PIX, :] = nt(ident, both)
    field_out[...] = cells[...].astype(BF16)
    for t in range(TPD):
        base = t * PIX
        rim = jnp.concatenate(
            [
                cells[base : base + 8, :],
                cells[pl.ds(base + 7, 8, stride=8), :],
                cells[base + 56 : base + 64, :],
                cells[pl.ds(base, 8, stride=8), :],
            ],
            axis=0,
        )
        rim_out[t * 32 : (t + 1) * 32, :] = rim.astype(BF16)
    lane, row = iota((4, 128), 1), iota((4, 128), 0)
    edge_lane = ((lane < 32) & (lax.div(lane, 8) == row)).astype(BF16)
    corner_lane = (lane - 32 == row).astype(BF16)

    def spread(edges, corners):
        wide = nn(edges[...].astype(F32).astype(BF16), edge_lane)
        wide += nn(corners[...].astype(F32).astype(BF16), corner_lane)
        return wide.astype(I32)

    source, code = spread(esrc, csrc), spread(ecode, ccode)
    lane = iota(source.shape, 1)
    cell = lane & 7
    along_side = (code >> 1) * 8 + jnp.where((code & 1) == 1, 7 - cell, cell)
    at_corner = jnp.where(
        code == 0, 0, jnp.where(code == 1, 7, jnp.where(code == 2, 23, 16))
    )
    index[...] = source * 32 + jnp.where(lane < 32, along_side, at_corner)
    devices = index_out.shape[0]
    rows = [index[pl.ds(i, devices, stride=TPD), :] for i in range(TPD)]
    index_out[...] = jnp.concatenate(
        [r[:, :32] for r in rows]
        + [r[:, 32:36] for r in rows]
        + [jnp.full((devices, 128 - 36 * TPD), -1000000, I32)],
        axis=1,
    )


def prepare(inp, hid, esrc, ecode, csrc, ccode):
    devices = NQ * NZ
    vmem = pl.BlockSpec(memory_space=pltpu.VMEM)
    return pl.pallas_call(
        prepare_kernel,
        out_shape=(
            jax.ShapeDtypeStruct((TPD * PIX, 128), BF16),
            jax.ShapeDtypeStruct((RIM, 128), BF16),
            jax.ShapeDtypeStruct((devices, 128), I32),
        ),
        in_specs=[vmem] * 6,
        out_specs=(vmem,) * 3,
        scratch_shapes=[
            pltpu.VMEM((TPD * PIX, 128), F32),
            pltpu.VMEM((devices * TPD, 128), I32),
        ],
        name="prepare",
    )(inp, hid, esrc, ecode, csrc, ccode)


def halo_kernel(
    rim, field, index, field_all, margin_all, table, picked, arrived, sems_s, sems_r
):
    q, y, x, z, c = position()
    to = peers()
    entry_barrier(to)
    for d in range(1, NZ):
        send(rim, table.at[z], sems_s.at[0], sems_r.at[0], to["z"](d))
    for d in range(1, NC):
        send(field, field_all.at[c], sems_s.at[1], sems_r.at[1], to["c"](d))
    table[z] = rim[...]
    field_all[c] = field[...]

    first = q * (NZ * RIM)
    choosers = []
    for d in range(NQ):
        row = index[pl.ds(lax.rem(q + d, NQ) * NZ + z, 1), :]
        down = jnp.broadcast_to((row - first).astype(F32), (128, 128)).T
        choosers.append(
            jnp.concatenate(
                [
                    (down == (iota((128, 128), 1) + 128 * k).astype(F32)).astype(BF16)
                    for k in range(NZ * RIM // 128)
                ],
                axis=1,
            )
        )
    await_bytes(table.at[pl.ds(0, NZ - 1)], sems_r.at[0])
    cells = table[...].reshape(NZ * RIM, 128)
    for d in range(NQ):
        picked[d] = nn(choosers[d], cells)[:MARGIN].astype(BF16)
        if d:
            send(picked.at[d], arrived.at[d - 1], sems_s.at[2], sems_r.at[2], to["q"](d))
    await_bytes(arrived, sems_r.at[2])
    total = picked[0].astype(F32)
    for d in range(1, NQ):
        total += arrived[d - 1].astype(F32)
    margin_all[c] = total.astype(BF16)
    for d in range(1, NC):
        send(margin_all.at[c], margin_all.at[c], sems_s.at[3], sems_r.at[3], to["c"](d))
    await_bytes(field_all.at[pl.ds(0, NC - 1)], sems_r.at[1])
    await_bytes(margin_all.at[pl.ds(0, NC - 1)], sems_r.at[3])
    await_bytes(table.at[pl.ds(0, NZ - 1)], sems_s.at[0])
    await_bytes(field_all.at[pl.ds(0, NC - 1)], sems_s.at[1])
    await_bytes(arrived, sems_s.at[2])
    await_bytes(margin_all.at[pl.ds(0, NC - 1)], sems_s.at[3])


def halo(rim, field, index):
    vmem = pl.BlockSpec(memory_space=pltpu.VMEM)
    return pl.pallas_call(
        halo_kernel,
        out_shape=(
            jax.ShapeDtypeStruct((NC, TPD * PIX, 128), BF16),
            jax.ShapeDtypeStruct((NC, MARGIN, 128), BF16),
        ),
        in_specs=[vmem] * 3,
        out_specs=(vmem,) * 2,
        scratch_shapes=[
            pltpu.VMEM((NZ, RIM, 128), BF16),
            pltpu.VMEM((NQ, MARGIN, 128), BF16),
            pltpu.VMEM((NQ - 1, MARGIN, 128), BF16),
            pltpu.SemaphoreType.DMA((4,)),
            pltpu.SemaphoreType.DMA((4,)),
        ],
        compiler_params=pltpu.CompilerParams(
            collective_id=0, has_side_effects=True, vmem_limit_bytes=VMEM_LIMIT
        ),
        name="halo",
    )(rim, field, index)


def step_kernel(
    field_all,
    margin_all,
    kern,
    bias,
    cell_prev,
    cell_up,
    hidden_up,
    hidden_out,
    cell_out,
    cell_grad_out,
    grad_out,
    bias_out,
    dpad_out,
    wide,
    windows,
    accs,
):
    for k in range(4):
        pair, half = 2 * (k % 2), 64 * (k // 2)

        def lanes(ref):
            return jnp.concatenate(
                [ref[pair][:, half : half + 64], ref[pair + 1][:, half : half + 64]], axis=1
            ).astype(F32)

        body, margin = lanes(field_all), lanes(margin_all)
        for t in range(TPD):
            base, rim = t * 80, t * 32
            wide[1, k, base : base + 8, :] = margin[rim : rim + 8]
            wide[1, k, base + 8 : base + 72, :] = body[t * PIX : (t + 1) * PIX]
            wide[1, k, base + 72 : base + 80, :] = margin[rim + 16 : rim + 24]
        wide[0, k, 1:BODY, :] = wide[1, k, 0 : BODY - 1, :]
        wide[2, k, 0 : BODY - 1, :] = wide[1, k, 1:BODY, :]
        for t in range(TPD):
            base, rim, corner = t * 80, t * 32, RIM + t * 4
            left, right = wide.at[0, k], wide.at[2, k]
            left[base : base + 1, :] = margin[corner : corner + 1]
            left[pl.ds(base + 8, 8, stride=8), :] = margin[rim + 24 : rim + 32]
            left[base + 72 : base + 73, :] = margin[corner + 3 : corner + 4]
            right[base + 7 : base + 8, :] = margin[corner + 1 : corner + 2]
            right[pl.ds(base + 15, 8, stride=8), :] = margin[rim + 8 : rim + 16]
            right[base + 79 : base + 80, :] = margin[corner + 2 : corner + 3]
    for o in range(9):
        a, b = o // 3, o % 3
        for k in range(4):
            for t in range(TPD):
                base = t * 80 + a * 8
                windows[o, t * PIX : (t + 1) * PIX, k * 128 : (k + 1) * 128] = wide[
                    b, k, base : base + PIX, :
                ].astype(BF16)

    gates = bias[...] + nt(kern[0], windows[0])
    for o in range(1, 9):
        gates = gates + nt(kern[o], windows[o])
    in_gate = jax.nn.sigmoid(gates[0:64])
    forget = jax.nn.sigmoid(gates[64:128])
    cand = jnp.tanh(gates[128:192])
    out_gate = jax.nn.sigmoid(gates[192:256])
    before = jnp.concatenate([cell_prev[t] for t in range(TPD)], axis=1)
    above = jnp.concatenate([cell_up[t] for t in range(TPD)], axis=1)
    upstream = jnp.concatenate([hidden_up[t].astype(F32) for t in range(TPD)], axis=1)
    cell_new = forget * before + in_gate * cand
    squashed = jnp.tanh(cell_new)
    hidden_new = (out_gate * squashed).astype(BF16)
    dcell = above + upstream * out_gate * (1.0 - squashed * squashed)
    cell_grad = dcell * forget
    for t in range(TPD):
        at = slice(t * PIX, (t + 1) * PIX)
        hidden_out[t] = hidden_new[:, at]
        cell_out[t] = cell_new[:, at]
        cell_grad_out[t] = cell_grad[:, at]
    dgates = jnp.concatenate(
        [
            dcell * cand * in_gate * (1.0 - in_gate),
            dcell * before * forget * (1.0 - forget),
            dcell * in_gate * (1.0 - cand * cand),
            upstream * squashed * out_gate * (1.0 - out_gate),
        ],
        axis=0,
    ).astype(BF16)
    bias_out[...] = nt(jnp.ones((8, TPD * PIX), BF16), dgates)
    for o in range(9):
        grad = nn(dgates, windows[o]).astype(BF16)
        for k in range(4):
            grad_out[o, k] = grad[:, k * 128 : (k + 1) * 128]
    turned = nt(eye(TPD * PIX), dgates).astype(BF16)
    accs[...] = jnp.zeros(accs.shape, F32)
    for o in range(9):
        a, b = o // 3, o % 3
        product = nn(turned, kern[o])
        for k in range(4):
            for t in range(TPD):
                base = 8 + t * 80 + a * 8
                accs[b, k, base : base + PIX, :] += product[
                    t * PIX : (t + 1) * PIX, k * 128 : (k + 1) * 128
                ]
    column = iota((BODY, 128), 0) & 7
    blocks = []
    for k in range(4):
        body = accs[1, k, 8 : 8 + BODY, :]
        body += jnp.where(column < 7, accs[0, k, 9 : 9 + BODY, :], 0.0)
        body += jnp.where(column > 0, accs[2, k, 7 : 7 + BODY, :], 0.0)
        left, right = accs.at[0, k], accs.at[2, k]
        blocks.append(
            (
                body,
                left[pl.ds(8, 32, stride=8), :],
                right[pl.ds(15, 32, stride=8), :],
            )
        )
    for c in range(NC):
        half = slice((c % 2) * 64, (c % 2) * 64 + 64)
        low, high = blocks[c // 2], blocks[2 + c // 2]
        start = 0
        for one, two in zip(low, high):
            rows = one.shape[0]
            dpad_out[c, start : start + rows, :] = jnp.concatenate(
                [one[:, half], two[:, half]], axis=1
            ).astype(BF16)
            start += rows


def step(field_all, margin_all, kern, bias, cell_prev, cell_up, hidden_up):
    vmem = pl.BlockSpec(memory_space=pltpu.VMEM)
    state = cell_prev.shape
    return pl.pallas_call(
        step_kernel,
        out_shape=(
            jax.ShapeDtypeStruct(state, BF16),
            jax.ShapeDtypeStruct(state, F32),
            jax.ShapeDtypeStruct(state, F32),
            jax.ShapeDtypeStruct((9, 4, 256, 128), BF16),
            jax.ShapeDtypeStruct((8, 256), F32),
            jax.ShapeDtypeStruct((NC, DROWS, 128), BF16),
        ),
        in_specs=[vmem] * 7,
        out_specs=(vmem,) * 6,
        scratch_shapes=[
            pltpu.VMEM((3, 4, BODY, 128), F32),
            pltpu.VMEM((9, TPD * PIX, 512), BF16),
            pltpu.VMEM((3, 4, 8 + BODY + 32, 128), F32),
        ],
        compiler_params=pltpu.CompilerParams(vmem_limit_bytes=VMEM_LIMIT),
        name="step",
    )(field_all, margin_all, kern, bias, cell_prev, cell_up, hidden_up)


def axis_size(axis):
    return {"x": NX, "y": NY, "z": NZ}[axis]


def reduce_kernel(
    grad,
    bias,
    dpad,
    index,
    grad_out,
    bias_out,
    inner_out,
    side_out,
    dpad_in,
    dsum,
    margin_own,
    margin_send,
    margin_in,
    slot_sum,
    slot_send,
    slot_in,
    bias_in_q,
    bias_mid,
    bias_in_z,
    *rest,
):
    jobs = len(JOBS)
    landing = [rest[5 * j : 5 * j + 3] for j in range(jobs)]
    passing = [rest[5 * j + 3 : 5 * j + 5] for j in range(jobs)]
    small_s, small_r, job_s, job_r = rest[5 * jobs :]
    q, y, x, z, c = position()
    here = {"x": x, "y": y, "z": z}
    to = peers()

    def rows_of(j, stage):
        rows = JOBS[j][1] * UNIT
        for axis in JOBS[j][2][:stage]:
            rows //= axis_size(axis)
        return rows

    def start_of(j, stage):
        first = JOBS[j][0] * UNIT
        rows = JOBS[j][1] * UNIT
        for axis in JOBS[j][2][:stage]:
            rows //= axis_size(axis)
            first = first + here[axis] * rows
        return pl.multiple_of(first, 16) if stage else first

    def scatter(j, stage):
        axis = JOBS[j][2][stage]
        size, rows = axis_size(axis), rows_of(j, stage + 1)
        for d in range(1, size):
            chunk = lax.rem(here[axis] + d, size) * rows
            if stage == 0:
                src = grad.at[pl.ds(pl.multiple_of(JOBS[j][0] * UNIT + chunk, 16), rows)]
            else:
                src = passing[j][stage - 1].at[pl.ds(pl.multiple_of(chunk, 16), rows)]
            send(
                src,
                landing[j][stage].at[d - 1],
                job_s.at[j, stage],
                job_r.at[j, stage],
                to[axis](d),
            )

    def gather(j, stage):
        axis = JOBS[j][2][stage]
        size, rows = axis_size(axis), rows_of(j, stage + 1)
        mine = grad_out.at[pl.ds(start_of(j, stage + 1), rows)]
        for d in range(1, size):
            send(mine, mine, job_s.at[j, 3 + stage], job_r.at[j, 3 + stage], to[axis](d))

    def add_up(j, stage):
        axis = JOBS[j][2][stage]
        rows = rows_of(j, stage + 1)
        await_bytes(landing[j][stage], job_r.at[j, stage])
        mine = here[axis] * rows
        block = min(rows, 128)
        while rows % block:
            block -= 16

        def one(i, carry):
            at = pl.multiple_of(i * block, 16)
            if stage == 0:
                from_row = pl.multiple_of(JOBS[j][0] * UNIT + mine + at, 16)
                total = grad[pl.ds(from_row, block), :].astype(F32)
            else:
                from_row = pl.multiple_of(mine + at, 16)
                total = passing[j][stage - 1][pl.ds(from_row, block), :].astype(F32)
            for d in range(axis_size(axis) - 1):
                total += landing[j][stage][d, pl.ds(at, block), :].astype(F32)
            if stage < 2:
                passing[j][stage][pl.ds(at, block), :] = total.astype(BF16)
            else:
                into = pl.multiple_of(start_of(j, 3) + at, 16)
                grad_out[pl.ds(into, block), :] = total.astype(BF16)
            return carry

        if rows == block:
            one(0, 0)
        else:
            lax.fori_loop(0, rows // block, one, 0)

    def gathered(j, stage):
        axis = JOBS[j][2][stage]
        rows = rows_of(j, stage + 1) * (axis_size(axis) - 1)
        await_bytes(grad_out.at[pl.ds(0, rows)], job_r.at[j, 3 + stage])

    entry_barrier(to)
    for d in range(1, NC):
        send(
            dpad.at[lax.rem(c + d, NC)],
            dpad_in.at[d - 1],
            small_s.at[0],
            small_r.at[0],
            to["c"](d),
        )
    for j in range(jobs):
        scatter(j, 0)
    for d in range(1, NQ):
        send(bias, bias_in_q.at[d - 1], small_s.at[1], small_r.at[1], to["q"](d))

    await_bytes(dpad_in, small_r.at[0])
    total = dpad[c].astype(F32)
    for d in range(NC - 1):
        total += dpad_in[d].astype(F32)
    dsum[...] = total
    left, right = BODY, BODY + 32
    margin_own[...] = jnp.zeros(margin_own.shape, F32)
    for t in range(TPD):
        base, rim, corner, col = t * 80, t * 32, RIM + t * 4, t * 10
        margin_own[rim : rim + 8, :] = dsum[base : base + 8, :]
        margin_own[rim + 8 : rim + 16, :] = dsum[right + col + 1 : right + col + 9, :]
        margin_own[rim + 16 : rim + 24, :] = dsum[base + 72 : base + 80, :]
        margin_own[rim + 24 : rim + 32, :] = dsum[left + col + 1 : left + col + 9, :]
        margin_own[corner : corner + 1, :] = dsum[left + col : left + col + 1, :]
        margin_own[corner + 1 : corner + 2, :] = dsum[right + col : right + col + 1, :]
        margin_own[corner + 2 : corner + 3, :] = dsum[right + col + 9 : right + col + 10, :]
        margin_own[corner + 3 : corner + 4, :] = dsum[left + col + 9 : left + col + 10, :]
        inner_out[t * PIX : (t + 1) * PIX, :] = dsum[base + 8 : base + 72, :]
    margin_send[...] = margin_own[...].astype(BF16)
    for d in range(1, NQ):
        send(margin_send, margin_in.at[d - 1], small_s.at[2], small_r.at[2], to["q"](d))

    for j in range(jobs):
        add_up(j, 0)
        scatter(j, 1)

    first = q * (NZ * RIM)
    choosers = []
    for d in range(NQ):
        row = index[pl.ds(lax.rem(q + NQ - d, NQ) * NZ + z, 1), :][:, :MARGIN]
        chooser = (iota((NZ * RIM, MARGIN), 0) == row - first).astype(F32).astype(BF16)
        choosers.append(chooser)
    await_bytes(margin_in, small_r.at[2])
    sums = nn(choosers[0], margin_send[...])
    for d in range(1, NQ):
        sums += nn(choosers[d], margin_in[d - 1])
    slot_sum[...] = sums.reshape(NZ, RIM, 128)
    slot_send[...] = slot_sum[...].astype(BF16)
    for d in range(1, NZ):
        send(
            slot_send.at[lax.rem(z + d, NZ)],
            slot_in.at[d - 1],
            small_s.at[3],
            small_r.at[3],
            to["z"](d),
        )
    await_bytes(bias_in_q, small_r.at[1])
    total = bias[...]
    for d in range(NQ - 1):
        total += bias_in_q[d]
    bias_mid[...] = total
    for d in range(1, NZ):
        send(bias_mid, bias_in_z.at[d - 1], small_s.at[4], small_r.at[4], to["z"](d))

    for j in range(jobs):
        add_up(j, 1)
        scatter(j, 2)

    await_bytes(slot_in, small_r.at[3])
    total = slot_sum[z]
    for d in range(NZ - 1):
        total += slot_in[d].astype(F32)
    side_out[...] = total
    await_bytes(bias_in_z, small_r.at[4])
    total = bias_mid[...]
    for d in range(NZ - 1):
        total += bias_in_z[d]
    bias_out[...] = total

    for j in range(jobs):
        add_up(j, 2)
        gather(j, 2)
    for stage in (2, 1):
        for j in range(jobs):
            gathered(j, stage)
            gather(j, stage - 1)
    for j in range(jobs):
        gathered(j, 0)

    await_bytes(dpad_in, small_s.at[0])
    await_bytes(bias_in_q, small_s.at[1])
    await_bytes(margin_in, small_s.at[2])
    await_bytes(slot_in, small_s.at[3])
    await_bytes(bias_in_z, small_s.at[4])
    for j in range(jobs):
        for stage in range(3):
            await_bytes(landing[j][stage], job_s.at[j, stage])
            axis = JOBS[j][2][stage]
            rows = rows_of(j, stage + 1) * (axis_size(axis) - 1)
            await_bytes(grad_out.at[pl.ds(0, rows)], job_s.at[j, 3 + stage])


def reduce_all(grad, bias, dpad, index):
    vmem = pl.BlockSpec(memory_space=pltpu.VMEM)
    scratch = [
        pltpu.VMEM((NC - 1, DROWS, 128), BF16),
        pltpu.VMEM((DROWS, 128), F32),
        pltpu.VMEM((MARGIN, 128), F32),
        pltpu.VMEM((MARGIN, 128), BF16),
        pltpu.VMEM((NQ - 1, MARGIN, 128), BF16),
        pltpu.VMEM((NZ, RIM, 128), F32),
        pltpu.VMEM((NZ, RIM, 128), BF16),
        pltpu.VMEM((NZ - 1, RIM, 128), BF16),
        pltpu.VMEM((NQ - 1, 8, 256), F32),
        pltpu.VMEM((8, 256), F32),
        pltpu.VMEM((NZ - 1, 8, 256), F32),
    ]
    for _, units, order in JOBS:
        rows, held = units * UNIT, []
        for axis in order:
            size = axis_size(axis)
            rows //= size
            scratch.append(pltpu.VMEM((size - 1, rows, 128), BF16))
            held.append(pltpu.VMEM((rows, 128), BF16))
        scratch += held[:2]
    scratch += [
        pltpu.SemaphoreType.DMA((5,)),
        pltpu.SemaphoreType.DMA((5,)),
        pltpu.SemaphoreType.DMA((len(JOBS), 6)),
        pltpu.SemaphoreType.DMA((len(JOBS), 6)),
    ]
    return pl.pallas_call(
        reduce_kernel,
        out_shape=(
            jax.ShapeDtypeStruct((9 * UNIT, 128), BF16),
            jax.ShapeDtypeStruct((8, 256), F32),
            jax.ShapeDtypeStruct((TPD * PIX, 128), F32),
            jax.ShapeDtypeStruct((RIM, 128), F32),
        ),
        in_specs=[vmem] * 4,
        out_specs=(vmem,) * 4,
        scratch_shapes=scratch,
        compiler_params=pltpu.CompilerParams(
            collective_id=1, has_side_effects=True, vmem_limit_bytes=VMEM_LIMIT
        ),
        name="reduce_all",
    )(grad, bias, dpad, index)


def finish_kernel(grad, inner, sides, grad_out, input_out, hidden_out, cells):
    for k in range(4):
        grad_out[0, :, k * 128 : (k + 1) * 128] = grad[0, k].astype(F32)

    @pl.when(pl.program_id(0) == 0)
    def _():
        cells[...] = inner[...]
        for t in range(TPD):
            base, rim = t * PIX, t * 32
            cells[base : base + 8, :] += sides[rim : rim + 8, :]
            cells[pl.ds(base + 7, 8, stride=8), :] += sides[rim + 8 : rim + 16, :]
            cells[base + 56 : base + 64, :] += sides[rim + 16 : rim + 24, :]
            cells[pl.ds(base, 8, stride=8), :] += sides[rim + 24 : rim + 32, :]
        ident = eye(128)
        for t in range(TPD):
            rounded = cells[t * PIX : (t + 1) * PIX, :].astype(BF16)
            turned = nt(ident, rounded).astype(BF16)
            input_out[t] = turned[0:64]
            hidden_out[t] = turned[64:128]


def finish(grad, inner, sides):
    whole = lambda shape: pl.BlockSpec(shape, lambda i: (0,) * len(shape))
    state = jax.ShapeDtypeStruct((TPD, 64, PIX), BF16)
    return pl.pallas_call(
        finish_kernel,
        grid=(9,),
        out_shape=(jax.ShapeDtypeStruct((9, 256, 512), F32), state, state),
        in_specs=[
            pl.BlockSpec((1, 4, 256, 128), lambda i: (i, 0, 0, 0)),
            whole(inner.shape),
            whole(sides.shape),
        ],
        out_specs=(
            pl.BlockSpec((1, 256, 512), lambda i: (i, 0, 0)),
            whole(state.shape),
            whole(state.shape),
        ),
        scratch_shapes=[pltpu.VMEM((TPD * PIX, 128), F32)],
        name="finish",
    )(grad, inner, sides)


def local(
    inputs,
    prior_hidden_state,
    cell_prev,
    kernel,
    gate_bias,
    hidden_upstream,
    cell_upstream,
    edge_source,
    edge_code,
    corner_source,
    corner_code,
):
    field, rim, index = prepare(
        inputs, prior_hidden_state, edge_source, edge_code, corner_source, corner_code
    )
    field_all, margin_all = halo(rim, field, index)
    hidden_new, cell_new, cell_grad, grad, bias, dpad = step(
        field_all,
        margin_all,
        kernel.reshape(9, 256, 512),
        gate_bias.reshape(256, 1),
        cell_prev,
        cell_upstream,
        hidden_upstream,
    )
    grad, bias, inner, sides = reduce_all(grad.reshape(9 * UNIT, 128), bias, dpad, index)
    kernel_grad, input_grad, hidden_grad = finish(grad.reshape(9, 4, 256, 128), inner, sides)
    return (
        hidden_new,
        cell_new,
        kernel_grad.reshape(9, 4, 64, 512),
        bias[0].reshape(4, 64),
        input_grad,
        hidden_grad,
        cell_grad,
    )


def solution(mesh):
    tiles, whole = P("tile", "chan", None), P()
    gates = P(None, None, "chan", None)
    bias = P(None, "chan")
    in_specs = (tiles, tiles, tiles, gates, bias, tiles, tiles, whole, whole, whole, whole)
    out_specs = (tiles, tiles, gates, bias, tiles, tiles, tiles)
    return jax.shard_map(local, mesh=mesh, in_specs=in_specs, out_specs=out_specs, check_vma=False)
```

```python
import functools

import jax
import jax.numpy as jnp
from jax import lax
from jax.experimental import pallas as pl
from jax.experimental.pallas import tpu as pltpu
from jax.sharding import PartitionSpec as P

F32, BF16, I32 = jnp.float32, jnp.bfloat16, jnp.int32
MESH = pl.DeviceIdType.MESH
NY, NX, NZ = 2, 4, 8
NQ = NY * NX
NC = 4
TPD = 3
PIX = 64
RIM = 32 * TPD
MARGIN = 112
BODY = 80 * TPD
DROWS = BODY + 64
UNIT = 1024
JOBS = ("yxz", "xyz", "zxy", "yxz", "xyz", "zxy", "yxz", "xyz", "yxz")
VMEM_LIMIT = 56 * 1024 * 1024


def nn(a, b):
    return lax.dot_general(a, b, (((1,), (0,)), ((), ())), preferred_element_type=F32)


def tn(a, b):
    return lax.dot_general(a, b, (((0,), (0,)), ((), ())), preferred_element_type=F32)


def nt(a, b):
    return lax.dot_general(a, b, (((1,), (1,)), ((), ())), preferred_element_type=F32)


def iota(shape, dim):
    return lax.broadcasted_iota(I32, shape, dim)


def eye(n):
    return (iota((n, n), 0) == iota((n, n), 1)).astype(BF16)


def position():
    t = lax.axis_index("tile")
    z, q = lax.rem(t, NZ), lax.div(t, NZ)
    return q, lax.div(q, NX), lax.rem(q, NX), z, lax.axis_index("chan")


def peers():
    q, y, x, z, c = position()
    return {
        "z": lambda d: (q * NZ + lax.rem(z + d, NZ), c),
        "q": lambda d: (lax.rem(q + d, NQ) * NZ + z, c),
        "x": lambda d: ((y * NX + lax.rem(x + d, NX)) * NZ + z, c),
        "y": lambda d: ((lax.rem(y + d, NY) * NX + x) * NZ + z, c),
        "c": lambda d: (q * NZ + z, lax.rem(c + d, NC)),
    }


def greet(to):
    barrier = pltpu.get_barrier_semaphore()
    count = 0
    for axis, size in (("z", NZ), ("q", NQ), ("c", NC)):
        for d in range(1, size):
            pl.semaphore_signal(barrier, inc=1, device_id=to[axis](d), device_id_type=MESH)
            count += 1
    return count


def send(src, dst, send_sem, recv_sem, device):
    pltpu.make_async_remote_copy(
        src_ref=src,
        dst_ref=dst,
        send_sem=send_sem,
        recv_sem=recv_sem,
        device_id=device,
        device_id_type=MESH,
    ).start()


def await_bytes(like, sem):
    pltpu.make_async_copy(like, like, sem).wait()


def axis_size(axis):
    return {"x": NX, "y": NY, "z": NZ}[axis]


def rows_of(order, stage):
    rows = UNIT
    for axis in order[:stage]:
        rows //= axis_size(axis)
    return rows


def own_cells(inp, hid, cells, field, rim):
    ident = eye(PIX)
    for t in range(TPD):
        both = jnp.concatenate([inp[t], hid[t]], axis=0)
        cells[t * PIX : (t + 1) * PIX, :] = nt(ident, both)
    field[...] = cells[...].astype(BF16)
    for t in range(TPD):
        base = t * PIX
        sides = jnp.concatenate(
            [
                cells[base : base + 8, :],
                cells[pl.ds(base + 7, 8, stride=8), :],
                cells[base + 56 : base + 64, :],
                cells[pl.ds(base, 8, stride=8), :],
            ],
            axis=0,
        )
        rim[t * 32 : (t + 1) * 32, :] = sides.astype(BF16)


def source_cells(esrc, ecode, csrc, ccode, by_tile, index):
    lane, row = iota((4, 128), 1), iota((4, 128), 0)
    edge_lane = ((lane < 32) & (lax.div(lane, 8) == row)).astype(F32).astype(BF16)
    corner_lane = (lane - 32 == row).astype(F32).astype(BF16)

    def spread(edges, corners):
        wide = tn(edges[...].astype(F32).astype(BF16), edge_lane)
        wide += tn(corners[...].astype(F32).astype(BF16), corner_lane)
        return wide.astype(I32)

    source, code = spread(esrc, csrc), spread(ecode, ccode)
    lane = iota(source.shape, 1)
    cell = lane & 7
    along_side = (code >> 1) * 8 + jnp.where((code & 1) == 1, 7 - cell, cell)
    at_corner = jnp.where(
        code == 0, 0, jnp.where(code == 1, 7, jnp.where(code == 2, 23, 16))
    )
    by_tile[...] = source * 32 + jnp.where(lane < 32, along_side, at_corner)
    devices = index.shape[0]
    rows = [by_tile[pl.ds(i, devices, stride=TPD), :] for i in range(TPD)]
    index[...] = jnp.concatenate(
        [r[:, :32] for r in rows]
        + [r[:, 32:36] for r in rows]
        + [jnp.full((devices, 128 - 36 * TPD), -1000000, I32)],
        axis=1,
    )


def whole_kernel(
    inp,
    hid,
    cell_prev,
    kern_hbm,
    gate_bias,
    hidden_up,
    cell_up,
    esrc,
    ecode,
    csrc,
    ccode,
    hidden_out,
    cell_out,
    cell_grad_out,
    grad_out,
    bias_out,
    inner_out,
    side_out,
    kern,
    kern_sem,
    cells,
    field,
    rim,
    by_tile,
    index,
    table,
    picked,
    arrived,
    field_all,
    margin_all,
    wide,
    windows,
    accs,
    grad,
    bias,
    dpad,
    dpad_in,
    dsum,
    margin_own,
    margin_send,
    margin_in,
    slot_sum,
    slot_send,
    slot_in,
    bias_in_q,
    bias_mid,
    bias_in_z,
    *rest,
):
    jobs = len(JOBS)
    landing = [rest[5 * j : 5 * j + 3] for j in range(jobs)]
    passing = [rest[5 * j + 3 : 5 * j + 5] for j in range(jobs)]
    small_s, small_r, job_s, job_r = rest[5 * jobs :]
    q, y, x, z, c = position()
    here = {"x": x, "y": y, "z": z}
    to = peers()

    greeted = greet(to)
    load = pltpu.make_async_copy(kern_hbm, kern, kern_sem)
    load.start()
    own_cells(inp, hid, cells, field, rim)
    pl.semaphore_wait(pltpu.get_barrier_semaphore(), greeted)

    for d in range(1, NZ):
        send(rim, table.at[z], small_s.at[5], small_r.at[5], to["z"](d))
    for d in range(1, NC):
        send(field, field_all.at[c], small_s.at[6], small_r.at[6], to["c"](d))
    table[z] = rim[...]
    field_all[c] = field[...]
    source_cells(esrc, ecode, csrc, ccode, by_tile, index)

    first = q * (NZ * RIM)
    choosers = []
    for d in range(NQ):
        row = index[pl.ds(lax.rem(q + d, NQ) * NZ + z, 1), :]
        down = jnp.broadcast_to((row - first).astype(F32), (128, 128)).T
        choosers.append(
            jnp.concatenate(
                [
                    (down == (iota((128, 128), 1) + 128 * k).astype(F32)).astype(BF16)
                    for k in range(NZ * RIM // 128)
                ],
                axis=1,
            )
        )
    await_bytes(table.at[pl.ds(0, NZ - 1)], small_r.at[5])
    rims = table[...].reshape(NZ * RIM, 128)
    for d in list(range(1, NQ)) + [0]:
        picked[d] = nn(choosers[d], rims)[:MARGIN].astype(BF16)
        if d:
            send(picked.at[d], arrived.at[d - 1], small_s.at[7], small_r.at[7], to["q"](d))

    def lanes(ref, k):
        pair, half = 2 * (k % 2), 64 * (k // 2)
        return jnp.concatenate(
            [ref[pair][:, half : half + 64], ref[pair + 1][:, half : half + 64]], axis=1
        ).astype(F32)

    await_bytes(field_all.at[pl.ds(0, NC - 1)], small_r.at[6])
    for k in range(4):
        body = lanes(field_all, k)
        for t in range(TPD):
            wide[1, k, t * 80 + 8 : t * 80 + 72, :] = body[t * PIX : (t + 1) * PIX]

    await_bytes(arrived, small_r.at[7])
    total = picked[0].astype(F32)
    for d in range(1, NQ):
        total += arrived[d - 1].astype(F32)
    margin_all[c] = total.astype(BF16)
    for d in range(1, NC):
        send(margin_all.at[c], margin_all.at[c], small_s.at[8], small_r.at[8], to["c"](d))
    load.wait()
    await_bytes(margin_all.at[pl.ds(0, NC - 1)], small_r.at[8])

    for k in range(4):
        margin = lanes(margin_all, k)
        for t in range(TPD):
            base, at = t * 80, t * 32
            wide[1, k, base : base + 8, :] = margin[at : at + 8]
            wide[1, k, base + 72 : base + 80, :] = margin[at + 16 : at + 24]
        wide[0, k, 1:BODY, :] = wide[1, k, 0 : BODY - 1, :]
        wide[2, k, 0 : BODY - 1, :] = wide[1, k, 1:BODY, :]
        for t in range(TPD):
            base, at, corner = t * 80, t * 32, RIM + t * 4
            left, right = wide.at[0, k], wide.at[2, k]
            left[base : base + 1, :] = margin[corner : corner + 1]
            left[pl.ds(base + 8, 8, stride=8), :] = margin[at + 24 : at + 32]
            left[base + 72 : base + 73, :] = margin[corner + 3 : corner + 4]
            right[base + 7 : base + 8, :] = margin[corner + 1 : corner + 2]
            right[pl.ds(base + 15, 8, stride=8), :] = margin[at + 8 : at + 16]
            right[base + 79 : base + 80, :] = margin[corner + 2 : corner + 3]
    for o in range(9):
        a, b = o // 3, o % 3
        for k in range(4):
            for t in range(TPD):
                base = t * 80 + a * 8
                windows[o, t * PIX : (t + 1) * PIX, k * 128 : (k + 1) * 128] = wide[
                    b, k, base : base + PIX, :
                ].astype(BF16)

    def gate(k):
        column = jnp.broadcast_to(gate_bias[k : k + 1, :], (64, 64)).T
        return jnp.concatenate([column] * TPD, axis=1)

    gates = jnp.concatenate([gate(k) for k in range(4)], axis=0)
    for o in range(9):
        gates = gates + nt(kern[o], windows[o])
    in_gate = jax.nn.sigmoid(gates[0:64])
    forget = jax.nn.sigmoid(gates[64:128])
    cand = jnp.tanh(gates[128:192])
    out_gate = jax.nn.sigmoid(gates[192:256])
    before = jnp.concatenate([cell_prev[t] for t in range(TPD)], axis=1)
    above = jnp.concatenate([cell_up[t] for t in range(TPD)], axis=1)
    upstream = jnp.concatenate([hidden_up[t].astype(F32) for t in range(TPD)], axis=1)
    cell_new = forget * before + in_gate * cand
    squashed = jnp.tanh(cell_new)
    hidden_new = (out_gate * squashed).astype(BF16)
    dcell = above + upstream * out_gate * (1.0 - squashed * squashed)
    cell_grad = dcell * forget
    dgates = jnp.concatenate(
        [
            dcell * cand * in_gate * (1.0 - in_gate),
            dcell * before * forget * (1.0 - forget),
            dcell * in_gate * (1.0 - cand * cand),
            upstream * squashed * out_gate * (1.0 - out_gate),
        ],
        axis=0,
    ).astype(BF16)

    def start_of(j, stage):
        start, rows = j * UNIT, UNIT
        for axis in JOBS[j][:stage]:
            rows //= axis_size(axis)
            start = start + here[axis] * rows
        return pl.multiple_of(start, 16) if stage else start

    def scatter(j, stage):
        axis = JOBS[j][stage]
        size, rows = axis_size(axis), rows_of(JOBS[j], stage + 1)
        for d in range(1, size):
            chunk = lax.rem(here[axis] + d, size) * rows
            if stage == 0:
                src = grad.at[pl.ds(pl.multiple_of(j * UNIT + chunk, 16), rows)]
            else:
                src = passing[j][stage - 1].at[pl.ds(pl.multiple_of(chunk, 16), rows)]
            send(
                src,
                landing[j][stage].at[d - 1],
                job_s.at[j, stage],
                job_r.at[j, stage],
                to[axis](d),
            )

    def gather(j, stage):
        axis = JOBS[j][stage]
        size, rows = axis_size(axis), rows_of(JOBS[j], stage + 1)
        mine = grad_out.at[pl.ds(start_of(j, stage + 1), rows)]
        for d in range(1, size):
            send(mine, mine, job_s.at[j, 3 + stage], job_r.at[j, 3 + stage], to[axis](d))

    def add_up(j, stage):
        axis = JOBS[j][stage]
        rows = rows_of(JOBS[j], stage + 1)
        await_bytes(landing[j][stage], job_r.at[j, stage])
        mine = here[axis] * rows
        if stage == 0:
            source, mine = grad, j * UNIT + mine
        else:
            source = passing[j][stage - 1]
        total = source[pl.ds(pl.multiple_of(mine, 16), rows), :].astype(F32)
        for d in range(axis_size(axis) - 1):
            total += landing[j][stage][d].astype(F32)
        if stage < 2:
            passing[j][stage][...] = total.astype(BF16)
        else:
            grad_out[pl.ds(start_of(j, 3), rows), :] = total.astype(BF16)

    def gathered(j, stage):
        axis = JOBS[j][stage]
        rows = rows_of(JOBS[j], stage + 1) * (axis_size(axis) - 1)
        await_bytes(grad_out.at[pl.ds(0, rows)], job_r.at[j, 3 + stage])

    for j in range(jobs):
        product = nn(dgates, windows[j]).astype(BF16)
        for k in range(4):
            at = j * UNIT + k * 256
            grad[at : at + 256, :] = product[:, k * 128 : (k + 1) * 128]
        scatter(j, 0)

    turned = nt(eye(TPD * PIX), dgates).astype(BF16)
    accs[...] = jnp.zeros(accs.shape, F32)
    for o in range(9):
        a, b = o // 3, o % 3
        product = nn(turned, kern[o])
        for k in range(4):
            for t in range(TPD):
                base = 8 + t * 80 + a * 8
                accs[b, k, base : base + PIX, :] += product[
                    t * PIX : (t + 1) * PIX, k * 128 : (k + 1) * 128
                ]
    column = iota((BODY, 128), 0) & 7
    blocks = []
    for k in range(4):
        body = accs[1, k, 8 : 8 + BODY, :]
        body += jnp.where(column < 7, accs[0, k, 9 : 9 + BODY, :], 0.0)
        body += jnp.where(column > 0, accs[2, k, 7 : 7 + BODY, :], 0.0)
        left, right = accs.at[0, k], accs.at[2, k]
        blocks.append(
            (
                body,
                left[pl.ds(8, 32, stride=8), :],
                right[pl.ds(15, 32, stride=8), :],
            )
        )
    for e in range(NC):
        half = slice((e % 2) * 64, (e % 2) * 64 + 64)
        start = 0
        for one, two in zip(blocks[e // 2], blocks[2 + e // 2]):
            rows = one.shape[0]
            dpad[e, start : start + rows, :] = jnp.concatenate(
                [one[:, half], two[:, half]], axis=1
            ).astype(BF16)
            start += rows
    for d in range(1, NC):
        send(
            dpad.at[lax.rem(c + d, NC)],
            dpad_in.at[d - 1],
            small_s.at[0],
            small_r.at[0],
            to["c"](d),
        )
    bias[...] = nt(jnp.ones((8, TPD * PIX), BF16), dgates)
    for d in range(1, NQ):
        send(bias, bias_in_q.at[d - 1], small_s.at[1], small_r.at[1], to["q"](d))
    for t in range(TPD):
        at = slice(t * PIX, (t + 1) * PIX)
        hidden_out[t] = hidden_new[:, at]
        cell_out[t] = cell_new[:, at]
        cell_grad_out[t] = cell_grad[:, at]

    await_bytes(dpad_in, small_r.at[0])
    total = dpad[c].astype(F32)
    for d in range(NC - 1):
        total += dpad_in[d].astype(F32)
    dsum[...] = total
    left, right = BODY, BODY + 32
    margin_own[...] = jnp.zeros(margin_own.shape, F32)
    for t in range(TPD):
        base, at, corner, col = t * 80, t * 32, RIM + t * 4, t * 10
        margin_own[at : at + 8, :] = dsum[base : base + 8, :]
        margin_own[at + 8 : at + 16, :] = dsum[right + col + 1 : right + col + 9, :]
        margin_own[at + 16 : at + 24, :] = dsum[base + 72 : base + 80, :]
        margin_own[at + 24 : at + 32, :] = dsum[left + col + 1 : left + col + 9, :]
        margin_own[corner : corner + 1, :] = dsum[left + col : left + col + 1, :]
        margin_own[corner + 1 : corner + 2, :] = dsum[right + col : right + col + 1, :]
        margin_own[corner + 2 : corner + 3, :] = dsum[right + col + 9 : right + col + 10, :]
        margin_own[corner + 3 : corner + 4, :] = dsum[left + col + 9 : left + col + 10, :]
        inner_out[t * PIX : (t + 1) * PIX, :] = dsum[base + 8 : base + 72, :]
    margin_send[...] = margin_own[...].astype(BF16)
    for d in range(1, NQ):
        send(margin_send, margin_in.at[d - 1], small_s.at[2], small_r.at[2], to["q"](d))

    for j in range(jobs):
        add_up(j, 0)
        scatter(j, 1)

    choosers = []
    for d in range(NQ):
        row = index[pl.ds(lax.rem(q + NQ - d, NQ) * NZ + z, 1), :][:, :MARGIN]
        chooser = (iota((NZ * RIM, MARGIN), 0) == row - first).astype(F32).astype(BF16)
        choosers.append(chooser)
    await_bytes(margin_in, small_r.at[2])
    sums = nn(choosers[0], margin_send[...])
    for d in range(1, NQ):
        sums += nn(choosers[d], margin_in[d - 1])
    slot_sum[...] = sums.reshape(NZ, RIM, 128)
    slot_send[...] = slot_sum[...].astype(BF16)
    for d in range(1, NZ):
        send(
            slot_send.at[lax.rem(z + d, NZ)],
            slot_in.at[d - 1],
            small_s.at[3],
            small_r.at[3],
            to["z"](d),
        )
    await_bytes(bias_in_q, small_r.at[1])
    total = bias[...]
    for d in range(NQ - 1):
        total += bias_in_q[d]
    bias_mid[...] = total
    for d in range(1, NZ):
        send(bias_mid, bias_in_z.at[d - 1], small_s.at[4], small_r.at[4], to["z"](d))

    for j in range(jobs):
        add_up(j, 1)
        scatter(j, 2)

    await_bytes(slot_in, small_r.at[3])
    total = slot_sum[z]
    for d in range(NZ - 1):
        total += slot_in[d].astype(F32)
    side_out[...] = total
    await_bytes(bias_in_z, small_r.at[4])
    total = bias_mid[...]
    for d in range(NZ - 1):
        total += bias_in_z[d]
    bias_out[...] = total

    for j in range(jobs):
        add_up(j, 2)
        gather(j, 2)
    for stage in (2, 1):
        for j in range(jobs):
            gathered(j, stage)
            gather(j, stage - 1)
    for j in range(jobs):
        gathered(j, 0)

    await_bytes(dpad_in, small_s.at[0])
    await_bytes(bias_in_q, small_s.at[1])
    await_bytes(margin_in, small_s.at[2])
    await_bytes(slot_in, small_s.at[3])
    await_bytes(bias_in_z, small_s.at[4])
    await_bytes(table.at[pl.ds(0, NZ - 1)], small_s.at[5])
    await_bytes(field_all.at[pl.ds(0, NC - 1)], small_s.at[6])
    await_bytes(arrived, small_s.at[7])
    await_bytes(margin_all.at[pl.ds(0, NC - 1)], small_s.at[8])
    for j in range(jobs):
        for stage in range(3):
            await_bytes(landing[j][stage], job_s.at[j, stage])
            axis = JOBS[j][stage]
            rows = rows_of(JOBS[j], stage + 1) * (axis_size(axis) - 1)
            await_bytes(grad_out.at[pl.ds(0, rows)], job_s.at[j, 3 + stage])


def whole(inp, hid, cell_prev, kern, gate_bias, hidden_up, cell_up, lists):
    vmem = pl.BlockSpec(memory_space=pltpu.VMEM)
    state = cell_prev.shape
    devices = NQ * NZ
    scratch = [
        pltpu.VMEM(kern.shape, BF16),
        pltpu.SemaphoreType.DMA,
        pltpu.VMEM((TPD * PIX, 128), F32),
        pltpu.VMEM((TPD * PIX, 128), BF16),
        pltpu.VMEM((RIM, 128), BF16),
        pltpu.VMEM((devices * TPD, 128), I32),
        pltpu.VMEM((devices, 128), I32),
        pltpu.VMEM((NZ, RIM, 128), BF16),
        pltpu.VMEM((NQ, MARGIN, 128), BF16),
        pltpu.VMEM((NQ - 1, MARGIN, 128), BF16),
        pltpu.VMEM((NC, TPD * PIX, 128), BF16),
        pltpu.VMEM((NC, MARGIN, 128), BF16),
        pltpu.VMEM((3, 4, BODY, 128), F32),
        pltpu.VMEM((9, TPD * PIX, 512), BF16),
        pltpu.VMEM((3, 4, 8 + BODY + 32, 128), F32),
        pltpu.VMEM((9 * UNIT, 128), BF16),
        pltpu.VMEM((8, 256), F32),
        pltpu.VMEM((NC, DROWS, 128), BF16),
        pltpu.VMEM((NC - 1, DROWS, 128), BF16),
        pltpu.VMEM((DROWS, 128), F32),
        pltpu.VMEM((MARGIN, 128), F32),
        pltpu.VMEM((MARGIN, 128), BF16),
        pltpu.VMEM((NQ - 1, MARGIN, 128), BF16),
        pltpu.VMEM((NZ, RIM, 128), F32),
        pltpu.VMEM((NZ, RIM, 128), BF16),
        pltpu.VMEM((NZ - 1, RIM, 128), BF16),
        pltpu.VMEM((NQ - 1, 8, 256), F32),
        pltpu.VMEM((8, 256), F32),
        pltpu.VMEM((NZ - 1, 8, 256), F32),
    ]
    for order in JOBS:
        for stage in range(3):
            rows = rows_of(order, stage + 1)
            scratch.append(pltpu.VMEM((axis_size(order[stage]) - 1, rows, 128), BF16))
        for stage in range(2):
            scratch.append(pltpu.VMEM((rows_of(order, stage + 1), 128), BF16))
    scratch += [
        pltpu.SemaphoreType.DMA((9,)),
        pltpu.SemaphoreType.DMA((9,)),
        pltpu.SemaphoreType.DMA((len(JOBS), 6)),
        pltpu.SemaphoreType.DMA((len(JOBS), 6)),
    ]
    return pl.pallas_call(
        whole_kernel,
        out_shape=(
            jax.ShapeDtypeStruct(state, BF16),
            jax.ShapeDtypeStruct(state, F32),
            jax.ShapeDtypeStruct(state, F32),
            jax.ShapeDtypeStruct((9 * UNIT, 128), BF16),
            jax.ShapeDtypeStruct((8, 256), F32),
            jax.ShapeDtypeStruct((TPD * PIX, 128), F32),
            jax.ShapeDtypeStruct((RIM, 128), F32),
        ),
        in_specs=[vmem] * 3 + [pl.BlockSpec(memory_space=pl.ANY)] + [vmem] * 7,
        out_specs=(vmem,) * 7,
        scratch_shapes=scratch,
        compiler_params=pltpu.CompilerParams(
            collective_id=0, has_side_effects=True, vmem_limit_bytes=VMEM_LIMIT
        ),
        name="whole",
    )(inp, hid, cell_prev, kern, gate_bias, hidden_up, cell_up, *lists)


def finish_kernel(
    hidden,
    cell,
    cell_grad,
    grad,
    bias,
    inner,
    sides,
    hidden_out,
    cell_out,
    cell_grad_out,
    grad_out,
    bias_out,
    input_out,
    prior_out,
    held,
    wide,
    cells,
    sems_in,
    sems_out,
):
    def fetch(o):
        return pltpu.make_async_copy(grad.at[o], held.at[o], sems_in.at[o])

    def put(o):
        return pltpu.make_async_copy(wide.at[o], grad_out.at[o], sems_out.at[o])

    for o in range(9):
        fetch(o).start()
    for o in range(9):
        fetch(o).wait()
        for k in range(4):
            wide[o, :, k * 128 : (k + 1) * 128] = held[o, k].astype(F32)
        put(o).start()
    hidden_out[...] = hidden[...]
    cell_out[...] = cell[...]
    cell_grad_out[...] = cell_grad[...]
    for k in range(4):
        bias_out[k : k + 1, :] = bias[0:1, k * 64 : (k + 1) * 64]
    cells[...] = inner[...]
    for t in range(TPD):
        base, at = t * PIX, t * 32
        cells[base : base + 8, :] += sides[at : at + 8, :]
        cells[pl.ds(base + 7, 8, stride=8), :] += sides[at + 8 : at + 16, :]
        cells[base + 56 : base + 64, :] += sides[at + 16 : at + 24, :]
        cells[pl.ds(base, 8, stride=8), :] += sides[at + 24 : at + 32, :]
    ident = eye(128)
    for t in range(TPD):
        rounded = cells[t * PIX : (t + 1) * PIX, :].astype(BF16)
        turned = nt(ident, rounded).astype(BF16)
        input_out[t] = turned[0:64]
        prior_out[t] = turned[64:128]
    for o in range(9):
        put(o).wait()


def finish(hidden, cell, cell_grad, grad, bias, inner, sides):
    vmem, hbm = pl.BlockSpec(memory_space=pltpu.VMEM), pl.BlockSpec(memory_space=pl.ANY)
    return pl.pallas_call(
        finish_kernel,
        out_shape=(
            jax.ShapeDtypeStruct(hidden.shape, BF16),
            jax.ShapeDtypeStruct(hidden.shape, F32),
            jax.ShapeDtypeStruct(hidden.shape, F32),
            jax.ShapeDtypeStruct((9, 256, 512), F32),
            jax.ShapeDtypeStruct((4, 64), F32),
            jax.ShapeDtypeStruct(hidden.shape, BF16),
            jax.ShapeDtypeStruct(hidden.shape, BF16),
        ),
        in_specs=[vmem] * 3 + [hbm] + [vmem] * 3,
        out_specs=(vmem,) * 3 + (hbm,) + (vmem,) * 3,
        scratch_shapes=[
            pltpu.VMEM(grad.shape, BF16),
            pltpu.VMEM((9, 256, 512), F32),
            pltpu.VMEM(inner.shape, F32),
            pltpu.SemaphoreType.DMA((9,)),
            pltpu.SemaphoreType.DMA((9,)),
        ],
        compiler_params=pltpu.CompilerParams(vmem_limit_bytes=VMEM_LIMIT),
        name="finish",
    )(hidden, cell, cell_grad, grad, bias, inner, sides)


def local(
    inputs,
    prior_hidden_state,
    cell_prev,
    kernel,
    gate_bias,
    hidden_upstream,
    cell_upstream,
    edge_source,
    edge_code,
    corner_source,
    corner_code,
):
    hidden_new, cell_new, cell_grad, grad, bias, inner, sides = whole(
        inputs,
        prior_hidden_state,
        cell_prev,
        kernel.reshape(9, 256, 512),
        gate_bias,
        hidden_upstream,
        cell_upstream,
        [a.T for a in (edge_source, edge_code, corner_source, corner_code)],
    )
    hidden_new, cell_new, cell_grad, kernel_grad, bias_grad, input_grad, hidden_grad = finish(
        hidden_new, cell_new, cell_grad, grad.reshape(9, 4, 256, 128), bias, inner, sides
    )
    return (
        hidden_new,
        cell_new,
        kernel_grad.reshape(9, 4, 64, 512),
        bias_grad,
        input_grad,
        hidden_grad,
        cell_grad,
    )


def solution(mesh):
    tiles, whole = P("tile", "chan", None), P()
    gates = P(None, None, "chan", None)
    bias = P(None, "chan")
    in_specs = (tiles, tiles, tiles, gates, bias, tiles, tiles, whole, whole, whole, whole)
    out_specs = (tiles, tiles, gates, bias, tiles, tiles, tiles)
    return jax.shard_map(local, mesh=mesh, in_specs=in_specs, out_specs=out_specs, check_vma=False)
```

```python
import functools

import jax
import jax.numpy as jnp
from jax import lax
from jax.experimental import pallas as pl
from jax.experimental.pallas import tpu as pltpu
from jax.sharding import PartitionSpec as P

F32, BF16, I32 = jnp.float32, jnp.bfloat16, jnp.int32
MESH = pl.DeviceIdType.MESH
NY, NX, NZ = 2, 4, 8
NQ = NY * NX
NC = 4
TPD = 3
PIX = 64
RIM = 32 * TPD
MARGIN = 112
BODY = 80 * TPD
DROWS = BODY + 64
SHARE = 16
GROUPS = ((0, 3), (3, 6), (6, 9))
ORDERS = ("yxz", "zyx", "yxz", "zxy", "yxz", "zyx", "yxz", "zxy", "zyx")
VMEM_LIMIT = 56 * 1024 * 1024


def nn(a, b):
    return lax.dot_general(a, b, (((1,), (0,)), ((), ())), preferred_element_type=F32)


def tn(a, b):
    return lax.dot_general(a, b, (((0,), (0,)), ((), ())), preferred_element_type=F32)


def nt(a, b):
    return lax.dot_general(a, b, (((1,), (1,)), ((), ())), preferred_element_type=F32)


def iota(shape, dim):
    return lax.broadcasted_iota(I32, shape, dim)


def eye(n):
    return (iota((n, n), 0) == iota((n, n), 1)).astype(BF16)


def position():
    t = lax.axis_index("tile")
    z, q = lax.rem(t, NZ), lax.div(t, NZ)
    return q, lax.div(q, NX), lax.rem(q, NX), z, lax.axis_index("chan")


def peers():
    q, y, x, z, c = position()
    return {
        "z": lambda d: (q * NZ + lax.rem(z + d, NZ), c),
        "q": lambda d: (lax.rem(q + d, NQ) * NZ + z, c),
        "x": lambda d: ((y * NX + lax.rem(x + d, NX)) * NZ + z, c),
        "y": lambda d: ((lax.rem(y + d, NY) * NX + x) * NZ + z, c),
        "c": lambda d: (q * NZ + z, lax.rem(c + d, NC)),
    }


def greet(to):
    barrier = pltpu.get_barrier_semaphore()
    count = 0
    for axis, size in (("z", NZ), ("q", NQ), ("c", NC)):
        for d in range(1, size):
            pl.semaphore_signal(barrier, inc=1, device_id=to[axis](d), device_id_type=MESH)
            count += 1
    return count


def send(src, dst, send_sem, recv_sem, device):
    pltpu.make_async_remote_copy(
        src_ref=src,
        dst_ref=dst,
        send_sem=send_sem,
        recv_sem=recv_sem,
        device_id=device,
        device_id_type=MESH,
    ).start()


def await_bytes(like, sem):
    pltpu.make_async_copy(like, like, sem).wait()


def axis_size(axis):
    return {"x": NX, "y": NY, "z": NZ}[axis]


def ring_steps(o):
    return (NZ // 2, NZ // 2 - 1) if o % 2 == 0 else (NZ // 2 - 1, NZ // 2)


def own_cells(inp, hid, cells, field, rim):
    ident = eye(PIX)
    for t in range(TPD):
        both = jnp.concatenate([inp[t], hid[t]], axis=0)
        cells[t * PIX : (t + 1) * PIX, :] = nt(ident, both)
    field[...] = cells[...].astype(BF16)
    for t in range(TPD):
        base = t * PIX
        sides = jnp.concatenate(
            [
                cells[base : base + 8, :],
                cells[pl.ds(base + 7, 8, stride=8), :],
                cells[base + 56 : base + 64, :],
                cells[pl.ds(base, 8, stride=8), :],
            ],
            axis=0,
        )
        rim[t * 32 : (t + 1) * 32, :] = sides.astype(BF16)


def source_cells(esrc, ecode, csrc, ccode, by_tile, index):
    lane, row = iota((4, 128), 1), iota((4, 128), 0)
    edge_lane = ((lane < 32) & (lax.div(lane, 8) == row)).astype(F32).astype(BF16)
    corner_lane = (lane - 32 == row).astype(F32).astype(BF16)

    def spread(edges, corners):
        wide = tn(edges[...].astype(F32).astype(BF16), edge_lane)
        wide += tn(corners[...].astype(F32).astype(BF16), corner_lane)
        return wide.astype(I32)

    source, code = spread(esrc, csrc), spread(ecode, ccode)
    lane = iota(source.shape, 1)
    cell = lane & 7
    along_side = (code >> 1) * 8 + jnp.where((code & 1) == 1, 7 - cell, cell)
    at_corner = jnp.where(
        code == 0, 0, jnp.where(code == 1, 7, jnp.where(code == 2, 23, 16))
    )
    by_tile[...] = source * 32 + jnp.where(lane < 32, along_side, at_corner)
    devices = index.shape[0]
    rows = [by_tile[pl.ds(i, devices, stride=TPD), :] for i in range(TPD)]
    index[...] = jnp.concatenate(
        [r[:, :32] for r in rows]
        + [r[:, 32:36] for r in rows]
        + [jnp.full((devices, 128 - 36 * TPD), -1000000, I32)],
        axis=1,
    )


def whole_kernel(
    inp,
    hid,
    cell_prev,
    kern_hbm,
    gate_bias,
    hidden_up,
    cell_up,
    esrc,
    ecode,
    csrc,
    ccode,
    hidden_out,
    cell_out,
    cell_grad_out,
    grad_out,
    bias_out,
    inner_out,
    side_out,
    kern,
    kern_sem,
    cells,
    field,
    rim,
    by_tile,
    index,
    table,
    picked,
    arrived,
    field_all,
    margin_all,
    wide,
    windows,
    accs,
    field_near,
    margin_near,
    wide_near,
    windows_near,
    turned_own,
    turned_near,
    grad,
    grad_in,
    gauge,
    bias,
    dpad,
    dpad_in,
    dsum,
    margin_own,
    margin_send,
    margin_in,
    slot_sum,
    slot_send,
    slot_in,
    bias_in_q,
    bias_mid,
    bias_in_z,
    small_s,
    small_r,
    sum_s,
    sum_r,
    all_s,
    all_r,
    ring_s,
    ring_r,
):
    q, y, x, z, c = position()
    to = peers()

    def quarter(d):
        return lax.rem(lax.rem(q + d, NQ), NX)

    greeted = greet(to)
    load = pltpu.make_async_copy(kern_hbm, kern, kern_sem)
    load.start()
    own_cells(inp, hid, cells, field, rim)
    pl.semaphore_wait(pltpu.get_barrier_semaphore(), greeted)

    for d in range(1, NZ):
        send(rim, table.at[z], small_s.at[5], small_r.at[5], to["z"](d))
    for d in range(1, NC):
        send(field, field_all.at[c], small_s.at[6], small_r.at[6], to["c"](d))
    table[z] = rim[...]
    field_all[c] = field[...]
    source_cells(esrc, ecode, csrc, ccode, by_tile, index)

    first = q * (NZ * RIM)
    choosers = []
    for d in range(NQ):
        row = index[pl.ds(lax.rem(q + d, NQ) * NZ + z, 1), :]
        down = jnp.broadcast_to((row - first).astype(F32), (128, 128)).T
        choosers.append(
            jnp.concatenate(
                [
                    (down == (iota((128, 128), 1) + 128 * k).astype(F32)).astype(BF16)
                    for k in range(NZ * RIM // 128)
                ],
                axis=1,
            )
        )
    await_bytes(table.at[pl.ds(0, NZ - 1)], small_r.at[5])
    rims = table[...].reshape(NZ * RIM, 128)
    for d in list(range(1, NQ)) + [0]:
        picked[d] = nn(choosers[d], rims)[:MARGIN].astype(BF16)
        if d:
            send(picked.at[d], arrived.at[d - 1], small_s.at[7], small_r.at[7], to["q"](d))

    def lanes(ref, k):
        pair, half = 2 * (k % 2), 64 * (k // 2)
        return jnp.concatenate(
            [ref[pair][:, half : half + 64], ref[pair + 1][:, half : half + 64]], axis=1
        ).astype(F32)

    await_bytes(field_all.at[pl.ds(0, NC - 1)], small_r.at[6])
    for d in range(1, NQ):
        send(
            field_all.at[quarter(d)],
            field_near.at[d],
            small_s.at[9],
            small_r.at[9],
            to["q"](d),
        )
    field_near[0] = field_all[x]
    for k in range(4):
        body = lanes(field_all, k)
        for t in range(TPD):
            wide[1, k, t * 80 + 8 : t * 80 + 72, :] = body[t * PIX : (t + 1) * PIX]

    await_bytes(arrived, small_r.at[7])
    total = picked[0].astype(F32)
    for d in range(1, NQ):
        total += arrived[d - 1].astype(F32)
    margin_all[c] = total.astype(BF16)
    for d in range(1, NC):
        send(margin_all.at[c], margin_all.at[c], small_s.at[8], small_r.at[8], to["c"](d))
    load.wait()
    await_bytes(margin_all.at[pl.ds(0, NC - 1)], small_r.at[8])
    for d in range(1, NQ):
        send(
            margin_all.at[quarter(d)],
            margin_near.at[d],
            small_s.at[10],
            small_r.at[10],
            to["q"](d),
        )
    margin_near[0] = margin_all[x]

    for k in range(4):
        margin = lanes(margin_all, k)
        for t in range(TPD):
            base, at = t * 80, t * 32
            wide[1, k, base : base + 8, :] = margin[at : at + 8]
            wide[1, k, base + 72 : base + 80, :] = margin[at + 16 : at + 24]
        wide[0, k, 1:BODY, :] = wide[1, k, 0 : BODY - 1, :]
        wide[2, k, 0 : BODY - 1, :] = wide[1, k, 1:BODY, :]
        for t in range(TPD):
            base, at, corner = t * 80, t * 32, RIM + t * 4
            left, right = wide.at[0, k], wide.at[2, k]
            left[base : base + 1, :] = margin[corner : corner + 1]
            left[pl.ds(base + 8, 8, stride=8), :] = margin[at + 24 : at + 32]
            left[base + 72 : base + 73, :] = margin[corner + 3 : corner + 4]
            right[base + 7 : base + 8, :] = margin[corner + 1 : corner + 2]
            right[pl.ds(base + 15, 8, stride=8), :] = margin[at + 8 : at + 16]
            right[base + 79 : base + 80, :] = margin[corner + 2 : corner + 3]
    for o in range(9):
        a, b = o // 3, o % 3
        for k in range(4):
            for t in range(TPD):
                base = t * 80 + a * 8
                windows[o, t * PIX : (t + 1) * PIX, k * 128 : (k + 1) * 128] = wide[
                    b, k, base : base + PIX, :
                ].astype(BF16)

    def gate(k):
        column = jnp.broadcast_to(gate_bias[k : k + 1, :], (64, 64)).T
        return jnp.concatenate([column] * TPD, axis=1)

    gates = jnp.concatenate([gate(k) for k in range(4)], axis=0)
    for o in range(9):
        gates = gates + nt(kern[o], windows[o])
    in_gate = jax.nn.sigmoid(gates[0:64])
    forget = jax.nn.sigmoid(gates[64:128])
    cand = jnp.tanh(gates[128:192])
    out_gate = jax.nn.sigmoid(gates[192:256])
    before = jnp.concatenate([cell_prev[t] for t in range(TPD)], axis=1)
    above = jnp.concatenate([cell_up[t] for t in range(TPD)], axis=1)
    upstream = jnp.concatenate([hidden_up[t].astype(F32) for t in range(TPD)], axis=1)
    cell_new = forget * before + in_gate * cand
    squashed = jnp.tanh(cell_new)
    hidden_new = (out_gate * squashed).astype(BF16)
    dcell = above + upstream * out_gate * (1.0 - squashed * squashed)
    cell_grad = dcell * forget
    dgates = jnp.concatenate(
        [
            dcell * cand * in_gate * (1.0 - in_gate),
            dcell * before * forget * (1.0 - forget),
            dcell * in_gate * (1.0 - cand * cand),
            upstream * squashed * out_gate * (1.0 - out_gate),
        ],
        axis=0,
    ).astype(BF16)

    turned = nt(eye(TPD * PIX), dgates).astype(BF16)
    for h in range(NY):
        turned_own[h] = turned[:, h * 128 : (h + 1) * 128]
    for d in range(1, NQ):
        send(
            turned_own.at[lax.div(lax.rem(q + d, NQ), NX)],
            turned_near.at[d],
            small_s.at[11],
            small_r.at[11],
            to["q"](d),
        )
    turned_near[0] = turned_own[y]

    accs[...] = jnp.zeros(accs.shape, F32)
    for o in range(9):
        a, b = o // 3, o % 3
        product = nn(turned, kern[o])
        for k in range(4):
            for t in range(TPD):
                base = 8 + t * 80 + a * 8
                accs[b, k, base : base + PIX, :] += product[
                    t * PIX : (t + 1) * PIX, k * 128 : (k + 1) * 128
                ]
    column = iota((BODY, 128), 0) & 7
    blocks = []
    for k in range(4):
        body = accs[1, k, 8 : 8 + BODY, :]
        body += jnp.where(column < 7, accs[0, k, 9 : 9 + BODY, :], 0.0)
        body += jnp.where(column > 0, accs[2, k, 7 : 7 + BODY, :], 0.0)
        left, right = accs.at[0, k], accs.at[2, k]
        blocks.append(
            (
                body,
                left[pl.ds(8, 32, stride=8), :],
                right[pl.ds(15, 32, stride=8), :],
            )
        )
    for e in range(NC):
        half = slice((e % 2) * 64, (e % 2) * 64 + 64)
        start = 0
        for one, two in zip(blocks[e // 2], blocks[2 + e // 2]):
            rows = one.shape[0]
            dpad[e, start : start + rows, :] = jnp.concatenate(
                [one[:, half], two[:, half]], axis=1
            ).astype(BF16)
            start += rows
    for d in range(1, NC):
        send(
            dpad.at[lax.rem(c + d, NC)],
            dpad_in.at[d - 1],
            small_s.at[0],
            small_r.at[0],
            to["c"](d),
        )
    bias[...] = nt(jnp.ones((8, TPD * PIX), BF16), dgates)
    for d in range(1, NQ):
        send(bias, bias_in_q.at[d - 1], small_s.at[1], small_r.at[1], to["q"](d))
    for t in range(TPD):
        at = slice(t * PIX, (t + 1) * PIX)
        hidden_out[t] = hidden_new[:, at]
        cell_out[t] = cell_new[:, at]
        cell_grad_out[t] = cell_grad[:, at]

    await_bytes(field_near.at[pl.ds(0, NQ - 1)], small_r.at[9])
    await_bytes(margin_near.at[pl.ds(0, NQ - 1)], small_r.at[10])

    def windows_of(s, carry):
        body, margin = field_near[s].astype(F32), margin_near[s].astype(F32)
        left, right = wide_near.at[0], wide_near.at[2]
        for t in range(TPD):
            base, at = t * 80, t * 32
            wide_near[1, base : base + 8, :] = margin[at : at + 8]
            wide_near[1, base + 8 : base + 72, :] = body[t * PIX : (t + 1) * PIX]
            wide_near[1, base + 72 : base + 80, :] = margin[at + 16 : at + 24]
        wide_near[0, 1:BODY, :] = wide_near[1, 0 : BODY - 1, :]
        wide_near[2, 0 : BODY - 1, :] = wide_near[1, 1:BODY, :]
        for t in range(TPD):
            base, at, corner = t * 80, t * 32, RIM + t * 4
            left[base : base + 1, :] = margin[corner : corner + 1]
            left[pl.ds(base + 8, 8, stride=8), :] = margin[at + 24 : at + 32]
            left[base + 72 : base + 73, :] = margin[corner + 3 : corner + 4]
            right[base + 7 : base + 8, :] = margin[corner + 1 : corner + 2]
            right[pl.ds(base + 15, 8, stride=8), :] = margin[at + 8 : at + 16]
            right[base + 79 : base + 80, :] = margin[corner + 2 : corner + 3]
        for o in range(9):
            for t in range(TPD):
                base = t * 80 + (o // 3) * 8
                row = pl.multiple_of(s * (TPD * PIX) + t * PIX, PIX)
                windows_near[pl.ds(row, PIX), o * 128 : (o + 1) * 128] = wide_near[
                    o % 3, base : base + PIX, :
                ].astype(BF16)
        return carry

    lax.fori_loop(0, NQ, windows_of, 0)
    await_bytes(turned_near.at[pl.ds(0, NQ - 1)], small_r.at[11])
    near = nt(eye(128), turned_near[...].reshape(NQ * TPD * PIX, 128)).astype(BF16)
    for g, (low, high) in enumerate(GROUPS):
        product = nn(near, windows_near[:, low * 128 : high * 128]).astype(BF16)
        for o in range(low, high):
            grad[o] = product[:, (o - low) * 128 : (o - low + 1) * 128]
        for d in range(1, NZ):
            at = pl.multiple_of(lax.rem(z + d, NZ) * SHARE, SHARE)
            send(
                grad.at[pl.ds(low, high - low), pl.ds(at, SHARE)],
                grad_in.at[d - 1, pl.ds(low, high - low)],
                sum_s.at[g],
                sum_r.at[g],
                to["z"](d),
            )

    await_bytes(dpad_in, small_r.at[0])
    total = dpad[c].astype(F32)
    for d in range(NC - 1):
        total += dpad_in[d].astype(F32)
    dsum[...] = total
    left, right = BODY, BODY + 32
    margin_own[...] = jnp.zeros(margin_own.shape, F32)
    for t in range(TPD):
        base, at, corner, col = t * 80, t * 32, RIM + t * 4, t * 10
        margin_own[at : at + 8, :] = dsum[base : base + 8, :]
        margin_own[at + 8 : at + 16, :] = dsum[right + col + 1 : right + col + 9, :]
        margin_own[at + 16 : at + 24, :] = dsum[base + 72 : base + 80, :]
        margin_own[at + 24 : at + 32, :] = dsum[left + col + 1 : left + col + 9, :]
        margin_own[corner : corner + 1, :] = dsum[left + col : left + col + 1, :]
        margin_own[corner + 1 : corner + 2, :] = dsum[right + col : right + col + 1, :]
        margin_own[corner + 2 : corner + 3, :] = dsum[right + col + 9 : right + col + 10, :]
        margin_own[corner + 3 : corner + 4, :] = dsum[left + col + 9 : left + col + 10, :]
        inner_out[t * PIX : (t + 1) * PIX, :] = dsum[base + 8 : base + 72, :]
    margin_send[...] = margin_own[...].astype(BF16)
    for d in range(1, NQ):
        send(margin_send, margin_in.at[d - 1], small_s.at[2], small_r.at[2], to["q"](d))

    choosers = []
    for d in range(NQ):
        row = index[pl.ds(lax.rem(q + NQ - d, NQ) * NZ + z, 1), :][:, :MARGIN]
        chooser = (iota((NZ * RIM, MARGIN), 0) == row - first).astype(F32).astype(BF16)
        choosers.append(chooser)
    await_bytes(margin_in, small_r.at[2])
    sums = nn(choosers[0], margin_send[...])
    for d in range(1, NQ):
        sums += nn(choosers[d], margin_in[d - 1])
    slot_sum[...] = sums.reshape(NZ, RIM, 128)
    slot_send[...] = slot_sum[...].astype(BF16)
    for d in range(1, NZ):
        send(
            slot_send.at[lax.rem(z + d, NZ)],
            slot_in.at[d - 1],
            small_s.at[3],
            small_r.at[3],
            to["z"](d),
        )
    await_bytes(bias_in_q, small_r.at[1])
    total = bias[...]
    for d in range(NQ - 1):
        total += bias_in_q[d]
    bias_mid[...] = total
    for d in range(1, NZ):
        send(bias_mid, bias_in_z.at[d - 1], small_s.at[4], small_r.at[4], to["z"](d))

    def box(o, full, at_z=None):
        return grad_out.at[
            o,
            slice(None) if "x" in full else x,
            slice(None) if "y" in full else y,
            slice(None) if "z" in full else (z if at_z is None else at_z),
        ]

    def box_rows(full):
        rows = SHARE
        for axis in full:
            rows *= axis_size(axis)
        return rows

    def bytes_of(rows):
        return gauge.at[pl.ds(0, rows)]

    def on_ring(o, stage):
        return stage == 2 and ORDERS[o][2] == "z"

    def ring_send(o, step, side):
        share = lax.rem(z + NZ + (1 - step if side == 0 else step - 1), NZ)
        mine = box(o, "xy", share)
        at = (o, side * (NZ // 2) + step - 1)
        send(mine, mine, ring_s.at[at], ring_r.at[at], to["z"](1 if side == 0 else NZ - 1))

    def ring_wait(o, step, side):
        await_bytes(bytes_of(box_rows("xy")), ring_r.at[o, side * (NZ // 2) + step - 1])

    def gather(o, stage):
        if on_ring(o, stage):
            for side in range(2):
                ring_send(o, 1, side)
            return
        axis, full = ORDERS[o][stage], ORDERS[o][:stage]
        mine = box(o, full)
        for d in range(1, axis_size(axis)):
            send(mine, mine, all_s.at[o, stage], all_r.at[o, stage], to[axis](d))

    def stage_bytes(o, stage):
        axis, full = ORDERS[o][stage], ORDERS[o][:stage]
        return bytes_of(box_rows(full) * (axis_size(axis) - 1))

    def gathered(o, stage):
        await_bytes(stage_bytes(o, stage), all_r.at[o, stage])

    for g, (low, high) in enumerate(GROUPS):
        some = pl.ds(low, high - low)
        await_bytes(grad_in.at[:, some], sum_r.at[g])
        total = grad[some, pl.ds(pl.multiple_of(z * SHARE, SHARE), SHARE), :].astype(F32)
        for d in range(NZ - 1):
            total += grad_in[d, some].astype(F32)
        for o in range(low, high):
            grad_out[o, x, y, z] = total[o - low].astype(BF16)
            gather(o, 0)

    await_bytes(slot_in, small_r.at[3])
    total = slot_sum[z]
    for d in range(NZ - 1):
        total += slot_in[d].astype(F32)
    side_out[...] = total
    await_bytes(bias_in_z, small_r.at[4])
    total = bias_mid[...]
    for d in range(NZ - 1):
        total += bias_in_z[d]
    bias_out[...] = total

    for stage in (0, 1):
        for o in range(9):
            gathered(o, stage)
            gather(o, stage + 1)
    for step in range(1, NZ // 2 + 1):
        for o in range(9):
            if on_ring(o, 2):
                for side in range(2):
                    if step <= ring_steps(o)[side]:
                        ring_wait(o, step, side)
                    if step < ring_steps(o)[side]:
                        ring_send(o, step + 1, side)
    for o in range(9):
        if not on_ring(o, 2):
            gathered(o, 2)

    await_bytes(dpad_in, small_s.at[0])
    await_bytes(bias_in_q, small_s.at[1])
    await_bytes(margin_in, small_s.at[2])
    await_bytes(slot_in, small_s.at[3])
    await_bytes(bias_in_z, small_s.at[4])
    await_bytes(table.at[pl.ds(0, NZ - 1)], small_s.at[5])
    await_bytes(field_all.at[pl.ds(0, NC - 1)], small_s.at[6])
    await_bytes(arrived, small_s.at[7])
    await_bytes(margin_all.at[pl.ds(0, NC - 1)], small_s.at[8])
    for near, sem in ((field_near, 9), (margin_near, 10), (turned_near, 11)):
        await_bytes(near.at[pl.ds(0, NQ - 1)], small_s.at[sem])
    for g, (low, high) in enumerate(GROUPS):
        await_bytes(grad_in.at[:, pl.ds(low, high - low)], sum_s.at[g])
    for o in range(9):
        for stage in range(3):
            if not on_ring(o, stage):
                await_bytes(stage_bytes(o, stage), all_s.at[o, stage])
                continue
            for side in range(2):
                for step in range(ring_steps(o)[side]):
                    await_bytes(
                        bytes_of(box_rows("xy")), ring_s.at[o, side * (NZ // 2) + step]
                    )


def whole(inp, hid, cell_prev, kern, gate_bias, hidden_up, cell_up, lists):
    vmem = pl.BlockSpec(memory_space=pltpu.VMEM)
    state = cell_prev.shape
    devices = NQ * NZ
    scratch = [
        pltpu.VMEM(kern.shape, BF16),
        pltpu.SemaphoreType.DMA,
        pltpu.VMEM((TPD * PIX, 128), F32),
        pltpu.VMEM((TPD * PIX, 128), BF16),
        pltpu.VMEM((RIM, 128), BF16),
        pltpu.VMEM((devices * TPD, 128), I32),
        pltpu.VMEM((devices, 128), I32),
        pltpu.VMEM((NZ, RIM, 128), BF16),
        pltpu.VMEM((NQ, MARGIN, 128), BF16),
        pltpu.VMEM((NQ - 1, MARGIN, 128), BF16),
        pltpu.VMEM((NC, TPD * PIX, 128), BF16),
        pltpu.VMEM((NC, MARGIN, 128), BF16),
        pltpu.VMEM((3, 4, BODY, 128), F32),
        pltpu.VMEM((9, TPD * PIX, 512), BF16),
        pltpu.VMEM((3, 4, 8 + BODY + 32, 128), F32),
        pltpu.VMEM((NQ, TPD * PIX, 128), BF16),
        pltpu.VMEM((NQ, MARGIN, 128), BF16),
        pltpu.VMEM((3, BODY, 128), F32),
        pltpu.VMEM((NQ * TPD * PIX, 9 * 128), BF16),
        pltpu.VMEM((NY, TPD * PIX, 128), BF16),
        pltpu.VMEM((NQ, TPD * PIX, 128), BF16),
        pltpu.VMEM((9, 128, 128), BF16),
        pltpu.VMEM((NZ - 1, 9, SHARE, 128), BF16),
        pltpu.VMEM((1024, 128), BF16),
        pltpu.VMEM((8, 256), F32),
        pltpu.VMEM((NC, DROWS, 128), BF16),
        pltpu.VMEM((NC - 1, DROWS, 128), BF16),
        pltpu.VMEM((DROWS, 128), F32),
        pltpu.VMEM((MARGIN, 128), F32),
        pltpu.VMEM((MARGIN, 128), BF16),
        pltpu.VMEM((NQ - 1, MARGIN, 128), BF16),
        pltpu.VMEM((NZ, RIM, 128), F32),
        pltpu.VMEM((NZ, RIM, 128), BF16),
        pltpu.VMEM((NZ - 1, RIM, 128), BF16),
        pltpu.VMEM((NQ - 1, 8, 256), F32),
        pltpu.VMEM((8, 256), F32),
        pltpu.VMEM((NZ - 1, 8, 256), F32),
    ]
    for shape in ((12,), (len(GROUPS),), (9, 3), (9, NZ)):
        scratch += [pltpu.SemaphoreType.DMA(shape)] * 2
    return pl.pallas_call(
        whole_kernel,
        out_shape=(
            jax.ShapeDtypeStruct(state, BF16),
            jax.ShapeDtypeStruct(state, F32),
            jax.ShapeDtypeStruct(state, F32),
            jax.ShapeDtypeStruct((9, NX, NY, NZ, SHARE, 128), BF16),
            jax.ShapeDtypeStruct((8, 256), F32),
            jax.ShapeDtypeStruct((TPD * PIX, 128), F32),
            jax.ShapeDtypeStruct((RIM, 128), F32),
        ),
        in_specs=[vmem] * 3 + [pl.BlockSpec(memory_space=pl.ANY)] + [vmem] * 7,
        out_specs=(vmem,) * 7,
        scratch_shapes=scratch,
        compiler_params=pltpu.CompilerParams(
            collective_id=0, has_side_effects=True, vmem_limit_bytes=VMEM_LIMIT
        ),
        name="whole",
    )(inp, hid, cell_prev, kern, gate_bias, hidden_up, cell_up, *lists)


def finish_kernel(
    hidden,
    cell,
    cell_grad,
    grad,
    bias,
    inner,
    sides,
    hidden_out,
    cell_out,
    cell_grad_out,
    grad_out,
    bias_out,
    input_out,
    prior_out,
    held,
    wide,
    cells,
    sems_in,
    sems_out,
):
    def fetch(o):
        return pltpu.make_async_copy(grad.at[o], held.at[o], sems_in.at[o])

    def put(o):
        return pltpu.make_async_copy(wide.at[o], grad_out.at[o], sems_out.at[o])

    for o in range(9):
        fetch(o).start()
    for o in range(9):
        fetch(o).wait()
        for k in range(4):
            pair, half = 2 * (k % 2), 64 * (k // 2)
            wide[o, :, k * 128 : (k + 1) * 128] = jnp.concatenate(
                [held[o, pair, :, half : half + 64], held[o, pair + 1, :, half : half + 64]],
                axis=1,
            ).astype(F32)
        put(o).start()
    hidden_out[...] = hidden[...]
    cell_out[...] = cell[...]
    cell_grad_out[...] = cell_grad[...]
    for k in range(4):
        bias_out[k : k + 1, :] = bias[0:1, k * 64 : (k + 1) * 64]
    cells[...] = inner[...]
    for t in range(TPD):
        base, at = t * PIX, t * 32
        cells[base : base + 8, :] += sides[at : at + 8, :]
        cells[pl.ds(base + 7, 8, stride=8), :] += sides[at + 8 : at + 16, :]
        cells[base + 56 : base + 64, :] += sides[at + 16 : at + 24, :]
        cells[pl.ds(base, 8, stride=8), :] += sides[at + 24 : at + 32, :]
    ident = eye(128)
    for t in range(TPD):
        rounded = cells[t * PIX : (t + 1) * PIX, :].astype(BF16)
        turned = nt(ident, rounded).astype(BF16)
        input_out[t] = turned[0:64]
        prior_out[t] = turned[64:128]
    for o in range(9):
        put(o).wait()


def finish(hidden, cell, cell_grad, grad, bias, inner, sides):
    vmem, hbm = pl.BlockSpec(memory_space=pltpu.VMEM), pl.BlockSpec(memory_space=pl.ANY)
    return pl.pallas_call(
        finish_kernel,
        out_shape=(
            jax.ShapeDtypeStruct(hidden.shape, BF16),
            jax.ShapeDtypeStruct(hidden.shape, F32),
            jax.ShapeDtypeStruct(hidden.shape, F32),
            jax.ShapeDtypeStruct((9, 256, 512), F32),
            jax.ShapeDtypeStruct((4, 64), F32),
            jax.ShapeDtypeStruct(hidden.shape, BF16),
            jax.ShapeDtypeStruct(hidden.shape, BF16),
        ),
        in_specs=[vmem] * 3 + [hbm] + [vmem] * 3,
        out_specs=(vmem,) * 3 + (hbm,) + (vmem,) * 3,
        scratch_shapes=[
            pltpu.VMEM(grad.shape, BF16),
            pltpu.VMEM((9, 256, 512), F32),
            pltpu.VMEM(inner.shape, F32),
            pltpu.SemaphoreType.DMA((9,)),
            pltpu.SemaphoreType.DMA((9,)),
        ],
        compiler_params=pltpu.CompilerParams(vmem_limit_bytes=VMEM_LIMIT),
        name="finish",
    )(hidden, cell, cell_grad, grad, bias, inner, sides)


def local(
    inputs,
    prior_hidden_state,
    cell_prev,
    kernel,
    gate_bias,
    hidden_upstream,
    cell_upstream,
    edge_source,
    edge_code,
    corner_source,
    corner_code,
):
    hidden_new, cell_new, cell_grad, grad, bias, inner, sides = whole(
        inputs,
        prior_hidden_state,
        cell_prev,
        kernel.reshape(9, 256, 512),
        gate_bias,
        hidden_upstream,
        cell_upstream,
        [a.T for a in (edge_source, edge_code, corner_source, corner_code)],
    )
    hidden_new, cell_new, cell_grad, kernel_grad, bias_grad, input_grad, hidden_grad = finish(
        hidden_new, cell_new, cell_grad, grad.reshape(9, NX, NY * NZ * SHARE, 128), bias, inner, sides
    )
    return (
        hidden_new,
        cell_new,
        kernel_grad.reshape(9, 4, 64, 512),
        bias_grad,
        input_grad,
        hidden_grad,
        cell_grad,
    )


def solution(mesh):
    tiles, whole = P("tile", "chan", None), P()
    gates = P(None, None, "chan", None)
    bias = P(None, "chan")
    in_specs = (tiles, tiles, tiles, gates, bias, tiles, tiles, whole, whole, whole, whole)
    out_specs = (tiles, tiles, gates, bias, tiles, tiles, tiles)
    return jax.shard_map(local, mesh=mesh, in_specs=in_specs, out_specs=out_specs, check_vma=False)
```

```python
import functools

import jax
import jax.numpy as jnp
from jax import lax
from jax.experimental import pallas as pl
from jax.experimental.pallas import tpu as pltpu
from jax.sharding import PartitionSpec as P

F32, BF16, I32 = jnp.float32, jnp.bfloat16, jnp.int32
MESH = pl.DeviceIdType.MESH
NY, NX, NZ = 2, 4, 8
NQ = NY * NX
NC = 4
TPD = 3
PIX = 64
RIM = 32 * TPD
MARGIN = 112
BODY = 80 * TPD
DROWS = BODY + 64
SHARE = 16
GROUPS = ((0, 3), (3, 6), (6, 9))
ORDERS = ("yxz", "zyx", "yxz", "zxy", "yxz", "zyx", "yxz", "zxy", "zyx")
VMEM_LIMIT = 56 * 1024 * 1024


def nn(a, b):
    return lax.dot_general(a, b, (((1,), (0,)), ((), ())), preferred_element_type=F32)


def tn(a, b):
    return lax.dot_general(a, b, (((0,), (0,)), ((), ())), preferred_element_type=F32)


def nt(a, b):
    return lax.dot_general(a, b, (((1,), (1,)), ((), ())), preferred_element_type=F32)


def iota(shape, dim):
    return lax.broadcasted_iota(I32, shape, dim)


def eye(n):
    return (iota((n, n), 0) == iota((n, n), 1)).astype(BF16)


def position():
    t = lax.axis_index("tile")
    z, q = lax.rem(t, NZ), lax.div(t, NZ)
    return q, lax.div(q, NX), lax.rem(q, NX), z, lax.axis_index("chan")


def peers():
    q, y, x, z, c = position()
    return {
        "z": lambda d: (q * NZ + lax.rem(z + d, NZ), c),
        "q": lambda d: (lax.rem(q + d, NQ) * NZ + z, c),
        "x": lambda d: ((y * NX + lax.rem(x + d, NX)) * NZ + z, c),
        "y": lambda d: ((lax.rem(y + d, NY) * NX + x) * NZ + z, c),
        "c": lambda d: (q * NZ + z, lax.rem(c + d, NC)),
    }


def greet(to):
    barrier = pltpu.get_barrier_semaphore()
    count = 0
    for axis, size in (("z", NZ), ("q", NQ), ("c", NC)):
        for d in range(1, size):
            pl.semaphore_signal(barrier, inc=1, device_id=to[axis](d), device_id_type=MESH)
            count += 1
    return count


def send(src, dst, send_sem, recv_sem, device):
    pltpu.make_async_remote_copy(
        src_ref=src,
        dst_ref=dst,
        send_sem=send_sem,
        recv_sem=recv_sem,
        device_id=device,
        device_id_type=MESH,
    ).start()


def await_bytes(like, sem):
    pltpu.make_async_copy(like, like, sem).wait()


def axis_size(axis):
    return {"x": NX, "y": NY, "z": NZ}[axis]


def ring_steps(o):
    return (NZ // 2, NZ // 2 - 1) if o % 2 == 0 else (NZ // 2 - 1, NZ // 2)


def own_cells(inp, hid, cells, field, rim):
    ident = eye(PIX)
    for t in range(TPD):
        both = jnp.concatenate([inp[t], hid[t]], axis=0)
        cells[t * PIX : (t + 1) * PIX, :] = nt(ident, both)
    field[...] = cells[...].astype(BF16)
    for t in range(TPD):
        base = t * PIX
        sides = jnp.concatenate(
            [
                cells[base : base + 8, :],
                cells[pl.ds(base + 7, 8, stride=8), :],
                cells[base + 56 : base + 64, :],
                cells[pl.ds(base, 8, stride=8), :],
            ],
            axis=0,
        )
        rim[t * 32 : (t + 1) * 32, :] = sides.astype(BF16)


def source_cells(esrc, ecode, csrc, ccode, by_tile, index):
    lane, row = iota((4, 128), 1), iota((4, 128), 0)
    edge_lane = ((lane < 32) & (lax.div(lane, 8) == row)).astype(F32).astype(BF16)
    corner_lane = (lane - 32 == row).astype(F32).astype(BF16)

    def spread(edges, corners):
        wide = tn(edges[...].astype(F32).astype(BF16), edge_lane)
        wide += tn(corners[...].astype(F32).astype(BF16), corner_lane)
        return wide.astype(I32)

    source, code = spread(esrc, csrc), spread(ecode, ccode)
    lane = iota(source.shape, 1)
    cell = lane & 7
    along_side = (code >> 1) * 8 + jnp.where((code & 1) == 1, 7 - cell, cell)
    at_corner = jnp.where(
        code == 0, 0, jnp.where(code == 1, 7, jnp.where(code == 2, 23, 16))
    )
    by_tile[...] = source * 32 + jnp.where(lane < 32, along_side, at_corner)
    devices = index.shape[0]
    rows = [by_tile[pl.ds(i, devices, stride=TPD), :] for i in range(TPD)]
    index[...] = jnp.concatenate(
        [r[:, :32] for r in rows]
        + [r[:, 32:36] for r in rows]
        + [jnp.full((devices, 128 - 36 * TPD), -1000000, I32)],
        axis=1,
    )


def whole_kernel(
    inp_hbm,
    hid_hbm,
    esrc_hbm,
    ecode_hbm,
    csrc_hbm,
    ccode_hbm,
    cell_prev_hbm,
    bias_hbm,
    hidden_up_hbm,
    cell_up_hbm,
    kern_hbm,
    hidden_hbm,
    cell_hbm,
    cell_grad_hbm,
    grad_hbm,
    bias_sum_hbm,
    inner_hbm,
    side_hbm,
    inp,
    hid,
    esrc,
    ecode,
    csrc,
    ccode,
    cell_prev,
    gate_bias,
    hidden_up,
    cell_up,
    hidden_out,
    cell_out,
    cell_grad_out,
    bias_out,
    inner_out,
    side_out,
    kern,
    cells,
    field,
    rim,
    by_tile,
    index,
    table,
    picked,
    arrived,
    field_all,
    margin_all,
    field_blocks,
    margin_blocks,
    wide,
    accs,
    field_near,
    margin_near,
    wide_near,
    windows_near,
    turned_own,
    turned_near,
    grad,
    grad_in,
    grad_all,
    gauge,
    bias,
    dpad,
    dpad_in,
    dsum,
    margin_own,
    margin_send,
    margin_in,
    slot_sum,
    slot_send,
    slot_in,
    slot_chooser,
    bias_in,
    small_s,
    small_r,
    sum_s,
    sum_r,
    all_s,
    all_r,
    ring_s,
    ring_r,
    out_sems,
    load_sems,
    store_sems,
):
    q, y, x, z, c = position()
    to = peers()

    def quarter(d):
        return lax.rem(lax.rem(q + d, NQ), NX)

    greeted = greet(to)
    loads = [
        pltpu.make_async_copy(far, near, load_sems.at[i])
        for i, (far, near) in enumerate(
            (
                (inp_hbm, inp),
                (hid_hbm, hid),
                (esrc_hbm, esrc),
                (ecode_hbm, ecode),
                (csrc_hbm, csrc),
                (ccode_hbm, ccode),
                (cell_prev_hbm, cell_prev),
                (bias_hbm, gate_bias),
                (hidden_up_hbm, hidden_up),
                (cell_up_hbm, cell_up),
                (kern_hbm, kern),
            )
        )
    ]
    for load in loads:
        load.start()
    stores = [
        pltpu.make_async_copy(near, far, store_sems.at[i])
        for i, (near, far) in enumerate(
            (
                (hidden_out, hidden_hbm),
                (cell_out, cell_hbm),
                (cell_grad_out, cell_grad_hbm),
                (inner_out, inner_hbm),
                (side_out, side_hbm),
                (bias_out, bias_sum_hbm),
            )
        )
    ]
    for load in loads[:2]:
        load.wait()
    own_cells(inp, hid, cells, field, rim)
    margin_in[:, MARGIN:128, :] = jnp.zeros((NQ, 128 - MARGIN, 128), BF16)
    pl.semaphore_wait(pltpu.get_barrier_semaphore(), greeted)

    for d in range(1, NZ):
        send(rim, table.at[z], small_s.at[5], small_r.at[5], to["z"](d))
    for d in range(1, NC):
        send(field, field_all.at[c], small_s.at[6], small_r.at[6], to["c"](d))
    table[z] = rim[...]
    field_all[c] = field[...]
    for load in loads[2:6]:
        load.wait()
    source_cells(esrc, ecode, csrc, ccode, by_tile, index)

    first = q * (NZ * RIM)
    choosers = []
    for d in range(NQ):
        row = index[pl.ds(lax.rem(q + d, NQ) * NZ + z, 1), :]
        down = jnp.broadcast_to((row - first).astype(F32), (128, 128)).T
        choosers.append(
            jnp.concatenate(
                [
                    (down == (iota((128, 128), 1) + 128 * k).astype(F32)).astype(BF16)
                    for k in range(NZ * RIM // 128)
                ],
                axis=1,
            )
        )
    def lanes(ref, k):
        pair, half = 2 * (k % 2), 64 * (k // 2)
        return jnp.concatenate(
            [ref[pair][:, half : half + 64], ref[pair + 1][:, half : half + 64]], axis=1
        )

    await_bytes(field_all.at[pl.ds(0, NC - 1)], small_r.at[6])
    for k in range(4):
        field_blocks[k] = lanes(field_all, k)
    for d in range(1, NQ):
        send(
            field_blocks.at[quarter(d)],
            field_near.at[d],
            small_s.at[9],
            small_r.at[9],
            to["q"](d),
        )
    field_near[0] = field_blocks[x]
    for k in range(4):
        body = field_blocks[k].astype(F32)
        for t in range(TPD):
            base = t * 80
            wide[1, k, base + 8 : base + 72, :] = body[t * PIX : (t + 1) * PIX]
            wide[0, k, base + 9 : base + 72, :] = wide[1, k, base + 8 : base + 71, :]
            wide[2, k, base + 8 : base + 71, :] = wide[1, k, base + 9 : base + 72, :]

    await_bytes(table.at[pl.ds(0, NZ - 1)], small_r.at[5])
    rims = table[...].reshape(NZ * RIM, 128)
    for d in list(range(1, NQ)) + [0]:
        picked[d] = nn(choosers[d], rims)[:MARGIN].astype(BF16)
        if d:
            send(picked.at[d], arrived.at[d - 1], small_s.at[7], small_r.at[7], to["q"](d))

    await_bytes(arrived, small_r.at[7])
    total = picked[0].astype(F32)
    for d in range(1, NQ):
        total += arrived[d - 1].astype(F32)
    margin_all[c] = total.astype(BF16)
    for d in range(1, NC):
        send(margin_all.at[c], margin_all.at[c], small_s.at[8], small_r.at[8], to["c"](d))
    for load in loads[6:]:
        load.wait()
    await_bytes(margin_all.at[pl.ds(0, NC - 1)], small_r.at[8])
    for k in range(4):
        margin_blocks[k] = lanes(margin_all, k)
    for d in range(1, NQ):
        send(
            margin_blocks.at[quarter(d)],
            margin_near.at[d],
            small_s.at[10],
            small_r.at[10],
            to["q"](d),
        )
    margin_near[0] = margin_blocks[x]

    for k in range(4):
        margin = margin_blocks[k].astype(F32)
        left, right = wide.at[0, k], wide.at[2, k]
        for t in range(TPD):
            base, at, corner = t * 80, t * 32, RIM + t * 4
            for row, side in ((base, at), (base + 72, at + 16)):
                wide[1, k, row : row + 8, :] = margin[side : side + 8]
                left[row + 1 : row + 8, :] = margin[side : side + 7]
                right[row : row + 7, :] = margin[side + 1 : side + 8]
            left[base : base + 1, :] = margin[corner : corner + 1]
            left[pl.ds(base + 8, 8, stride=8), :] = margin[at + 24 : at + 32]
            left[base + 72 : base + 73, :] = margin[corner + 3 : corner + 4]
            right[base + 7 : base + 8, :] = margin[corner + 1 : corner + 2]
            right[pl.ds(base + 15, 8, stride=8), :] = margin[at + 8 : at + 16]
            right[base + 79 : base + 80, :] = margin[corner + 2 : corner + 3]

    def window(o):
        start = (o // 3) * 8
        return jnp.concatenate(
            [
                jnp.concatenate(
                    [
                        wide[o % 3, k, t * 80 + start : t * 80 + start + PIX, :]
                        for t in range(TPD)
                    ],
                    axis=0,
                ).astype(BF16)
                for k in range(4)
            ],
            axis=1,
        )

    def gate(k):
        column = jnp.broadcast_to(gate_bias[k : k + 1, :], (64, 64)).T
        return jnp.concatenate([column] * TPD, axis=1)

    gates = jnp.concatenate([gate(k) for k in range(4)], axis=0)
    for o in range(9):
        gates = gates + nt(kern[o], window(o))
    in_gate = jax.nn.sigmoid(gates[0:64])
    forget = jax.nn.sigmoid(gates[64:128])
    cand = jnp.tanh(gates[128:192])
    out_gate = jax.nn.sigmoid(gates[192:256])
    before = jnp.concatenate([cell_prev[t] for t in range(TPD)], axis=1)
    above = jnp.concatenate([cell_up[t] for t in range(TPD)], axis=1)
    upstream = jnp.concatenate([hidden_up[t].astype(F32) for t in range(TPD)], axis=1)
    cell_new = forget * before + in_gate * cand
    squashed = jnp.tanh(cell_new)
    hidden_new = (out_gate * squashed).astype(BF16)
    dcell = above + upstream * out_gate * (1.0 - squashed * squashed)
    cell_grad = dcell * forget
    dgates = jnp.concatenate(
        [
            dcell * cand * in_gate * (1.0 - in_gate),
            dcell * before * forget * (1.0 - forget),
            dcell * in_gate * (1.0 - cand * cand),
            upstream * squashed * out_gate * (1.0 - out_gate),
        ],
        axis=0,
    ).astype(BF16)

    turned = nt(eye(TPD * PIX), dgates).astype(BF16)
    for h in range(NY):
        turned_own[h] = turned[:, h * 128 : (h + 1) * 128]
    for d in range(1, NQ):
        send(
            turned_own.at[lax.div(lax.rem(q + d, NQ), NX)],
            turned_near.at[d],
            small_s.at[11],
            small_r.at[11],
            to["q"](d),
        )
    turned_near[0] = turned_own[y]

    accs[...] = jnp.zeros(accs.shape, F32)
    for o in range(9):
        a, b = o // 3, o % 3
        product = nn(turned, kern[o])
        for k in range(4):
            for t in range(TPD):
                base = 8 + t * 80 + a * 8
                accs[b, k, base : base + PIX, :] += product[
                    t * PIX : (t + 1) * PIX, k * 128 : (k + 1) * 128
                ]
    column = iota((BODY, 128), 0) & 7
    blocks = []
    for k in range(4):
        body = accs[1, k, 8 : 8 + BODY, :]
        body += jnp.where(column < 7, accs[0, k, 9 : 9 + BODY, :], 0.0)
        body += jnp.where(column > 0, accs[2, k, 7 : 7 + BODY, :], 0.0)
        left, right = accs.at[0, k], accs.at[2, k]
        blocks.append(
            (
                body,
                left[pl.ds(8, 32, stride=8), :],
                right[pl.ds(15, 32, stride=8), :],
            )
        )
    for e in range(NC):
        half = slice((e % 2) * 64, (e % 2) * 64 + 64)
        start = 0
        for one, two in zip(blocks[e // 2], blocks[2 + e // 2]):
            rows = one.shape[0]
            dpad[e, start : start + rows, :] = jnp.concatenate(
                [one[:, half], two[:, half]], axis=1
            ).astype(BF16)
            start += rows
    for t in range(TPD):
        at = slice(t * PIX, (t + 1) * PIX)
        hidden_out[t] = hidden_new[:, at]
        cell_out[t] = cell_new[:, at]
        cell_grad_out[t] = cell_grad[:, at]
    for store in stores[:3]:
        store.start()

    await_bytes(field_near.at[pl.ds(0, NQ - 1)], small_r.at[9])
    await_bytes(margin_near.at[pl.ds(0, NQ - 1)], small_r.at[10])

    def windows_of(s, carry):
        body, margin = field_near[s].astype(F32), margin_near[s].astype(F32)
        left, right = wide_near.at[0], wide_near.at[2]
        for t in range(TPD):
            base, at = t * 80, t * 32
            wide_near[1, base : base + 8, :] = margin[at : at + 8]
            wide_near[1, base + 8 : base + 72, :] = body[t * PIX : (t + 1) * PIX]
            wide_near[1, base + 72 : base + 80, :] = margin[at + 16 : at + 24]
        wide_near[0, 1:BODY, :] = wide_near[1, 0 : BODY - 1, :]
        wide_near[2, 0 : BODY - 1, :] = wide_near[1, 1:BODY, :]
        for t in range(TPD):
            base, at, corner = t * 80, t * 32, RIM + t * 4
            left[base : base + 1, :] = margin[corner : corner + 1]
            left[pl.ds(base + 8, 8, stride=8), :] = margin[at + 24 : at + 32]
            left[base + 72 : base + 73, :] = margin[corner + 3 : corner + 4]
            right[base + 7 : base + 8, :] = margin[corner + 1 : corner + 2]
            right[pl.ds(base + 15, 8, stride=8), :] = margin[at + 8 : at + 16]
            right[base + 79 : base + 80, :] = margin[corner + 2 : corner + 3]
        for o in range(9):
            for t in range(TPD):
                base = t * 80 + (o // 3) * 8
                row = pl.multiple_of(s * (TPD * PIX) + t * PIX, PIX)
                windows_near[pl.ds(row, PIX), o * 128 : (o + 1) * 128] = wide_near[
                    o % 3, base : base + PIX, :
                ].astype(BF16)
        return carry

    lax.fori_loop(0, NQ, windows_of, 0)
    await_bytes(turned_near.at[pl.ds(0, NQ - 1)], small_r.at[11])
    near = nt(eye(128), turned_near[...].reshape(NQ * TPD * PIX, 128)).astype(BF16)
    bias[...] = nt(jnp.ones((8, NQ * TPD * PIX), BF16), near)
    for d in range(1, NZ):
        send(bias, bias_in.at[d - 1], small_s.at[1], small_r.at[1], to["z"](d))
    for g, (low, high) in enumerate(GROUPS):
        product = nn(near, windows_near[:, low * 128 : high * 128]).astype(BF16)
        for o in range(low, high):
            grad[o] = product[:, (o - low) * 128 : (o - low + 1) * 128]
        for d in range(1, NZ):
            at = pl.multiple_of(lax.rem(z + d, NZ) * SHARE, SHARE)
            send(
                grad.at[pl.ds(low, high - low), pl.ds(at, SHARE)],
                grad_in.at[d - 1, pl.ds(low, high - low)],
                sum_s.at[g],
                sum_r.at[g],
                to["z"](d),
            )

    for d in range(1, NC):
        send(
            dpad.at[lax.rem(c + d, NC)],
            dpad_in.at[d - 1],
            small_s.at[0],
            small_r.at[0],
            to["c"](d),
        )
    await_bytes(dpad_in, small_r.at[0])
    total = dpad[c].astype(F32)
    for d in range(NC - 1):
        total += dpad_in[d].astype(F32)
    dsum[...] = total
    left, right = BODY, BODY + 32
    margin_own[...] = jnp.zeros(margin_own.shape, F32)
    for t in range(TPD):
        base, at, corner, col = t * 80, t * 32, RIM + t * 4, t * 10
        margin_own[at : at + 8, :] = dsum[base : base + 8, :]
        margin_own[at + 8 : at + 16, :] = dsum[right + col + 1 : right + col + 9, :]
        margin_own[at + 16 : at + 24, :] = dsum[base + 72 : base + 80, :]
        margin_own[at + 24 : at + 32, :] = dsum[left + col + 1 : left + col + 9, :]
        margin_own[corner : corner + 1, :] = dsum[left + col : left + col + 1, :]
        margin_own[corner + 1 : corner + 2, :] = dsum[right + col : right + col + 1, :]
        margin_own[corner + 2 : corner + 3, :] = dsum[right + col + 9 : right + col + 10, :]
        margin_own[corner + 3 : corner + 4, :] = dsum[left + col + 9 : left + col + 10, :]
        inner_out[t * PIX : (t + 1) * PIX, :] = dsum[base + 8 : base + 72, :]
    stores[3].start()
    margin_send[...] = margin_own[...].astype(BF16)
    for d in range(1, NQ):
        send(
            margin_send,
            margin_in.at[d, pl.ds(0, MARGIN)],
            small_s.at[2],
            small_r.at[2],
            to["q"](d),
        )
    margin_in[0, 0:MARGIN, :] = margin_send[...]
    for d in range(NQ):
        row = index[pl.ds(lax.rem(q + NQ - d, NQ) * NZ + z, 1), :]
        chooser = (iota((NZ * RIM, 128), 0) == row - first).astype(F32).astype(BF16)
        slot_chooser[:, d * 128 : (d + 1) * 128] = chooser

    def box(o, full, at_z=None):
        return grad_all.at[
            o,
            slice(None) if "x" in full else x,
            slice(None) if "y" in full else y,
            slice(None) if "z" in full else (z if at_z is None else at_z),
        ]

    def box_rows(full):
        rows = SHARE
        for axis in full:
            rows *= axis_size(axis)
        return rows

    def bytes_of(rows):
        return gauge.at[pl.ds(0, rows)]

    def on_ring(o, stage):
        return stage == 2 and ORDERS[o][2] == "z"

    def ring_send(o, step, side):
        share = lax.rem(z + NZ + (1 - step if side == 0 else step - 1), NZ)
        mine = box(o, "xy", share)
        at = (o, side * (NZ // 2) + step - 1)
        send(mine, mine, ring_s.at[at], ring_r.at[at], to["z"](1 if side == 0 else NZ - 1))

    def ring_wait(o, step, side):
        await_bytes(bytes_of(box_rows("xy")), ring_r.at[o, side * (NZ // 2) + step - 1])

    def gather(o, stage):
        if on_ring(o, stage):
            for side in range(2):
                ring_send(o, 1, side)
            return
        axis, full = ORDERS[o][stage], ORDERS[o][:stage]
        mine = box(o, full)
        for d in range(1, axis_size(axis)):
            send(mine, mine, all_s.at[o, stage], all_r.at[o, stage], to[axis](d))

    def stage_bytes(o, stage):
        axis, full = ORDERS[o][stage], ORDERS[o][:stage]
        return bytes_of(box_rows(full) * (axis_size(axis) - 1))

    def gathered(o, stage):
        await_bytes(stage_bytes(o, stage), all_r.at[o, stage])

    for g, (low, high) in enumerate(GROUPS):
        some = pl.ds(low, high - low)
        await_bytes(grad_in.at[:, some], sum_r.at[g])
        total = grad[some, pl.ds(pl.multiple_of(z * SHARE, SHARE), SHARE), :].astype(F32)
        for d in range(NZ - 1):
            total += grad_in[d, some].astype(F32)
        for o in range(low, high):
            grad_all[o, x, y, z] = total[o - low].astype(BF16)
            gather(o, 0)

    await_bytes(margin_in.at[pl.ds(1, NQ - 1), pl.ds(0, MARGIN)], small_r.at[2])
    sums = nn(slot_chooser[...], margin_in[...].reshape(NQ * 128, 128))
    slot_sum[...] = sums.reshape(NZ, RIM, 128)
    slot_send[...] = slot_sum[...].astype(BF16)
    for d in range(1, NZ):
        send(
            slot_send.at[lax.rem(z + d, NZ)],
            slot_in.at[d - 1],
            small_s.at[3],
            small_r.at[3],
            to["z"](d),
        )
    await_bytes(bias_in, small_r.at[1])
    total = bias[...]
    for d in range(NZ - 1):
        total += bias_in[d]
    bias_out[y] = total
    send(bias_out.at[y], bias_out.at[y], small_s.at[4], small_r.at[4], to["y"](1))

    def put(o):
        return pltpu.make_async_copy(grad_all.at[o], grad_hbm.at[o], out_sems.at[o])

    for stage in (0, 1):
        for o in range(9):
            gathered(o, stage)
            gather(o, stage + 1)
    await_bytes(slot_in, small_r.at[3])
    total = slot_sum[z]
    for d in range(NZ - 1):
        total += slot_in[d].astype(F32)
    side_out[...] = total
    stores[4].start()
    for step in range(1, NZ // 2 + 1):
        for o in range(9):
            if on_ring(o, 2):
                for side in range(2):
                    if step <= ring_steps(o)[side]:
                        ring_wait(o, step, side)
                    if step < ring_steps(o)[side]:
                        ring_send(o, step + 1, side)
                if step == NZ // 2:
                    put(o).start()
            elif step == 3:
                gathered(o, 2)
                put(o).start()
    await_bytes(bias, small_r.at[4])
    stores[5].start()
    for store in stores:
        store.wait()
    for o in range(9):
        put(o).wait()

    await_bytes(dpad_in, small_s.at[0])
    await_bytes(bias_in, small_s.at[1])
    await_bytes(margin_in.at[pl.ds(1, NQ - 1), pl.ds(0, MARGIN)], small_s.at[2])
    await_bytes(slot_in, small_s.at[3])
    await_bytes(bias, small_s.at[4])
    await_bytes(table.at[pl.ds(0, NZ - 1)], small_s.at[5])
    await_bytes(field_all.at[pl.ds(0, NC - 1)], small_s.at[6])
    await_bytes(arrived, small_s.at[7])
    await_bytes(margin_all.at[pl.ds(0, NC - 1)], small_s.at[8])
    for near, sem in ((field_near, 9), (margin_near, 10), (turned_near, 11)):
        await_bytes(near.at[pl.ds(0, NQ - 1)], small_s.at[sem])
    for g, (low, high) in enumerate(GROUPS):
        await_bytes(grad_in.at[:, pl.ds(low, high - low)], sum_s.at[g])
    for o in range(9):
        for stage in range(3):
            if not on_ring(o, stage):
                await_bytes(stage_bytes(o, stage), all_s.at[o, stage])
                continue
            for side in range(2):
                for step in range(ring_steps(o)[side]):
                    await_bytes(
                        bytes_of(box_rows("xy")), ring_s.at[o, side * (NZ // 2) + step]
                    )


def whole(inp, hid, cell_prev, kern, gate_bias, hidden_up, cell_up, lists):
    hbm = pl.BlockSpec(memory_space=pl.ANY)
    state = cell_prev.shape
    devices = NQ * NZ
    operands = (inp, hid, *lists, cell_prev, gate_bias, hidden_up, cell_up, kern)
    results = (
        jax.ShapeDtypeStruct(state, BF16),
        jax.ShapeDtypeStruct(state, F32),
        jax.ShapeDtypeStruct(state, F32),
        jax.ShapeDtypeStruct((9, NX, NY, NZ, SHARE, 128), BF16),
        jax.ShapeDtypeStruct((NY, 8, 128), F32),
        jax.ShapeDtypeStruct((TPD * PIX, 128), F32),
        jax.ShapeDtypeStruct((RIM, 128), F32),
    )
    scratch = [pltpu.VMEM(a.shape, a.dtype) for a in operands[:-1]]
    scratch += [pltpu.VMEM(a.shape, a.dtype) for a in results[:3] + results[4:]]
    scratch += [
        pltpu.VMEM(kern.shape, BF16),
        pltpu.VMEM((TPD * PIX, 128), F32),
        pltpu.VMEM((TPD * PIX, 128), BF16),
        pltpu.VMEM((RIM, 128), BF16),
        pltpu.VMEM((devices * TPD, 128), I32),
        pltpu.VMEM((devices, 128), I32),
        pltpu.VMEM((NZ, RIM, 128), BF16),
        pltpu.VMEM((NQ, MARGIN, 128), BF16),
        pltpu.VMEM((NQ - 1, MARGIN, 128), BF16),
        pltpu.VMEM((NC, TPD * PIX, 128), BF16),
        pltpu.VMEM((NC, MARGIN, 128), BF16),
        pltpu.VMEM((4, TPD * PIX, 128), BF16),
        pltpu.VMEM((4, MARGIN, 128), BF16),
        pltpu.VMEM((3, 4, BODY, 128), F32),
        pltpu.VMEM((3, 4, 8 + BODY + 32, 128), F32),
        pltpu.VMEM((NQ, TPD * PIX, 128), BF16),
        pltpu.VMEM((NQ, MARGIN, 128), BF16),
        pltpu.VMEM((3, BODY, 128), F32),
        pltpu.VMEM((NQ * TPD * PIX, 9 * 128), BF16),
        pltpu.VMEM((NY, TPD * PIX, 128), BF16),
        pltpu.VMEM((NQ, TPD * PIX, 128), BF16),
        pltpu.VMEM((9, 128, 128), BF16),
        pltpu.VMEM((NZ - 1, 9, SHARE, 128), BF16),
        pltpu.VMEM((9, NX, NY, NZ, SHARE, 128), BF16),
        pltpu.VMEM((1024, 128), BF16),
        pltpu.VMEM((8, 128), F32),
        pltpu.VMEM((NC, DROWS, 128), BF16),
        pltpu.VMEM((NC - 1, DROWS, 128), BF16),
        pltpu.VMEM((DROWS, 128), F32),
        pltpu.VMEM((MARGIN, 128), F32),
        pltpu.VMEM((MARGIN, 128), BF16),
        pltpu.VMEM((NQ, 128, 128), BF16),
        pltpu.VMEM((NZ, RIM, 128), F32),
        pltpu.VMEM((NZ, RIM, 128), BF16),
        pltpu.VMEM((NZ - 1, RIM, 128), BF16),
        pltpu.VMEM((NZ * RIM, NQ * 128), BF16),
        pltpu.VMEM((NZ - 1, 8, 128), F32),
    ]
    for shape in ((12,), (len(GROUPS),), (9, 3), (9, NZ)):
        scratch += [pltpu.SemaphoreType.DMA(shape)] * 2
    for count in (9, len(operands), len(results) - 1):
        scratch.append(pltpu.SemaphoreType.DMA((count,)))
    return pl.pallas_call(
        whole_kernel,
        out_shape=results,
        in_specs=[hbm] * len(operands),
        out_specs=(hbm,) * len(results),
        scratch_shapes=scratch,
        compiler_params=pltpu.CompilerParams(
            collective_id=0, has_side_effects=True, vmem_limit_bytes=VMEM_LIMIT
        ),
        name="whole",
    )(*operands)


def finish_kernel(
    hidden_hbm,
    cell_hbm,
    cell_grad_hbm,
    grad,
    bias_hbm,
    inner_hbm,
    sides_hbm,
    hidden_out,
    cell_out,
    cell_grad_out,
    grad_out,
    bias_out_hbm,
    input_out_hbm,
    prior_out_hbm,
    held,
    wide,
    bias,
    cells,
    sides,
    hidden,
    cell,
    cell_grad,
    bias_out,
    input_out,
    prior_out,
    sems_in,
    sems_out,
    sems,
):
    def fetch(o):
        return pltpu.make_async_copy(grad.at[o], held.at[o], sems_in.at[o])

    def put(o):
        return pltpu.make_async_copy(wide.at[o], grad_out.at[o], sems_out.at[o])

    small = [
        pltpu.make_async_copy(source, target, sems.at[i])
        for i, (source, target) in enumerate(
            (
                (bias_hbm, bias),
                (inner_hbm, cells),
                (sides_hbm, sides),
                (hidden_hbm, hidden),
                (cell_hbm, cell),
                (cell_grad_hbm, cell_grad),
                (hidden, hidden_out),
                (cell, cell_out),
                (cell_grad, cell_grad_out),
                (bias_out, bias_out_hbm),
                (input_out, input_out_hbm),
                (prior_out, prior_out_hbm),
            )
        )
    ]
    fetch(0).start()
    for copy in small[:6]:
        copy.start()
    for o in range(1, 9):
        fetch(o).start()
    for o in range(9):
        fetch(o).wait()
        for k in range(4):
            wide[o, :, k * 128 : (k + 1) * 128] = held[o, k].astype(F32)
        put(o).start()
    for copy in small[:6]:
        copy.wait()
    for copy in small[6:9]:
        copy.start()
    for k in range(4):
        bias_out[k : k + 1, :] = bias[k // 2, 0:1, (k % 2) * 64 : (k % 2 + 1) * 64]
    for t in range(TPD):
        base, at = t * PIX, t * 32
        cells[base : base + 8, :] += sides[at : at + 8, :]
        cells[pl.ds(base + 7, 8, stride=8), :] += sides[at + 8 : at + 16, :]
        cells[base + 56 : base + 64, :] += sides[at + 16 : at + 24, :]
        cells[pl.ds(base, 8, stride=8), :] += sides[at + 24 : at + 32, :]
    ident = eye(128)
    for t in range(TPD):
        rounded = cells[t * PIX : (t + 1) * PIX, :].astype(BF16)
        turned = nt(ident, rounded).astype(BF16)
        input_out[t] = turned[0:64]
        prior_out[t] = turned[64:128]
    for copy in small[9:]:
        copy.start()
    for copy in small[6:]:
        copy.wait()
    for o in range(9):
        put(o).wait()


def finish(hidden, cell, cell_grad, grad, bias, inner, sides):
    hbm = pl.BlockSpec(memory_space=pl.ANY)
    state = hidden.shape
    return pl.pallas_call(
        finish_kernel,
        out_shape=(
            jax.ShapeDtypeStruct(state, BF16),
            jax.ShapeDtypeStruct(state, F32),
            jax.ShapeDtypeStruct(state, F32),
            jax.ShapeDtypeStruct((9, 256, 512), F32),
            jax.ShapeDtypeStruct((4, 64), F32),
            jax.ShapeDtypeStruct(state, BF16),
            jax.ShapeDtypeStruct(state, BF16),
        ),
        in_specs=[hbm] * 7,
        out_specs=(hbm,) * 7,
        scratch_shapes=[
            pltpu.VMEM(grad.shape, BF16),
            pltpu.VMEM((9, 256, 512), F32),
            pltpu.VMEM(bias.shape, F32),
            pltpu.VMEM(inner.shape, F32),
            pltpu.VMEM(sides.shape, F32),
            pltpu.VMEM(state, BF16),
            pltpu.VMEM(state, F32),
            pltpu.VMEM(state, F32),
            pltpu.VMEM((4, 64), F32),
            pltpu.VMEM(state, BF16),
            pltpu.VMEM(state, BF16),
            pltpu.SemaphoreType.DMA((9,)),
            pltpu.SemaphoreType.DMA((9,)),
            pltpu.SemaphoreType.DMA((12,)),
        ],
        compiler_params=pltpu.CompilerParams(vmem_limit_bytes=VMEM_LIMIT),
        name="finish",
    )(hidden, cell, cell_grad, grad, bias, inner, sides)


def local(
    inputs,
    prior_hidden_state,
    cell_prev,
    kernel,
    gate_bias,
    hidden_upstream,
    cell_upstream,
    edge_source,
    edge_code,
    corner_source,
    corner_code,
):
    hidden_new, cell_new, cell_grad, grad, bias, inner, sides = whole(
        inputs,
        prior_hidden_state,
        cell_prev,
        kernel.reshape(9, 256, 512),
        gate_bias,
        hidden_upstream,
        cell_upstream,
        [a.T for a in (edge_source, edge_code, corner_source, corner_code)],
    )
    hidden_new, cell_new, cell_grad, kernel_grad, bias_grad, input_grad, hidden_grad = finish(
        hidden_new, cell_new, cell_grad, grad.reshape(9, NX, NY * NZ * SHARE, 128), bias, inner, sides
    )
    return (
        hidden_new,
        cell_new,
        kernel_grad.reshape(9, 4, 64, 512),
        bias_grad,
        input_grad,
        hidden_grad,
        cell_grad,
    )


def solution(mesh):
    tiles, whole = P("tile", "chan", None), P()
    gates = P(None, None, "chan", None)
    bias = P(None, "chan")
    in_specs = (tiles, tiles, tiles, gates, bias, tiles, tiles, whole, whole, whole, whole)
    out_specs = (tiles, tiles, gates, bias, tiles, tiles, tiles)
    return jax.shard_map(local, mesh=mesh, in_specs=in_specs, out_specs=out_specs, check_vma=False)
```

```python
import functools

import jax
import jax.numpy as jnp
from jax import lax
from jax.experimental import pallas as pl
from jax.experimental.pallas import tpu as pltpu
from jax.sharding import PartitionSpec as P

F32, BF16, I32 = jnp.float32, jnp.bfloat16, jnp.int32
MESH = pl.DeviceIdType.MESH
NY, NX, NZ = 2, 4, 8
NQ = NY * NX
NC = 4
TPD = 3
PIX = 64
RIM = 32 * TPD
MARGIN = 112
BODY = 80 * TPD
DROWS = BODY + 64
SHARE = 16
GROUPS = ((0, 3), (3, 6), (6, 9))
JOBS = ((0, 3, "yxz"), (3, 6, "zxy"), (6, 9, "zyx"))
SCHEDULE = (
    ("sum", 0),
    ("sum", 1),
    ("sum", 2),
    ("slots",),
    ("go", 0, 0),
    ("go", 1, 0),
    ("go", 2, 0),
    ("go", 0, 1),
    ("go", 1, 1),
    ("go", 2, 1),
    ("ring", 1),
    ("ring", 2),
    ("ring", 3),
    ("ring", 4),
)
VMEM_LIMIT = 56 * 1024 * 1024


def nn(a, b):
    return lax.dot_general(a, b, (((1,), (0,)), ((), ())), preferred_element_type=F32)


def tn(a, b):
    return lax.dot_general(a, b, (((0,), (0,)), ((), ())), preferred_element_type=F32)


def nt(a, b):
    return lax.dot_general(a, b, (((1,), (1,)), ((), ())), preferred_element_type=F32)


def iota(shape, dim):
    return lax.broadcasted_iota(I32, shape, dim)


def eye(n):
    return (iota((n, n), 0) == iota((n, n), 1)).astype(BF16)


def position():
    t = lax.axis_index("tile")
    z, q = lax.rem(t, NZ), lax.div(t, NZ)
    return q, lax.div(q, NX), lax.rem(q, NX), z, lax.axis_index("chan")


def peers():
    q, y, x, z, c = position()
    return {
        "z": lambda d: (q * NZ + lax.rem(z + d, NZ), c),
        "q": lambda d: (lax.rem(q + d, NQ) * NZ + z, c),
        "x": lambda d: ((y * NX + lax.rem(x + d, NX)) * NZ + z, c),
        "y": lambda d: ((lax.rem(y + d, NY) * NX + x) * NZ + z, c),
        "c": lambda d: (q * NZ + z, lax.rem(c + d, NC)),
    }


def greet(to):
    barrier = pltpu.get_barrier_semaphore()
    count = 0
    for axis, size in (("z", NZ), ("q", NQ), ("c", NC)):
        for d in range(1, size):
            pl.semaphore_signal(barrier, inc=1, device_id=to[axis](d), device_id_type=MESH)
            count += 1
    return count


def send(src, dst, send_sem, recv_sem, device):
    pltpu.make_async_remote_copy(
        src_ref=src,
        dst_ref=dst,
        send_sem=send_sem,
        recv_sem=recv_sem,
        device_id=device,
        device_id_type=MESH,
    ).start()


def await_bytes(like, sem):
    pltpu.make_async_copy(like, like, sem).wait()


def axis_size(axis):
    return {"x": NX, "y": NY, "z": NZ}[axis]


def jobs_of(group):
    low, high = GROUPS[group]
    return [j for j, job in enumerate(JOBS) if low <= job[0] < high]


def ring_steps(j):
    return (NZ // 2, NZ // 2 - 1) if j % 2 == 0 else (NZ // 2 - 1, NZ // 2)


def own_cells(inp, hid, cells, field, rim):
    ident = eye(PIX)
    for t in range(TPD):
        both = jnp.concatenate([inp[t], hid[t]], axis=0)
        cells[t * PIX : (t + 1) * PIX, :] = nt(ident, both)
    field[...] = cells[...].astype(BF16)
    for t in range(TPD):
        base = t * PIX
        sides = jnp.concatenate(
            [
                cells[base : base + 8, :],
                cells[pl.ds(base + 7, 8, stride=8), :],
                cells[base + 56 : base + 64, :],
                cells[pl.ds(base, 8, stride=8), :],
            ],
            axis=0,
        )
        rim[t * 32 : (t + 1) * 32, :] = sides.astype(BF16)


def source_cells(esrc, ecode, csrc, ccode, by_tile, index):
    lane, row = iota((4, 128), 1), iota((4, 128), 0)
    edge_lane = ((lane < 32) & (lax.div(lane, 8) == row)).astype(F32).astype(BF16)
    corner_lane = (lane - 32 == row).astype(F32).astype(BF16)

    def spread(edges, corners):
        wide = tn(edges[...].astype(F32).astype(BF16), edge_lane)
        wide += tn(corners[...].astype(F32).astype(BF16), corner_lane)
        return wide.astype(I32)

    source, code = spread(esrc, csrc), spread(ecode, ccode)
    lane = iota(source.shape, 1)
    cell = lane & 7
    along_side = (code >> 1) * 8 + jnp.where((code & 1) == 1, 7 - cell, cell)
    at_corner = jnp.where(
        code == 0, 0, jnp.where(code == 1, 7, jnp.where(code == 2, 23, 16))
    )
    by_tile[...] = source * 32 + jnp.where(lane < 32, along_side, at_corner)
    devices = index.shape[0]
    rows = [by_tile[pl.ds(i, devices, stride=TPD), :] for i in range(TPD)]
    index[...] = jnp.concatenate(
        [r[:, :32] for r in rows]
        + [r[:, 32:36] for r in rows]
        + [jnp.full((devices, 128 - 36 * TPD), -1000000, I32)],
        axis=1,
    )


def whole_kernel(
    inp_hbm,
    hid_hbm,
    esrc_hbm,
    ecode_hbm,
    csrc_hbm,
    ccode_hbm,
    cell_prev_hbm,
    bias_hbm,
    hidden_up_hbm,
    cell_up_hbm,
    kern_hbm,
    hidden_hbm,
    cell_hbm,
    cell_grad_hbm,
    grad_hbm,
    bias_sum_hbm,
    inner_hbm,
    side_hbm,
    inp,
    hid,
    esrc,
    ecode,
    csrc,
    ccode,
    cell_prev,
    gate_bias,
    hidden_up,
    cell_up,
    hidden_out,
    cell_out,
    cell_grad_out,
    bias_out,
    inner_out,
    side_out,
    kern,
    cells,
    field,
    rim,
    by_tile,
    index,
    table,
    picked,
    arrived,
    field_all,
    margin_all,
    field_blocks,
    margin_blocks,
    wide,
    accs,
    field_near,
    margin_near,
    wide_near,
    windows_near,
    turned_own,
    turned_near,
    grad,
    grad_in,
    grad_all,
    gauge,
    bias,
    dpad,
    dpad_in,
    dsum,
    margin_own,
    margin_send,
    margin_in,
    slot_sum,
    slot_send,
    slot_in,
    slot_chooser,
    bias_in,
    small_s,
    small_r,
    sum_s,
    sum_r,
    all_s,
    all_r,
    ring_s,
    ring_r,
    out_sems,
    load_sems,
    store_sems,
):
    q, y, x, z, c = position()
    to = peers()

    def quarter(d):
        return lax.rem(lax.rem(q + d, NQ), NX)

    greeted = greet(to)
    loads = [
        pltpu.make_async_copy(far, near, load_sems.at[i])
        for i, (far, near) in enumerate(
            (
                (inp_hbm, inp),
                (hid_hbm, hid),
                (esrc_hbm, esrc),
                (ecode_hbm, ecode),
                (csrc_hbm, csrc),
                (ccode_hbm, ccode),
                (cell_prev_hbm, cell_prev),
                (bias_hbm, gate_bias),
                (hidden_up_hbm, hidden_up),
                (cell_up_hbm, cell_up),
                (kern_hbm, kern),
            )
        )
    ]
    for load in loads:
        load.start()
    stores = [
        pltpu.make_async_copy(near, far, store_sems.at[i])
        for i, (near, far) in enumerate(
            (
                (hidden_out, hidden_hbm),
                (cell_out, cell_hbm),
                (cell_grad_out, cell_grad_hbm),
                (inner_out, inner_hbm),
                (side_out, side_hbm),
                (bias_out, bias_sum_hbm),
            )
        )
    ]
    for load in loads[:2]:
        load.wait()
    own_cells(inp, hid, cells, field, rim)
    margin_in[:, MARGIN:128, :] = jnp.zeros((NQ, 128 - MARGIN, 128), BF16)
    pl.semaphore_wait(pltpu.get_barrier_semaphore(), greeted)

    for d in range(1, NZ):
        send(rim, table.at[z], small_s.at[5], small_r.at[5], to["z"](d))
    for d in range(1, NC):
        send(field, field_all.at[c], small_s.at[6], small_r.at[6], to["c"](d))
    table[z] = rim[...]
    field_all[c] = field[...]
    for load in loads[2:6]:
        load.wait()
    source_cells(esrc, ecode, csrc, ccode, by_tile, index)

    first = q * (NZ * RIM)
    choosers = []
    for d in range(NQ):
        row = index[pl.ds(lax.rem(q + d, NQ) * NZ + z, 1), :]
        down = jnp.broadcast_to((row - first).astype(F32), (128, 128)).T
        choosers.append(
            jnp.concatenate(
                [
                    (down == (iota((128, 128), 1) + 128 * k).astype(F32)).astype(BF16)
                    for k in range(NZ * RIM // 128)
                ],
                axis=1,
            )
        )
    def lanes(ref, k):
        pair, half = 2 * (k % 2), 64 * (k // 2)
        return jnp.concatenate(
            [ref[pair][:, half : half + 64], ref[pair + 1][:, half : half + 64]], axis=1
        )

    await_bytes(field_all.at[pl.ds(0, NC - 1)], small_r.at[6])
    for k in range(4):
        field_blocks[k] = lanes(field_all, k)
    for d in range(1, NQ):
        send(
            field_blocks.at[quarter(d)],
            field_near.at[d],
            small_s.at[9],
            small_r.at[9],
            to["q"](d),
        )
    field_near[0] = field_blocks[x]
    for k in range(4):
        body = field_blocks[k].astype(F32)
        for t in range(TPD):
            base = t * 80
            wide[1, k, base + 8 : base + 72, :] = body[t * PIX : (t + 1) * PIX]
            wide[0, k, base + 9 : base + 72, :] = wide[1, k, base + 8 : base + 71, :]
            wide[2, k, base + 8 : base + 71, :] = wide[1, k, base + 9 : base + 72, :]

    await_bytes(table.at[pl.ds(0, NZ - 1)], small_r.at[5])
    rims = table[...].reshape(NZ * RIM, 128)
    for d in list(range(1, NQ)) + [0]:
        picked[d] = nn(choosers[d], rims)[:MARGIN].astype(BF16)
        if d:
            send(picked.at[d], arrived.at[d - 1], small_s.at[7], small_r.at[7], to["q"](d))

    await_bytes(arrived, small_r.at[7])
    total = picked[0].astype(F32)
    for d in range(1, NQ):
        total += arrived[d - 1].astype(F32)
    margin_all[c] = total.astype(BF16)
    for d in range(1, NC):
        send(margin_all.at[c], margin_all.at[c], small_s.at[8], small_r.at[8], to["c"](d))
    for load in loads[6:]:
        load.wait()
    await_bytes(margin_all.at[pl.ds(0, NC - 1)], small_r.at[8])
    for k in range(4):
        margin_blocks[k] = lanes(margin_all, k)
    for d in range(1, NQ):
        send(
            margin_blocks.at[quarter(d)],
            margin_near.at[d],
            small_s.at[10],
            small_r.at[10],
            to["q"](d),
        )
    margin_near[0] = margin_blocks[x]

    for k in range(4):
        margin = margin_blocks[k].astype(F32)
        left, right = wide.at[0, k], wide.at[2, k]
        for t in range(TPD):
            base, at, corner = t * 80, t * 32, RIM + t * 4
            for row, side in ((base, at), (base + 72, at + 16)):
                wide[1, k, row : row + 8, :] = margin[side : side + 8]
                left[row + 1 : row + 8, :] = margin[side : side + 7]
                right[row : row + 7, :] = margin[side + 1 : side + 8]
            left[base : base + 1, :] = margin[corner : corner + 1]
            left[pl.ds(base + 8, 8, stride=8), :] = margin[at + 24 : at + 32]
            left[base + 72 : base + 73, :] = margin[corner + 3 : corner + 4]
            right[base + 7 : base + 8, :] = margin[corner + 1 : corner + 2]
            right[pl.ds(base + 15, 8, stride=8), :] = margin[at + 8 : at + 16]
            right[base + 79 : base + 80, :] = margin[corner + 2 : corner + 3]

    def window(o):
        start = (o // 3) * 8
        return jnp.concatenate(
            [
                jnp.concatenate(
                    [
                        wide[o % 3, k, t * 80 + start : t * 80 + start + PIX, :]
                        for t in range(TPD)
                    ],
                    axis=0,
                ).astype(BF16)
                for k in range(4)
            ],
            axis=1,
        )

    def gate(k):
        column = jnp.broadcast_to(gate_bias[k : k + 1, :], (64, 64)).T
        return jnp.concatenate([column] * TPD, axis=1)

    gates = jnp.concatenate([gate(k) for k in range(4)], axis=0)
    for o in range(9):
        gates = gates + nt(kern[o], window(o))
    in_gate = jax.nn.sigmoid(gates[0:64])
    forget = jax.nn.sigmoid(gates[64:128])
    cand = jnp.tanh(gates[128:192])
    out_gate = jax.nn.sigmoid(gates[192:256])
    before = jnp.concatenate([cell_prev[t] for t in range(TPD)], axis=1)
    above = jnp.concatenate([cell_up[t] for t in range(TPD)], axis=1)
    upstream = jnp.concatenate([hidden_up[t].astype(F32) for t in range(TPD)], axis=1)
    cell_new = forget * before + in_gate * cand
    squashed = jnp.tanh(cell_new)
    hidden_new = (out_gate * squashed).astype(BF16)
    dcell = above + upstream * out_gate * (1.0 - squashed * squashed)
    cell_grad = dcell * forget
    dgates = jnp.concatenate(
        [
            dcell * cand * in_gate * (1.0 - in_gate),
            dcell * before * forget * (1.0 - forget),
            dcell * in_gate * (1.0 - cand * cand),
            upstream * squashed * out_gate * (1.0 - out_gate),
        ],
        axis=0,
    ).astype(BF16)

    turned = nt(eye(TPD * PIX), dgates).astype(BF16)
    for h in range(NY):
        turned_own[h] = turned[:, h * 128 : (h + 1) * 128]
    for d in range(1, NQ):
        send(
            turned_own.at[lax.div(lax.rem(q + d, NQ), NX)],
            turned_near.at[d],
            small_s.at[11],
            small_r.at[11],
            to["q"](d),
        )
    turned_near[0] = turned_own[y]

    accs[...] = jnp.zeros(accs.shape, F32)
    for o in range(9):
        a, b = o // 3, o % 3
        product = nn(turned, kern[o])
        for k in range(4):
            for t in range(TPD):
                base = 8 + t * 80 + a * 8
                accs[b, k, base : base + PIX, :] += product[
                    t * PIX : (t + 1) * PIX, k * 128 : (k + 1) * 128
                ]
    column = iota((BODY, 128), 0) & 7
    blocks = []
    for k in range(4):
        body = accs[1, k, 8 : 8 + BODY, :]
        body += jnp.where(column < 7, accs[0, k, 9 : 9 + BODY, :], 0.0)
        body += jnp.where(column > 0, accs[2, k, 7 : 7 + BODY, :], 0.0)
        left, right = accs.at[0, k], accs.at[2, k]
        blocks.append(
            (
                body,
                left[pl.ds(8, 32, stride=8), :],
                right[pl.ds(15, 32, stride=8), :],
            )
        )
    for e in range(NC):
        half = slice((e % 2) * 64, (e % 2) * 64 + 64)
        start = 0
        for one, two in zip(blocks[e // 2], blocks[2 + e // 2]):
            rows = one.shape[0]
            dpad[e, start : start + rows, :] = jnp.concatenate(
                [one[:, half], two[:, half]], axis=1
            ).astype(BF16)
            start += rows
    for t in range(TPD):
        at = slice(t * PIX, (t + 1) * PIX)
        hidden_out[t] = hidden_new[:, at]
        cell_out[t] = cell_new[:, at]
        cell_grad_out[t] = cell_grad[:, at]
    for store in stores[:3]:
        store.start()

    await_bytes(field_near.at[pl.ds(0, NQ - 1)], small_r.at[9])
    await_bytes(margin_near.at[pl.ds(0, NQ - 1)], small_r.at[10])

    def windows_of(s, carry):
        body, margin = field_near[s].astype(F32), margin_near[s].astype(F32)
        left, right = wide_near.at[0], wide_near.at[2]
        for t in range(TPD):
            base, at = t * 80, t * 32
            wide_near[1, base : base + 8, :] = margin[at : at + 8]
            wide_near[1, base + 8 : base + 72, :] = body[t * PIX : (t + 1) * PIX]
            wide_near[1, base + 72 : base + 80, :] = margin[at + 16 : at + 24]
        wide_near[0, 1:BODY, :] = wide_near[1, 0 : BODY - 1, :]
        wide_near[2, 0 : BODY - 1, :] = wide_near[1, 1:BODY, :]
        for t in range(TPD):
            base, at, corner = t * 80, t * 32, RIM + t * 4
            left[base : base + 1, :] = margin[corner : corner + 1]
            left[pl.ds(base + 8, 8, stride=8), :] = margin[at + 24 : at + 32]
            left[base + 72 : base + 73, :] = margin[corner + 3 : corner + 4]
            right[base + 7 : base + 8, :] = margin[corner + 1 : corner + 2]
            right[pl.ds(base + 15, 8, stride=8), :] = margin[at + 8 : at + 16]
            right[base + 79 : base + 80, :] = margin[corner + 2 : corner + 3]
        for o in range(9):
            for t in range(TPD):
                base = t * 80 + (o // 3) * 8
                row = pl.multiple_of(s * (TPD * PIX) + t * PIX, PIX)
                windows_near[pl.ds(row, PIX), o * 128 : (o + 1) * 128] = wide_near[
                    o % 3, base : base + PIX, :
                ].astype(BF16)
        return carry

    lax.fori_loop(0, NQ, windows_of, 0)
    await_bytes(turned_near.at[pl.ds(0, NQ - 1)], small_r.at[11])
    for d in range(1, NC):
        send(
            dpad.at[lax.rem(c + d, NC)],
            dpad_in.at[d - 1],
            small_s.at[0],
            small_r.at[0],
            to["c"](d),
        )
    near = nt(eye(128), turned_near[...].reshape(NQ * TPD * PIX, 128)).astype(BF16)
    bias[...] = nt(jnp.ones((8, NQ * TPD * PIX), BF16), near)
    for d in range(1, NZ):
        send(bias, bias_in.at[d - 1], small_s.at[1], small_r.at[1], to["z"](d))
    for g, (low, high) in enumerate(GROUPS):
        product = nn(near, windows_near[:, low * 128 : high * 128]).astype(BF16)
        for o in range(low, high):
            grad[o] = product[:, (o - low) * 128 : (o - low + 1) * 128]
        for d in range(1, NZ):
            at = pl.multiple_of(lax.rem(z + d, NZ) * SHARE, SHARE)
            send(
                grad.at[pl.ds(low, high - low), pl.ds(at, SHARE)],
                grad_in.at[d - 1, pl.ds(low, high - low)],
                sum_s.at[g],
                sum_r.at[g],
                to["z"](d),
            )

    await_bytes(dpad_in, small_r.at[0])
    total = dpad[c].astype(F32)
    for d in range(NC - 1):
        total += dpad_in[d].astype(F32)
    dsum[...] = total
    left, right = BODY, BODY + 32
    margin_own[...] = jnp.zeros(margin_own.shape, F32)
    for t in range(TPD):
        base, at, corner, col = t * 80, t * 32, RIM + t * 4, t * 10
        margin_own[at : at + 8, :] = dsum[base : base + 8, :]
        margin_own[at + 8 : at + 16, :] = dsum[right + col + 1 : right + col + 9, :]
        margin_own[at + 16 : at + 24, :] = dsum[base + 72 : base + 80, :]
        margin_own[at + 24 : at + 32, :] = dsum[left + col + 1 : left + col + 9, :]
        margin_own[corner : corner + 1, :] = dsum[left + col : left + col + 1, :]
        margin_own[corner + 1 : corner + 2, :] = dsum[right + col : right + col + 1, :]
        margin_own[corner + 2 : corner + 3, :] = dsum[right + col + 9 : right + col + 10, :]
        margin_own[corner + 3 : corner + 4, :] = dsum[left + col + 9 : left + col + 10, :]
        inner_out[t * PIX : (t + 1) * PIX, :] = dsum[base + 8 : base + 72, :]
    stores[3].start()
    margin_send[...] = margin_own[...].astype(BF16)
    for d in range(1, NQ):
        send(
            margin_send,
            margin_in.at[d, pl.ds(0, MARGIN)],
            small_s.at[2],
            small_r.at[2],
            to["q"](d),
        )
    margin_in[0, 0:MARGIN, :] = margin_send[...]
    for d in range(NQ):
        row = index[pl.ds(lax.rem(q + NQ - d, NQ) * NZ + z, 1), :]
        chooser = (iota((NZ * RIM, 128), 0) == row - first).astype(F32).astype(BF16)
        slot_chooser[:, d * 128 : (d + 1) * 128] = chooser

    def box(j, full, at_z=None):
        return grad_all.at[
            pl.ds(JOBS[j][0], JOBS[j][1] - JOBS[j][0]),
            slice(None) if "x" in full else x,
            slice(None) if "y" in full else y,
            slice(None) if "z" in full else (z if at_z is None else at_z),
        ]

    def box_rows(j, full):
        rows = SHARE * (JOBS[j][1] - JOBS[j][0])
        for axis in full:
            rows *= axis_size(axis)
        return rows

    def bytes_of(rows):
        return gauge.at[pl.ds(0, rows)]

    def on_ring(j, stage):
        return stage == 2 and JOBS[j][2][2] == "z"

    def ring_send(j, step, side):
        share = lax.rem(z + NZ + (1 - step if side == 0 else step - 1), NZ)
        mine = box(j, "xy", share)
        at = (j, side * (NZ // 2) + step - 1)
        send(mine, mine, ring_s.at[at], ring_r.at[at], to["z"](1 if side == 0 else NZ - 1))

    def ring_wait(j, step, side):
        await_bytes(bytes_of(box_rows(j, "xy")), ring_r.at[j, side * (NZ // 2) + step - 1])

    def gather(j, stage):
        if on_ring(j, stage):
            for side in range(2):
                ring_send(j, 1, side)
            return
        axis, full = JOBS[j][2][stage], JOBS[j][2][:stage]
        mine = box(j, full)
        for d in range(1, axis_size(axis)):
            send(mine, mine, all_s.at[j, stage], all_r.at[j, stage], to[axis](d))

    def stage_bytes(j, stage):
        axis, full = JOBS[j][2][stage], JOBS[j][2][:stage]
        return bytes_of(box_rows(j, full) * (axis_size(axis) - 1))

    def gathered(j, stage):
        await_bytes(stage_bytes(j, stage), all_r.at[j, stage])

    def sum_over_z(g):
        low, high = GROUPS[g]
        some = pl.ds(low, high - low)
        await_bytes(grad_in.at[:, some], sum_r.at[g])
        total = grad[some, pl.ds(pl.multiple_of(z * SHARE, SHARE), SHARE), :].astype(F32)
        for d in range(NZ - 1):
            total += grad_in[d, some].astype(F32)
        for o in range(low, high):
            grad_all[o, x, y, z] = total[o - low].astype(BF16)
        for j in jobs_of(g):
            gather(j, 0)

    def advance(g, stage):
        for j in jobs_of(g):
            gathered(j, stage)
            gather(j, stage + 1)

    def slots():
        await_bytes(margin_in.at[pl.ds(1, NQ - 1), pl.ds(0, MARGIN)], small_r.at[2])
        sums = nn(slot_chooser[...], margin_in[...].reshape(NQ * 128, 128))
        slot_sum[...] = sums.reshape(NZ, RIM, 128)
        slot_send[...] = slot_sum[...].astype(BF16)
        for d in range(1, NZ):
            send(
                slot_send.at[lax.rem(z + d, NZ)],
                slot_in.at[d - 1],
                small_s.at[3],
                small_r.at[3],
                to["z"](d),
            )
        await_bytes(bias_in, small_r.at[1])
        total = bias[...]
        for d in range(NZ - 1):
            total += bias_in[d]
        bias_out[y] = total
        send(bias_out.at[y], bias_out.at[y], small_s.at[4], small_r.at[4], to["y"](1))

    def put(j):
        some = pl.ds(JOBS[j][0], JOBS[j][1] - JOBS[j][0])
        return pltpu.make_async_copy(grad_all.at[some], grad_hbm.at[some], out_sems.at[j])

    def ring(step):
        for j in range(len(JOBS)):
            if on_ring(j, 2):
                for side in range(2):
                    if step <= ring_steps(j)[side]:
                        ring_wait(j, step, side)
                    if step < ring_steps(j)[side]:
                        ring_send(j, step + 1, side)
                if step == NZ // 2:
                    put(j).start()

    moves = {"sum": sum_over_z, "go": advance, "ring": ring, "slots": slots}
    for name, *at in SCHEDULE:
        moves[name](*at)
    for j in range(len(JOBS)):
        if not on_ring(j, 2):
            gathered(j, 2)
            put(j).start()
    await_bytes(slot_in, small_r.at[3])
    total = slot_sum[z]
    for d in range(NZ - 1):
        total += slot_in[d].astype(F32)
    side_out[...] = total
    stores[4].start()
    await_bytes(bias, small_r.at[4])
    stores[5].start()
    for store in stores:
        store.wait()
    for j in range(len(JOBS)):
        put(j).wait()

    await_bytes(dpad_in, small_s.at[0])
    await_bytes(bias_in, small_s.at[1])
    await_bytes(margin_in.at[pl.ds(1, NQ - 1), pl.ds(0, MARGIN)], small_s.at[2])
    await_bytes(slot_in, small_s.at[3])
    await_bytes(bias, small_s.at[4])
    await_bytes(table.at[pl.ds(0, NZ - 1)], small_s.at[5])
    await_bytes(field_all.at[pl.ds(0, NC - 1)], small_s.at[6])
    await_bytes(arrived, small_s.at[7])
    await_bytes(margin_all.at[pl.ds(0, NC - 1)], small_s.at[8])
    for near, sem in ((field_near, 9), (margin_near, 10), (turned_near, 11)):
        await_bytes(near.at[pl.ds(0, NQ - 1)], small_s.at[sem])
    for g, (low, high) in enumerate(GROUPS):
        await_bytes(grad_in.at[:, pl.ds(low, high - low)], sum_s.at[g])
    for j in range(len(JOBS)):
        for stage in range(3):
            if not on_ring(j, stage):
                await_bytes(stage_bytes(j, stage), all_s.at[j, stage])
                continue
            for side in range(2):
                for step in range(ring_steps(j)[side]):
                    await_bytes(
                        bytes_of(box_rows(j, "xy")), ring_s.at[j, side * (NZ // 2) + step]
                    )


def whole(inp, hid, cell_prev, kern, gate_bias, hidden_up, cell_up, lists):
    hbm = pl.BlockSpec(memory_space=pl.ANY)
    state = cell_prev.shape
    devices = NQ * NZ
    operands = (inp, hid, *lists, cell_prev, gate_bias, hidden_up, cell_up, kern)
    results = (
        jax.ShapeDtypeStruct(state, BF16),
        jax.ShapeDtypeStruct(state, F32),
        jax.ShapeDtypeStruct(state, F32),
        jax.ShapeDtypeStruct((9, NX, NY, NZ, SHARE, 128), BF16),
        jax.ShapeDtypeStruct((NY, 8, 128), F32),
        jax.ShapeDtypeStruct((TPD * PIX, 128), F32),
        jax.ShapeDtypeStruct((RIM, 128), F32),
    )
    scratch = [pltpu.VMEM(a.shape, a.dtype) for a in operands[:-1]]
    scratch += [pltpu.VMEM(a.shape, a.dtype) for a in results[:3] + results[4:]]
    scratch += [
        pltpu.VMEM(kern.shape, BF16),
        pltpu.VMEM((TPD * PIX, 128), F32),
        pltpu.VMEM((TPD * PIX, 128), BF16),
        pltpu.VMEM((RIM, 128), BF16),
        pltpu.VMEM((devices * TPD, 128), I32),
        pltpu.VMEM((devices, 128), I32),
        pltpu.VMEM((NZ, RIM, 128), BF16),
        pltpu.VMEM((NQ, MARGIN, 128), BF16),
        pltpu.VMEM((NQ - 1, MARGIN, 128), BF16),
        pltpu.VMEM((NC, TPD * PIX, 128), BF16),
        pltpu.VMEM((NC, MARGIN, 128), BF16),
        pltpu.VMEM((4, TPD * PIX, 128), BF16),
        pltpu.VMEM((4, MARGIN, 128), BF16),
        pltpu.VMEM((3, 4, BODY, 128), F32),
        pltpu.VMEM((3, 4, 8 + BODY + 32, 128), F32),
        pltpu.VMEM((NQ, TPD * PIX, 128), BF16),
        pltpu.VMEM((NQ, MARGIN, 128), BF16),
        pltpu.VMEM((3, BODY, 128), F32),
        pltpu.VMEM((NQ * TPD * PIX, 9 * 128), BF16),
        pltpu.VMEM((NY, TPD * PIX, 128), BF16),
        pltpu.VMEM((NQ, TPD * PIX, 128), BF16),
        pltpu.VMEM((9, 128, 128), BF16),
        pltpu.VMEM((NZ - 1, 9, SHARE, 128), BF16),
        pltpu.VMEM((9, NX, NY, NZ, SHARE, 128), BF16),
        pltpu.VMEM((9 * 1024, 128), BF16),
        pltpu.VMEM((8, 128), F32),
        pltpu.VMEM((NC, DROWS, 128), BF16),
        pltpu.VMEM((NC - 1, DROWS, 128), BF16),
        pltpu.VMEM((DROWS, 128), F32),
        pltpu.VMEM((MARGIN, 128), F32),
        pltpu.VMEM((MARGIN, 128), BF16),
        pltpu.VMEM((NQ, 128, 128), BF16),
        pltpu.VMEM((NZ, RIM, 128), F32),
        pltpu.VMEM((NZ, RIM, 128), BF16),
        pltpu.VMEM((NZ - 1, RIM, 128), BF16),
        pltpu.VMEM((NZ * RIM, NQ * 128), BF16),
        pltpu.VMEM((NZ - 1, 8, 128), F32),
    ]
    for shape in ((12,), (len(GROUPS),), (len(JOBS), 3), (len(JOBS), NZ)):
        scratch += [pltpu.SemaphoreType.DMA(shape)] * 2
    for count in (len(JOBS), len(operands), len(results) - 1):
        scratch.append(pltpu.SemaphoreType.DMA((count,)))
    return pl.pallas_call(
        whole_kernel,
        out_shape=results,
        in_specs=[hbm] * len(operands),
        out_specs=(hbm,) * len(results),
        scratch_shapes=scratch,
        compiler_params=pltpu.CompilerParams(
            collective_id=0, has_side_effects=True, vmem_limit_bytes=VMEM_LIMIT
        ),
        name="whole",
    )(*operands)


def finish_kernel(
    hidden_hbm,
    cell_hbm,
    cell_grad_hbm,
    grad,
    bias_hbm,
    inner_hbm,
    sides_hbm,
    hidden_out,
    cell_out,
    cell_grad_out,
    grad_out,
    bias_out_hbm,
    input_out_hbm,
    prior_out_hbm,
    held,
    wide,
    bias,
    cells,
    sides,
    hidden,
    cell,
    cell_grad,
    bias_out,
    input_out,
    prior_out,
    sems_in,
    sems_out,
    sems,
):
    def fetch(o):
        return pltpu.make_async_copy(grad.at[o], held.at[o], sems_in.at[o])

    def put(o):
        return pltpu.make_async_copy(wide.at[o], grad_out.at[o], sems_out.at[o])

    small = [
        pltpu.make_async_copy(source, target, sems.at[i])
        for i, (source, target) in enumerate(
            (
                (bias_hbm, bias),
                (inner_hbm, cells),
                (sides_hbm, sides),
                (hidden_hbm, hidden),
                (cell_hbm, cell),
                (cell_grad_hbm, cell_grad),
                (hidden, hidden_out),
                (cell, cell_out),
                (cell_grad, cell_grad_out),
                (bias_out, bias_out_hbm),
                (input_out, input_out_hbm),
                (prior_out, prior_out_hbm),
            )
        )
    ]
    fetch(0).start()
    for copy in small[:6]:
        copy.start()
    for o in range(1, 9):
        fetch(o).start()
    for o in range(9):
        fetch(o).wait()
        for k in range(4):
            wide[o, :, k * 128 : (k + 1) * 128] = held[o, k].astype(F32)
        put(o).start()
    for copy in small[:6]:
        copy.wait()
    for copy in small[6:9]:
        copy.start()
    for k in range(4):
        bias_out[k : k + 1, :] = bias[k // 2, 0:1, (k % 2) * 64 : (k % 2 + 1) * 64]
    for t in range(TPD):
        base, at = t * PIX, t * 32
        cells[base : base + 8, :] += sides[at : at + 8, :]
        cells[pl.ds(base + 7, 8, stride=8), :] += sides[at + 8 : at + 16, :]
        cells[base + 56 : base + 64, :] += sides[at + 16 : at + 24, :]
        cells[pl.ds(base, 8, stride=8), :] += sides[at + 24 : at + 32, :]
    ident = eye(128)
    for t in range(TPD):
        rounded = cells[t * PIX : (t + 1) * PIX, :].astype(BF16)
        turned = nt(ident, rounded).astype(BF16)
        input_out[t] = turned[0:64]
        prior_out[t] = turned[64:128]
    for copy in small[9:]:
        copy.start()
    for copy in small[6:]:
        copy.wait()
    for o in range(9):
        put(o).wait()


def finish(hidden, cell, cell_grad, grad, bias, inner, sides):
    hbm = pl.BlockSpec(memory_space=pl.ANY)
    state = hidden.shape
    return pl.pallas_call(
        finish_kernel,
        out_shape=(
            jax.ShapeDtypeStruct(state, BF16),
            jax.ShapeDtypeStruct(state, F32),
            jax.ShapeDtypeStruct(state, F32),
            jax.ShapeDtypeStruct((9, 256, 512), F32),
            jax.ShapeDtypeStruct((4, 64), F32),
            jax.ShapeDtypeStruct(state, BF16),
            jax.ShapeDtypeStruct(state, BF16),
        ),
        in_specs=[hbm] * 7,
        out_specs=(hbm,) * 7,
        scratch_shapes=[
            pltpu.VMEM(grad.shape, BF16),
            pltpu.VMEM((9, 256, 512), F32),
            pltpu.VMEM(bias.shape, F32),
            pltpu.VMEM(inner.shape, F32),
            pltpu.VMEM(sides.shape, F32),
            pltpu.VMEM(state, BF16),
            pltpu.VMEM(state, F32),
            pltpu.VMEM(state, F32),
            pltpu.VMEM((4, 64), F32),
            pltpu.VMEM(state, BF16),
            pltpu.VMEM(state, BF16),
            pltpu.SemaphoreType.DMA((9,)),
            pltpu.SemaphoreType.DMA((9,)),
            pltpu.SemaphoreType.DMA((12,)),
        ],
        compiler_params=pltpu.CompilerParams(vmem_limit_bytes=VMEM_LIMIT),
        name="finish",
    )(hidden, cell, cell_grad, grad, bias, inner, sides)


def local(
    inputs,
    prior_hidden_state,
    cell_prev,
    kernel,
    gate_bias,
    hidden_upstream,
    cell_upstream,
    edge_source,
    edge_code,
    corner_source,
    corner_code,
):
    hidden_new, cell_new, cell_grad, grad, bias, inner, sides = whole(
        inputs,
        prior_hidden_state,
        cell_prev,
        kernel.reshape(9, 256, 512),
        gate_bias,
        hidden_upstream,
        cell_upstream,
        [a.T for a in (edge_source, edge_code, corner_source, corner_code)],
    )
    hidden_new, cell_new, cell_grad, kernel_grad, bias_grad, input_grad, hidden_grad = finish(
        hidden_new, cell_new, cell_grad, grad.reshape(9, NX, NY * NZ * SHARE, 128), bias, inner, sides
    )
    return (
        hidden_new,
        cell_new,
        kernel_grad.reshape(9, 4, 64, 512),
        bias_grad,
        input_grad,
        hidden_grad,
        cell_grad,
    )


def solution(mesh):
    tiles, whole = P("tile", "chan", None), P()
    gates = P(None, None, "chan", None)
    bias = P(None, "chan")
    in_specs = (tiles, tiles, tiles, gates, bias, tiles, tiles, whole, whole, whole, whole)
    out_specs = (tiles, tiles, gates, bias, tiles, tiles, tiles)
    return jax.shard_map(local, mesh=mesh, in_specs=in_specs, out_specs=out_specs, check_vma=False)
```

```python
import functools

import jax
import jax.numpy as jnp
from jax import lax
from jax.experimental import pallas as pl
from jax.experimental.pallas import tpu as pltpu
from jax.sharding import PartitionSpec as P

F32, BF16, I32 = jnp.float32, jnp.bfloat16, jnp.int32
MESH = pl.DeviceIdType.MESH
NY, NX, NZ = 2, 4, 8
NQ = NY * NX
NC = 4
TPD = 3
PIX = 64
RIM = 32 * TPD
MARGIN = 112
BODY = 80 * TPD
DROWS = BODY + 64
SHARE = 16
GROUPS = ((0, 3), (3, 6), (6, 9))
ORDERS = ("yxz", "yxz", "yxz", "zxy", "zxy", "zxy", "zyx", "zyx", "zyx")
VMEM_LIMIT = 56 * 1024 * 1024


def nn(a, b):
    return lax.dot_general(a, b, (((1,), (0,)), ((), ())), preferred_element_type=F32)


def tn(a, b):
    return lax.dot_general(a, b, (((0,), (0,)), ((), ())), preferred_element_type=F32)


def nt(a, b):
    return lax.dot_general(a, b, (((1,), (1,)), ((), ())), preferred_element_type=F32)


def iota(shape, dim):
    return lax.broadcasted_iota(I32, shape, dim)


def eye(n):
    return (iota((n, n), 0) == iota((n, n), 1)).astype(BF16)


def position():
    t = lax.axis_index("tile")
    z, q = lax.rem(t, NZ), lax.div(t, NZ)
    return q, lax.div(q, NX), lax.rem(q, NX), z, lax.axis_index("chan")


def peers():
    q, y, x, z, c = position()
    return {
        "z": lambda d: (q * NZ + lax.rem(z + d, NZ), c),
        "q": lambda d: (lax.rem(q + d, NQ) * NZ + z, c),
        "x": lambda d: ((y * NX + lax.rem(x + d, NX)) * NZ + z, c),
        "y": lambda d: ((lax.rem(y + d, NY) * NX + x) * NZ + z, c),
        "c": lambda d: (q * NZ + z, lax.rem(c + d, NC)),
    }


def greet(to):
    barrier = pltpu.get_barrier_semaphore()
    count = 0
    for axis, size in (("z", NZ), ("q", NQ), ("c", NC)):
        for d in range(1, size):
            pl.semaphore_signal(barrier, inc=1, device_id=to[axis](d), device_id_type=MESH)
            count += 1
    return count


def send(src, dst, send_sem, recv_sem, device):
    pltpu.make_async_remote_copy(
        src_ref=src,
        dst_ref=dst,
        send_sem=send_sem,
        recv_sem=recv_sem,
        device_id=device,
        device_id_type=MESH,
    ).start()


def await_bytes(like, sem):
    pltpu.make_async_copy(like, like, sem).wait()


def axis_size(axis):
    return {"x": NX, "y": NY, "z": NZ}[axis]


def ring_steps(o):
    return (NZ // 2, NZ // 2 - 1) if o % 2 == 0 else (NZ // 2 - 1, NZ // 2)


def own_cells(inp, hid, cells, field, rim):
    ident = eye(PIX)
    for t in range(TPD):
        both = jnp.concatenate([inp[t], hid[t]], axis=0)
        cells[t * PIX : (t + 1) * PIX, :] = nt(ident, both)
    field[...] = cells[...].astype(BF16)
    for t in range(TPD):
        base = t * PIX
        sides = jnp.concatenate(
            [
                cells[base : base + 8, :],
                cells[pl.ds(base + 7, 8, stride=8), :],
                cells[base + 56 : base + 64, :],
                cells[pl.ds(base, 8, stride=8), :],
            ],
            axis=0,
        )
        rim[t * 32 : (t + 1) * 32, :] = sides.astype(BF16)


def source_cells(esrc, ecode, csrc, ccode, by_tile, index):
    lane, row = iota((4, 128), 1), iota((4, 128), 0)
    edge_lane = ((lane < 32) & (lax.div(lane, 8) == row)).astype(F32).astype(BF16)
    corner_lane = (lane - 32 == row).astype(F32).astype(BF16)

    def spread(edges, corners):
        wide = tn(edges[...].astype(F32).astype(BF16), edge_lane)
        wide += tn(corners[...].astype(F32).astype(BF16), corner_lane)
        return wide.astype(I32)

    source, code = spread(esrc, csrc), spread(ecode, ccode)
    lane = iota(source.shape, 1)
    cell = lane & 7
    along_side = (code >> 1) * 8 + jnp.where((code & 1) == 1, 7 - cell, cell)
    at_corner = jnp.where(
        code == 0, 0, jnp.where(code == 1, 7, jnp.where(code == 2, 23, 16))
    )
    by_tile[...] = source * 32 + jnp.where(lane < 32, along_side, at_corner)
    devices = index.shape[0]
    rows = [by_tile[pl.ds(i, devices, stride=TPD), :] for i in range(TPD)]
    index[...] = jnp.concatenate(
        [r[:, :32] for r in rows]
        + [r[:, 32:36] for r in rows]
        + [jnp.full((devices, 128 - 36 * TPD), -1000000, I32)],
        axis=1,
    )


def whole_kernel(
    inp_hbm,
    hid_hbm,
    esrc_hbm,
    ecode_hbm,
    csrc_hbm,
    ccode_hbm,
    cell_prev_hbm,
    bias_hbm,
    hidden_up_hbm,
    cell_up_hbm,
    kern_hbm,
    hidden_hbm,
    cell_hbm,
    cell_grad_hbm,
    grad_hbm,
    bias_sum_hbm,
    inner_hbm,
    side_hbm,
    inp,
    hid,
    esrc,
    ecode,
    csrc,
    ccode,
    cell_prev,
    gate_bias,
    hidden_up,
    cell_up,
    hidden_out,
    cell_out,
    cell_grad_out,
    bias_out,
    inner_out,
    side_out,
    kern,
    cells,
    field,
    rim,
    by_tile,
    index,
    table,
    picked,
    arrived,
    field_all,
    margin_all,
    field_blocks,
    margin_blocks,
    wide,
    accs,
    field_near,
    margin_near,
    wide_near,
    windows_near,
    turned_own,
    turned_near,
    grad,
    grad_in,
    grad_all,
    gauge,
    bias,
    dpad,
    dpad_in,
    dsum,
    margin_own,
    margin_send,
    margin_in,
    slot_sum,
    slot_send,
    slot_in,
    slot_chooser,
    bias_in,
    small_s,
    small_r,
    sum_s,
    sum_r,
    all_s,
    all_r,
    ring_s,
    ring_r,
    out_sems,
    load_sems,
    store_sems,
):
    q, y, x, z, c = position()
    to = peers()

    def quarter(d):
        return lax.rem(lax.rem(q + d, NQ), NX)

    greeted = greet(to)
    loads = [
        pltpu.make_async_copy(far, near, load_sems.at[i])
        for i, (far, near) in enumerate(
            (
                (inp_hbm, inp),
                (hid_hbm, hid),
                (esrc_hbm, esrc),
                (ecode_hbm, ecode),
                (csrc_hbm, csrc),
                (ccode_hbm, ccode),
                (cell_prev_hbm, cell_prev),
                (bias_hbm, gate_bias),
                (hidden_up_hbm, hidden_up),
                (cell_up_hbm, cell_up),
                (kern_hbm, kern),
            )
        )
    ]
    for load in loads:
        load.start()
    stores = [
        pltpu.make_async_copy(near, far, store_sems.at[i])
        for i, (near, far) in enumerate(
            (
                (hidden_out, hidden_hbm),
                (cell_out, cell_hbm),
                (cell_grad_out, cell_grad_hbm),
                (inner_out, inner_hbm),
                (side_out, side_hbm),
                (bias_out, bias_sum_hbm),
            )
        )
    ]
    for load in loads[:2]:
        load.wait()
    own_cells(inp, hid, cells, field, rim)
    margin_in[:, MARGIN:128, :] = jnp.zeros((NQ, 128 - MARGIN, 128), BF16)
    pl.semaphore_wait(pltpu.get_barrier_semaphore(), greeted)

    for d in range(1, NZ):
        send(rim, table.at[z], small_s.at[5], small_r.at[5], to["z"](d))
    for d in range(1, NC):
        send(field, field_all.at[c], small_s.at[6], small_r.at[6], to["c"](d))
    table[z] = rim[...]
    field_all[c] = field[...]
    for load in loads[2:6]:
        load.wait()
    source_cells(esrc, ecode, csrc, ccode, by_tile, index)

    first = q * (NZ * RIM)
    choosers = []
    for d in range(NQ):
        row = index[pl.ds(lax.rem(q + d, NQ) * NZ + z, 1), :]
        down = jnp.broadcast_to((row - first).astype(F32), (128, 128)).T
        choosers.append(
            jnp.concatenate(
                [
                    (down == (iota((128, 128), 1) + 128 * k).astype(F32)).astype(BF16)
                    for k in range(NZ * RIM // 128)
                ],
                axis=1,
            )
        )
    def lanes(ref, k):
        pair, half = 2 * (k % 2), 64 * (k // 2)
        return jnp.concatenate(
            [ref[pair][:, half : half + 64], ref[pair + 1][:, half : half + 64]], axis=1
        )

    await_bytes(field_all.at[pl.ds(0, NC - 1)], small_r.at[6])
    for k in range(4):
        field_blocks[k] = lanes(field_all, k)
    for d in range(1, NQ):
        send(
            field_blocks.at[quarter(d)],
            field_near.at[d],
            small_s.at[9],
            small_r.at[9],
            to["q"](d),
        )
    field_near[0] = field_blocks[x]
    for k in range(4):
        body = field_blocks[k].astype(F32)
        for t in range(TPD):
            base = t * 80
            wide[1, k, base + 8 : base + 72, :] = body[t * PIX : (t + 1) * PIX]
            wide[0, k, base + 9 : base + 72, :] = wide[1, k, base + 8 : base + 71, :]
            wide[2, k, base + 8 : base + 71, :] = wide[1, k, base + 9 : base + 72, :]

    await_bytes(table.at[pl.ds(0, NZ - 1)], small_r.at[5])
    rims = table[...].reshape(NZ * RIM, 128)
    for d in list(range(1, NQ)) + [0]:
        picked[d] = nn(choosers[d], rims)[:MARGIN].astype(BF16)
        if d:
            send(picked.at[d], arrived.at[d - 1], small_s.at[7], small_r.at[7], to["q"](d))

    await_bytes(arrived, small_r.at[7])
    total = picked[0].astype(F32)
    for d in range(1, NQ):
        total += arrived[d - 1].astype(F32)
    margin_all[c] = total.astype(BF16)
    for d in range(1, NC):
        send(margin_all.at[c], margin_all.at[c], small_s.at[8], small_r.at[8], to["c"](d))
    for load in loads[6:]:
        load.wait()
    await_bytes(margin_all.at[pl.ds(0, NC - 1)], small_r.at[8])
    for k in range(4):
        margin_blocks[k] = lanes(margin_all, k)
    for d in range(1, NQ):
        send(
            margin_blocks.at[quarter(d)],
            margin_near.at[d],
            small_s.at[10],
            small_r.at[10],
            to["q"](d),
        )
    margin_near[0] = margin_blocks[x]

    for k in range(4):
        margin = margin_blocks[k].astype(F32)
        left, right = wide.at[0, k], wide.at[2, k]
        for t in range(TPD):
            base, at, corner = t * 80, t * 32, RIM + t * 4
            for row, side in ((base, at), (base + 72, at + 16)):
                wide[1, k, row : row + 8, :] = margin[side : side + 8]
                left[row + 1 : row + 8, :] = margin[side : side + 7]
                right[row : row + 7, :] = margin[side + 1 : side + 8]
            left[base : base + 1, :] = margin[corner : corner + 1]
            left[pl.ds(base + 8, 8, stride=8), :] = margin[at + 24 : at + 32]
            left[base + 72 : base + 73, :] = margin[corner + 3 : corner + 4]
            right[base + 7 : base + 8, :] = margin[corner + 1 : corner + 2]
            right[pl.ds(base + 15, 8, stride=8), :] = margin[at + 8 : at + 16]
            right[base + 79 : base + 80, :] = margin[corner + 2 : corner + 3]

    def window(o):
        start = (o // 3) * 8
        return jnp.concatenate(
            [
                jnp.concatenate(
                    [
                        wide[o % 3, k, t * 80 + start : t * 80 + start + PIX, :]
                        for t in range(TPD)
                    ],
                    axis=0,
                ).astype(BF16)
                for k in range(4)
            ],
            axis=1,
        )

    def gate(k):
        column = jnp.broadcast_to(gate_bias[k : k + 1, :], (64, 64)).T
        return jnp.concatenate([column] * TPD, axis=1)

    gates = jnp.concatenate([gate(k) for k in range(4)], axis=0)
    for o in range(9):
        gates = gates + nt(kern[o], window(o))
    in_gate = jax.nn.sigmoid(gates[0:64])
    forget = jax.nn.sigmoid(gates[64:128])
    cand = jnp.tanh(gates[128:192])
    out_gate = jax.nn.sigmoid(gates[192:256])
    before = jnp.concatenate([cell_prev[t] for t in range(TPD)], axis=1)
    above = jnp.concatenate([cell_up[t] for t in range(TPD)], axis=1)
    upstream = jnp.concatenate([hidden_up[t].astype(F32) for t in range(TPD)], axis=1)
    cell_new = forget * before + in_gate * cand
    squashed = jnp.tanh(cell_new)
    hidden_new = (out_gate * squashed).astype(BF16)
    dcell = above + upstream * out_gate * (1.0 - squashed * squashed)
    cell_grad = dcell * forget
    dgates = jnp.concatenate(
        [
            dcell * cand * in_gate * (1.0 - in_gate),
            dcell * before * forget * (1.0 - forget),
            dcell * in_gate * (1.0 - cand * cand),
            upstream * squashed * out_gate * (1.0 - out_gate),
        ],
        axis=0,
    ).astype(BF16)

    turned = nt(eye(TPD * PIX), dgates).astype(BF16)
    for h in range(NY):
        turned_own[h] = turned[:, h * 128 : (h + 1) * 128]
    for d in range(1, NQ):
        send(
            turned_own.at[lax.div(lax.rem(q + d, NQ), NX)],
            turned_near.at[d],
            small_s.at[11],
            small_r.at[11],
            to["q"](d),
        )
    turned_near[0] = turned_own[y]

    accs[...] = jnp.zeros(accs.shape, F32)
    for o in range(9):
        a, b = o // 3, o % 3
        product = nn(turned, kern[o])
        for k in range(4):
            for t in range(TPD):
                base = 8 + t * 80 + a * 8
                accs[b, k, base : base + PIX, :] += product[
                    t * PIX : (t + 1) * PIX, k * 128 : (k + 1) * 128
                ]
    column = iota((BODY, 128), 0) & 7
    blocks = []
    for k in range(4):
        body = accs[1, k, 8 : 8 + BODY, :]
        body += jnp.where(column < 7, accs[0, k, 9 : 9 + BODY, :], 0.0)
        body += jnp.where(column > 0, accs[2, k, 7 : 7 + BODY, :], 0.0)
        left, right = accs.at[0, k], accs.at[2, k]
        blocks.append(
            (
                body,
                left[pl.ds(8, 32, stride=8), :],
                right[pl.ds(15, 32, stride=8), :],
            )
        )
    for e in range(NC):
        half = slice((e % 2) * 64, (e % 2) * 64 + 64)
        start = 0
        for one, two in zip(blocks[e // 2], blocks[2 + e // 2]):
            rows = one.shape[0]
            dpad[e, start : start + rows, :] = jnp.concatenate(
                [one[:, half], two[:, half]], axis=1
            ).astype(BF16)
            start += rows
    for t in range(TPD):
        at = slice(t * PIX, (t + 1) * PIX)
        hidden_out[t] = hidden_new[:, at]
        cell_out[t] = cell_new[:, at]
        cell_grad_out[t] = cell_grad[:, at]
    for store in stores[:3]:
        store.start()

    await_bytes(field_near.at[pl.ds(0, NQ - 1)], small_r.at[9])
    await_bytes(margin_near.at[pl.ds(0, NQ - 1)], small_r.at[10])

    def windows_of(s, carry):
        body, margin = field_near[s].astype(F32), margin_near[s].astype(F32)
        left, right = wide_near.at[0], wide_near.at[2]
        for t in range(TPD):
            base, at = t * 80, t * 32
            wide_near[1, base : base + 8, :] = margin[at : at + 8]
            wide_near[1, base + 8 : base + 72, :] = body[t * PIX : (t + 1) * PIX]
            wide_near[1, base + 72 : base + 80, :] = margin[at + 16 : at + 24]
        wide_near[0, 1:BODY, :] = wide_near[1, 0 : BODY - 1, :]
        wide_near[2, 0 : BODY - 1, :] = wide_near[1, 1:BODY, :]
        for t in range(TPD):
            base, at, corner = t * 80, t * 32, RIM + t * 4
            left[base : base + 1, :] = margin[corner : corner + 1]
            left[pl.ds(base + 8, 8, stride=8), :] = margin[at + 24 : at + 32]
            left[base + 72 : base + 73, :] = margin[corner + 3 : corner + 4]
            right[base + 7 : base + 8, :] = margin[corner + 1 : corner + 2]
            right[pl.ds(base + 15, 8, stride=8), :] = margin[at + 8 : at + 16]
            right[base + 79 : base + 80, :] = margin[corner + 2 : corner + 3]
        for o in range(9):
            for t in range(TPD):
                base = t * 80 + (o // 3) * 8
                row = pl.multiple_of(s * (TPD * PIX) + t * PIX, PIX)
                windows_near[pl.ds(row, PIX), o * 128 : (o + 1) * 128] = wide_near[
                    o % 3, base : base + PIX, :
                ].astype(BF16)
        return carry

    lax.fori_loop(0, NQ, windows_of, 0)
    await_bytes(turned_near.at[pl.ds(0, NQ - 1)], small_r.at[11])
    near = nt(eye(128), turned_near[...].reshape(NQ * TPD * PIX, 128)).astype(BF16)
    bias[...] = nt(jnp.ones((8, NQ * TPD * PIX), BF16), near)
    for d in range(1, NZ):
        send(bias, bias_in.at[d - 1], small_s.at[1], small_r.at[1], to["z"](d))
    for g, (low, high) in enumerate(GROUPS):
        product = nn(near, windows_near[:, low * 128 : high * 128]).astype(BF16)
        for o in range(low, high):
            grad[o] = product[:, (o - low) * 128 : (o - low + 1) * 128]
        for d in range(1, NZ):
            at = pl.multiple_of(lax.rem(z + d, NZ) * SHARE, SHARE)
            send(
                grad.at[pl.ds(low, high - low), pl.ds(at, SHARE)],
                grad_in.at[d - 1, pl.ds(low, high - low)],
                sum_s.at[g],
                sum_r.at[g],
                to["z"](d),
            )

    for d in range(1, NC):
        send(
            dpad.at[lax.rem(c + d, NC)],
            dpad_in.at[d - 1],
            small_s.at[0],
            small_r.at[0],
            to["c"](d),
        )
    await_bytes(dpad_in, small_r.at[0])
    total = dpad[c].astype(F32)
    for d in range(NC - 1):
        total += dpad_in[d].astype(F32)
    dsum[...] = total
    left, right = BODY, BODY + 32
    margin_own[...] = jnp.zeros(margin_own.shape, F32)
    for t in range(TPD):
        base, at, corner, col = t * 80, t * 32, RIM + t * 4, t * 10
        margin_own[at : at + 8, :] = dsum[base : base + 8, :]
        margin_own[at + 8 : at + 16, :] = dsum[right + col + 1 : right + col + 9, :]
        margin_own[at + 16 : at + 24, :] = dsum[base + 72 : base + 80, :]
        margin_own[at + 24 : at + 32, :] = dsum[left + col + 1 : left + col + 9, :]
        margin_own[corner : corner + 1, :] = dsum[left + col : left + col + 1, :]
        margin_own[corner + 1 : corner + 2, :] = dsum[right + col : right + col + 1, :]
        margin_own[corner + 2 : corner + 3, :] = dsum[right + col + 9 : right + col + 10, :]
        margin_own[corner + 3 : corner + 4, :] = dsum[left + col + 9 : left + col + 10, :]
        inner_out[t * PIX : (t + 1) * PIX, :] = dsum[base + 8 : base + 72, :]
    stores[3].start()
    margin_send[...] = margin_own[...].astype(BF16)
    for d in range(1, NQ):
        send(
            margin_send,
            margin_in.at[d, pl.ds(0, MARGIN)],
            small_s.at[2],
            small_r.at[2],
            to["q"](d),
        )
    margin_in[0, 0:MARGIN, :] = margin_send[...]
    for d in range(NQ):
        row = index[pl.ds(lax.rem(q + NQ - d, NQ) * NZ + z, 1), :]
        chooser = (iota((NZ * RIM, 128), 0) == row - first).astype(F32).astype(BF16)
        slot_chooser[:, d * 128 : (d + 1) * 128] = chooser

    def box(o, full, at_z=None):
        return grad_all.at[
            o,
            slice(None) if "x" in full else x,
            slice(None) if "y" in full else y,
            slice(None) if "z" in full else (z if at_z is None else at_z),
        ]

    def box_rows(full):
        rows = SHARE
        for axis in full:
            rows *= axis_size(axis)
        return rows

    def bytes_of(rows):
        return gauge.at[pl.ds(0, rows)]

    def on_ring(o, stage):
        return stage == 2 and ORDERS[o][2] == "z"

    def ring_send(o, step, side):
        share = lax.rem(z + NZ + (1 - step if side == 0 else step - 1), NZ)
        mine = box(o, "xy", share)
        at = (o, side * (NZ // 2) + step - 1)
        send(mine, mine, ring_s.at[at], ring_r.at[at], to["z"](1 if side == 0 else NZ - 1))

    def ring_wait(o, step, side):
        await_bytes(bytes_of(box_rows("xy")), ring_r.at[o, side * (NZ // 2) + step - 1])

    def gather(o, stage):
        if on_ring(o, stage):
            for side in range(2):
                ring_send(o, 1, side)
            return
        axis, full = ORDERS[o][stage], ORDERS[o][:stage]
        mine = box(o, full)
        for d in range(1, axis_size(axis)):
            send(mine, mine, all_s.at[o, stage], all_r.at[o, stage], to[axis](d))

    def stage_bytes(o, stage):
        axis, full = ORDERS[o][stage], ORDERS[o][:stage]
        return bytes_of(box_rows(full) * (axis_size(axis) - 1))

    def gathered(o, stage):
        await_bytes(stage_bytes(o, stage), all_r.at[o, stage])

    for g, (low, high) in enumerate(GROUPS):
        some = pl.ds(low, high - low)
        await_bytes(grad_in.at[:, some], sum_r.at[g])
        total = grad[some, pl.ds(pl.multiple_of(z * SHARE, SHARE), SHARE), :].astype(F32)
        for d in range(NZ - 1):
            total += grad_in[d, some].astype(F32)
        for o in range(low, high):
            grad_all[o, x, y, z] = total[o - low].astype(BF16)
            gather(o, 0)

    await_bytes(margin_in.at[pl.ds(1, NQ - 1), pl.ds(0, MARGIN)], small_r.at[2])
    sums = nn(slot_chooser[...], margin_in[...].reshape(NQ * 128, 128))
    slot_sum[...] = sums.reshape(NZ, RIM, 128)
    slot_send[...] = slot_sum[...].astype(BF16)
    for d in range(1, NZ):
        send(
            slot_send.at[lax.rem(z + d, NZ)],
            slot_in.at[d - 1],
            small_s.at[3],
            small_r.at[3],
            to["z"](d),
        )
    await_bytes(bias_in, small_r.at[1])
    total = bias[...]
    for d in range(NZ - 1):
        total += bias_in[d]
    bias_out[y] = total
    send(bias_out.at[y], bias_out.at[y], small_s.at[4], small_r.at[4], to["y"](1))

    def put(o):
        return pltpu.make_async_copy(grad_all.at[o], grad_hbm.at[o], out_sems.at[o])

    for stage in (0, 1):
        for o in range(9):
            gathered(o, stage)
            gather(o, stage + 1)
    for step in range(1, NZ // 2 + 1):
        for o in range(9):
            if on_ring(o, 2):
                for side in range(2):
                    if step <= ring_steps(o)[side]:
                        ring_wait(o, step, side)
                    if step < ring_steps(o)[side]:
                        ring_send(o, step + 1, side)
                if step == NZ // 2:
                    put(o).start()
            elif step == 3:
                gathered(o, 2)
                put(o).start()
    await_bytes(slot_in, small_r.at[3])
    total = slot_sum[z]
    for d in range(NZ - 1):
        total += slot_in[d].astype(F32)
    side_out[...] = total
    stores[4].start()
    await_bytes(bias, small_r.at[4])
    stores[5].start()
    for store in stores:
        store.wait()
    for o in range(9):
        put(o).wait()

    await_bytes(dpad_in, small_s.at[0])
    await_bytes(bias_in, small_s.at[1])
    await_bytes(margin_in.at[pl.ds(1, NQ - 1), pl.ds(0, MARGIN)], small_s.at[2])
    await_bytes(slot_in, small_s.at[3])
    await_bytes(bias, small_s.at[4])
    await_bytes(table.at[pl.ds(0, NZ - 1)], small_s.at[5])
    await_bytes(field_all.at[pl.ds(0, NC - 1)], small_s.at[6])
    await_bytes(arrived, small_s.at[7])
    await_bytes(margin_all.at[pl.ds(0, NC - 1)], small_s.at[8])
    for near, sem in ((field_near, 9), (margin_near, 10), (turned_near, 11)):
        await_bytes(near.at[pl.ds(0, NQ - 1)], small_s.at[sem])
    for g, (low, high) in enumerate(GROUPS):
        await_bytes(grad_in.at[:, pl.ds(low, high - low)], sum_s.at[g])
    for o in range(9):
        for stage in range(3):
            if not on_ring(o, stage):
                await_bytes(stage_bytes(o, stage), all_s.at[o, stage])
                continue
            for side in range(2):
                for step in range(ring_steps(o)[side]):
                    await_bytes(
                        bytes_of(box_rows("xy")), ring_s.at[o, side * (NZ // 2) + step]
                    )


def whole(inp, hid, cell_prev, kern, gate_bias, hidden_up, cell_up, lists):
    hbm = pl.BlockSpec(memory_space=pl.ANY)
    state = cell_prev.shape
    devices = NQ * NZ
    operands = (inp, hid, *lists, cell_prev, gate_bias, hidden_up, cell_up, kern)
    results = (
        jax.ShapeDtypeStruct(state, BF16),
        jax.ShapeDtypeStruct(state, F32),
        jax.ShapeDtypeStruct(state, F32),
        jax.ShapeDtypeStruct((9, NX, NY, NZ, SHARE, 128), BF16),
        jax.ShapeDtypeStruct((NY, 8, 128), F32),
        jax.ShapeDtypeStruct((TPD * PIX, 128), F32),
        jax.ShapeDtypeStruct((RIM, 128), F32),
    )
    scratch = [pltpu.VMEM(a.shape, a.dtype) for a in operands[:-1]]
    scratch += [pltpu.VMEM(a.shape, a.dtype) for a in results[:3] + results[4:]]
    scratch += [
        pltpu.VMEM(kern.shape, BF16),
        pltpu.VMEM((TPD * PIX, 128), F32),
        pltpu.VMEM((TPD * PIX, 128), BF16),
        pltpu.VMEM((RIM, 128), BF16),
        pltpu.VMEM((devices * TPD, 128), I32),
        pltpu.VMEM((devices, 128), I32),
        pltpu.VMEM((NZ, RIM, 128), BF16),
        pltpu.VMEM((NQ, MARGIN, 128), BF16),
        pltpu.VMEM((NQ - 1, MARGIN, 128), BF16),
        pltpu.VMEM((NC, TPD * PIX, 128), BF16),
        pltpu.VMEM((NC, MARGIN, 128), BF16),
        pltpu.VMEM((4, TPD * PIX, 128), BF16),
        pltpu.VMEM((4, MARGIN, 128), BF16),
        pltpu.VMEM((3, 4, BODY, 128), F32),
        pltpu.VMEM((3, 4, 8 + BODY + 32, 128), F32),
        pltpu.VMEM((NQ, TPD * PIX, 128), BF16),
        pltpu.VMEM((NQ, MARGIN, 128), BF16),
        pltpu.VMEM((3, BODY, 128), F32),
        pltpu.VMEM((NQ * TPD * PIX, 9 * 128), BF16),
        pltpu.VMEM((NY, TPD * PIX, 128), BF16),
        pltpu.VMEM((NQ, TPD * PIX, 128), BF16),
        pltpu.VMEM((9, 128, 128), BF16),
        pltpu.VMEM((NZ - 1, 9, SHARE, 128), BF16),
        pltpu.VMEM((9, NX, NY, NZ, SHARE, 128), BF16),
        pltpu.VMEM((1024, 128), BF16),
        pltpu.VMEM((8, 128), F32),
        pltpu.VMEM((NC, DROWS, 128), BF16),
        pltpu.VMEM((NC - 1, DROWS, 128), BF16),
        pltpu.VMEM((DROWS, 128), F32),
        pltpu.VMEM((MARGIN, 128), F32),
        pltpu.VMEM((MARGIN, 128), BF16),
        pltpu.VMEM((NQ, 128, 128), BF16),
        pltpu.VMEM((NZ, RIM, 128), F32),
        pltpu.VMEM((NZ, RIM, 128), BF16),
        pltpu.VMEM((NZ - 1, RIM, 128), BF16),
        pltpu.VMEM((NZ * RIM, NQ * 128), BF16),
        pltpu.VMEM((NZ - 1, 8, 128), F32),
    ]
    for shape in ((12,), (len(GROUPS),), (9, 3), (9, NZ)):
        scratch += [pltpu.SemaphoreType.DMA(shape)] * 2
    for count in (9, len(operands), len(results) - 1):
        scratch.append(pltpu.SemaphoreType.DMA((count,)))
    return pl.pallas_call(
        whole_kernel,
        out_shape=results,
        in_specs=[hbm] * len(operands),
        out_specs=(hbm,) * len(results),
        scratch_shapes=scratch,
        compiler_params=pltpu.CompilerParams(
            collective_id=0, has_side_effects=True, vmem_limit_bytes=VMEM_LIMIT
        ),
        name="whole",
    )(*operands)


def finish_kernel(
    hidden_hbm,
    cell_hbm,
    cell_grad_hbm,
    grad,
    bias_hbm,
    inner_hbm,
    sides_hbm,
    hidden_out,
    cell_out,
    cell_grad_out,
    grad_out,
    bias_out_hbm,
    input_out_hbm,
    prior_out_hbm,
    held,
    wide,
    bias,
    cells,
    sides,
    hidden,
    cell,
    cell_grad,
    bias_out,
    input_out,
    prior_out,
    sems_in,
    sems_out,
    sems,
):
    def fetch(o):
        return pltpu.make_async_copy(grad.at[o], held.at[o], sems_in.at[o])

    def put(o):
        return pltpu.make_async_copy(wide.at[o], grad_out.at[o], sems_out.at[o])

    small = [
        pltpu.make_async_copy(source, target, sems.at[i])
        for i, (source, target) in enumerate(
            (
                (bias_hbm, bias),
                (inner_hbm, cells),
                (sides_hbm, sides),
                (hidden_hbm, hidden),
                (cell_hbm, cell),
                (cell_grad_hbm, cell_grad),
                (hidden, hidden_out),
                (cell, cell_out),
                (cell_grad, cell_grad_out),
                (bias_out, bias_out_hbm),
                (input_out, input_out_hbm),
                (prior_out, prior_out_hbm),
            )
        )
    ]
    fetch(0).start()
    for copy in small[:6]:
        copy.start()
    for o in range(1, 9):
        fetch(o).start()
    for o in range(9):
        fetch(o).wait()
        for k in range(4):
            wide[o, :, k * 128 : (k + 1) * 128] = held[o, k].astype(F32)
        put(o).start()
    for copy in small[:6]:
        copy.wait()
    for copy in small[6:9]:
        copy.start()
    for k in range(4):
        bias_out[k : k + 1, :] = bias[k // 2, 0:1, (k % 2) * 64 : (k % 2 + 1) * 64]
    for t in range(TPD):
        base, at = t * PIX, t * 32
        cells[base : base + 8, :] += sides[at : at + 8, :]
        cells[pl.ds(base + 7, 8, stride=8), :] += sides[at + 8 : at + 16, :]
        cells[base + 56 : base + 64, :] += sides[at + 16 : at + 24, :]
        cells[pl.ds(base, 8, stride=8), :] += sides[at + 24 : at + 32, :]
    ident = eye(128)
    for t in range(TPD):
        rounded = cells[t * PIX : (t + 1) * PIX, :].astype(BF16)
        turned = nt(ident, rounded).astype(BF16)
        input_out[t] = turned[0:64]
        prior_out[t] = turned[64:128]
    for copy in small[9:]:
        copy.start()
    for copy in small[6:]:
        copy.wait()
    for o in range(9):
        put(o).wait()


def finish(hidden, cell, cell_grad, grad, bias, inner, sides):
    hbm = pl.BlockSpec(memory_space=pl.ANY)
    state = hidden.shape
    return pl.pallas_call(
        finish_kernel,
        out_shape=(
            jax.ShapeDtypeStruct(state, BF16),
            jax.ShapeDtypeStruct(state, F32),
            jax.ShapeDtypeStruct(state, F32),
            jax.ShapeDtypeStruct((9, 256, 512), F32),
            jax.ShapeDtypeStruct((4, 64), F32),
            jax.ShapeDtypeStruct(state, BF16),
            jax.ShapeDtypeStruct(state, BF16),
        ),
        in_specs=[hbm] * 7,
        out_specs=(hbm,) * 7,
        scratch_shapes=[
            pltpu.VMEM(grad.shape, BF16),
            pltpu.VMEM((9, 256, 512), F32),
            pltpu.VMEM(bias.shape, F32),
            pltpu.VMEM(inner.shape, F32),
            pltpu.VMEM(sides.shape, F32),
            pltpu.VMEM(state, BF16),
            pltpu.VMEM(state, F32),
            pltpu.VMEM(state, F32),
            pltpu.VMEM((4, 64), F32),
            pltpu.VMEM(state, BF16),
            pltpu.VMEM(state, BF16),
            pltpu.SemaphoreType.DMA((9,)),
            pltpu.SemaphoreType.DMA((9,)),
            pltpu.SemaphoreType.DMA((12,)),
        ],
        compiler_params=pltpu.CompilerParams(vmem_limit_bytes=VMEM_LIMIT),
        name="finish",
    )(hidden, cell, cell_grad, grad, bias, inner, sides)


def local(
    inputs,
    prior_hidden_state,
    cell_prev,
    kernel,
    gate_bias,
    hidden_upstream,
    cell_upstream,
    edge_source,
    edge_code,
    corner_source,
    corner_code,
):
    hidden_new, cell_new, cell_grad, grad, bias, inner, sides = whole(
        inputs,
        prior_hidden_state,
        cell_prev,
        kernel.reshape(9, 256, 512),
        gate_bias,
        hidden_upstream,
        cell_upstream,
        [a.T for a in (edge_source, edge_code, corner_source, corner_code)],
    )
    hidden_new, cell_new, cell_grad, kernel_grad, bias_grad, input_grad, hidden_grad = finish(
        hidden_new, cell_new, cell_grad, grad.reshape(9, NX, NY * NZ * SHARE, 128), bias, inner, sides
    )
    return (
        hidden_new,
        cell_new,
        kernel_grad.reshape(9, 4, 64, 512),
        bias_grad,
        input_grad,
        hidden_grad,
        cell_grad,
    )


def solution(mesh):
    tiles, whole = P("tile", "chan", None), P()
    gates = P(None, None, "chan", None)
    bias = P(None, "chan")
    in_specs = (tiles, tiles, tiles, gates, bias, tiles, tiles, whole, whole, whole, whole)
    out_specs = (tiles, tiles, gates, bias, tiles, tiles, tiles)
    return jax.shard_map(local, mesh=mesh, in_specs=in_specs, out_specs=out_specs, check_vma=False)
```
